32 devices in a mesh: dp: 16 (over z, y, core), seq: 2 (over x).
Axes of the slice: x: 2, y: 2, z: 4, core: 2. Of those that a mesh axis runs over, the one named last changes fastest.
Arguments:
- frames: bfloat16 [64, 512, 1024], P('dp', 'seq'), may hold values from -6 to 6
- cotangent: bfloat16 [64, 512, 1024], P('dp', 'seq'), may hold values from -6 to 6
- lengths: int32 [64], P('dp'), may hold values from 51 to 500, as said below
- qkv_weight: bfloat16 [1024, 3072], replicated, may hold values from -0.1875 to 0.1875
- out_weight: bfloat16 [1024, 1024], replicated, may hold values from -1 to 1
- gate_weight: bfloat16 [1024, 4096], replicated, may hold values from -0.1875 to 0.1875
- up_weight: bfloat16 [1024, 4096], replicated, may hold values from -0.1875 to 0.1875
- down_weight: bfloat16 [4096, 1024], replicated, may hold values from -0.09375 to 0.09375
- gain_table: float32 [1024, 4], replicated, may hold values from 0.1 to 1.9
- bias_table: float32 [1024, 2], replicated, may hold values from -3 to 3
Outputs:
- output: bfloat16 [64, 512, 1024], P('dp', 'seq')
- input_grad: bfloat16 [64, 512, 1024], P('dp', 'seq')
- qkv_grad: float32 [1024, 3072], P('dp', 'seq')
- out_grad: float32 [1024, 1024], P('dp', 'seq')
- gate_grad: float32 [1024, 4096], P('dp', 'seq')
- up_grad: float32 [1024, 4096], P('dp', 'seq')
- down_grad: float32 [4096, 1024], P('dp', 'seq')
- gain_grad: float32 [1024, 4], P('dp', 'seq')
- bias_grad: float32 [1024, 2], P('dp', 'seq')
The draws below stay inside these ranges and needn't reach their ends.
Inputs may be any that keep to these rules, and one draw needn't show every extreme that they name: `lengths`: in the clips of each index of dp (4 clips), one clip, drawn from the seed, has exactly 500 frames.
All inputs are finite; a program needn't handle non-finite values.
Results may differ from the reference program's by a relative error of at most 0.014.
Values may be sent and summed in bfloat16 or wider, within the bound.
No kernel may reach another device: no remote copies, remote signals or barrier semaphores. Data moves between devices by JAX's collectives and lax.ppermute only.
A program may use at most 256 MiB of HBM per device.

```python
import math
import jax
import jax.numpy as jnp
from jax import lax

D = 1024
HEADS = 16
FF = 4096
PAD = 512
WINDOW = 128
CLIP_GRP = 4
CLIPS = 64


def draw_lengths(key, part):
    key = jax.random.fold_in(key, 7)
    first_key, second_key = jax.random.split(key)
    drawn = jax.random.randint(first_key, (CLIPS,), PAD // 10, PAD - 11)
    chosen = jax.random.randint(second_key, (CLIPS // CLIP_GRP,), 0, CLIP_GRP)
    places = jnp.arange(CLIPS) % CLIP_GRP
    picked = jnp.repeat(chosen, CLIP_GRP)
    return jnp.where(places == picked, PAD - 12, drawn).astype(jnp.int32)


def shard_levels(rng, shape, cuts, low, high):
    loudness = 1.0
    for dim, blocks in cuts:
        draws = jax.random.uniform(jax.random.fold_in(jax.random.fold_in(rng, 6), dim), (blocks,), jnp.float32, low / len(cuts), high / len(cuts))
        loudness = loudness * jnp.repeat(jnp.exp(draws), shape[dim] // blocks).reshape((-1,) + (1,) * (len(shape) - 1 - dim))
    return loudness


def normal_values(stream_key, extent, scale, bound, cuts=(), dtype=jnp.bfloat16):
    gain = shard_levels(stream_key, extent, cuts, -0.22, 0.18) if cuts else 1.0
    entries = jax.random.normal(stream_key, extent, jnp.float32) * scale * gain
    return jnp.minimum(jnp.maximum(entries, -bound), bound).astype(dtype)


def setup_inputs(seed: int = 0) -> dict:
    arg_keys = jax.random.split(jax.random.key(seed), 11)
    frames = normal_values(arg_keys[0], (CLIPS, PAD, D), 1.0, 6.0, ((0, 16), (1, 2)))
    cotangent = normal_values(arg_keys[1], (CLIPS, PAD, D), 1.0, 6.0, ((0, 16), (1, 2)))
    lengths = draw_lengths(jax.random.fold_in(arg_keys[10], 71), 0)
    qkv_weight = normal_values(arg_keys[3], (D, 3 * D), D ** -0.5, 0.1875)
    out_weight = normal_values(arg_keys[4], (D, D), (D // 32) ** -0.5, 1.0)
    gate_weight = normal_values(arg_keys[5], (D, FF), D ** -0.5, 0.1875)
    up_weight = normal_values(arg_keys[6], (D, FF), D ** -0.5, 0.1875)
    down_weight = normal_values(arg_keys[7], (FF, D), FF ** -0.5, 0.09375)
    gain_table = jnp.clip(1.0 + 0.18 * jax.random.normal(arg_keys[8], (D, 4), jnp.float32), 0.1, 1.9)
    bias_table = normal_values(arg_keys[9], (D, 2), 0.5, 3.0, (), jnp.float32)
    return dict(frames=frames, cotangent=cotangent, lengths=lengths, qkv_weight=qkv_weight, out_weight=out_weight, gate_weight=gate_weight, up_weight=up_weight, down_weight=down_weight, gain_table=gain_table, bias_table=bias_table)


@jax.custom_vjp
def low(v):
    return lax.optimization_barrier(v.astype(jnp.bfloat16)).astype(jnp.float32)

@jax.custom_vjp
def low_back(v):
    return v

def low_keep(v):
    return (low(v), None)

def low_pass(kept, grad):
    return (grad,)

def back_keep(v):
    return (v, None)

def back_low(kept, grad):
    return (low(grad),)
low.defvjp(low_keep, low_pass)
low_back.defvjp(back_keep, back_low)
NORM_EPS = 1e-05
MASKED = -1e+30
HIGHEST = lax.Precision.HIGHEST

def matmul(left_op, right_op):
    return jnp.dot(left_op, right_op, precision=HIGHEST, preferred_element_type=jnp.float32)

def layer_norm(values, gain_col, shift_col):
    row_mean = lax.optimization_barrier(jnp.mean(values, axis=-1, keepdims=True))
    centred = values - row_mean
    spread = lax.optimization_barrier(jnp.mean(centred * centred, axis=-1, keepdims=True))
    return centred * lax.rsqrt(spread + NORM_EPS) * gain_col + shift_col

def rotary_tables(places, head_dim):
    pair_count = head_dim // 2
    freq_rates = jnp.exp(jnp.arange(pair_count).astype(jnp.float32) * (-2.0 * math.log(10000.0) / head_dim))
    angles = places.astype(jnp.float32)[:, None] * freq_rates[None, :]
    return (jnp.cos(angles), jnp.sin(angles))

def rotate(values, cosine, sine_table):
    pair_count = values.shape[-1] // 2
    leading = values[..., :pair_count]
    trailing = values[..., pair_count:]
    cos_wide = cosine[:, None, :]
    sin_wide = sine_table[:, None, :]
    return jnp.concatenate([leading * cos_wide - trailing * sin_wide, trailing * cos_wide + leading * sin_wide], axis=-1)

def clip_attention(block_item):
    queries, key_rows, values, length = block_item
    products = low_back(jnp.einsum('qhd,khd->hqk', queries, key_rows, precision=HIGHEST))
    query_pos = jnp.arange(PAD)[:, None]
    key_pos = jnp.arange(PAD)[None, :]
    allowed = (key_pos <= query_pos) & (key_pos > query_pos - WINDOW) & (key_pos < length)
    scores = jnp.where(allowed[None], products * (1.0 / math.sqrt(queries.shape[-1])), MASKED)
    top_score = lax.optimization_barrier(jnp.max(scores, axis=-1, keepdims=True))
    exponent = jnp.exp(scores - top_score)
    weights = low(exponent / lax.optimization_barrier(jnp.sum(exponent, axis=-1, keepdims=True)))
    return jnp.einsum('hqk,khd->qhd', weights, values, precision=HIGHEST)

def layer(frames, qkv_weight, out_weight, gate_weight, up_weight, down_weight, gain_table, bias_table, lengths):
    clip_count = frames.shape[0]
    head_dim = D // HEADS
    places = jnp.arange(PAD)
    valid_rows = (places[None, :] < lengths[:, None]).astype(jnp.float32)[:, :, None]
    flat = frames.reshape(-1, D)
    normed_one = low(layer_norm(flat, gain_table[:, 0], bias_table[:, 0]))
    mixed = low_back(matmul(normed_one, qkv_weight)).reshape(clip_count, PAD, 3, HEADS, head_dim)
    cosine, sine_table = rotary_tables(places, head_dim)
    queries = low(rotate(mixed[:, :, 0], cosine, sine_table))
    key_rows = low(rotate(mixed[:, :, 1], cosine, sine_table))
    values = low(mixed[:, :, 2])
    context = lax.map(jax.checkpoint(clip_attention), (queries, key_rows, values, lengths))
    context = low(low_back(context.reshape(-1, D)))
    attended = low_back(matmul(context, out_weight))
    middle = flat + gain_table[:, 2] * attended
    normed_two = low(layer_norm(middle, gain_table[:, 1], bias_table[:, 1]))
    gate_rows = low_back(matmul(normed_two, gate_weight))
    upward = low_back(matmul(normed_two, up_weight))
    hidden = low(jax.nn.silu(gate_rows) * upward)
    branch = low_back(matmul(hidden, down_weight))
    return (middle + gain_table[:, 3] * branch).reshape(clip_count, PAD, D) * valid_rows

def reference(frames, cotangent, lengths, qkv_weight, out_weight, gate_weight, up_weight, down_weight, gain_table, bias_table):
    params = (qkv_weight.astype(jnp.float32), out_weight.astype(jnp.float32), gate_weight.astype(jnp.float32), up_weight.astype(jnp.float32), down_weight.astype(jnp.float32), gain_table.astype(jnp.float32), bias_table.astype(jnp.float32))
    block_size = 8
    frame_blocks = frames.astype(jnp.float32).reshape(-1, block_size, PAD, D)
    tangent_blocks = cotangent.astype(jnp.float32).reshape(-1, block_size, PAD, D)
    length_blocks = lengths.reshape(-1, block_size)

    def one_block(totals, block_item):
        block_frames, block_tangent, block_lengths = block_item

        def forward(inputs, *weights):
            return layer(inputs, *weights, block_lengths)
        result, pullback = jax.vjp(forward, block_frames, *params)
        gradients = pullback(block_tangent)
        totals = tuple((running + gradient for running, gradient in zip(totals, gradients[1:])))
        return (totals, (result.astype(jnp.bfloat16), gradients[0].astype(jnp.bfloat16)))
    zeros = tuple((jnp.zeros_like(matrix) for matrix in params))
    totals, (outputs, input_grads) = lax.scan(one_block, zeros, (frame_blocks, tangent_blocks, length_blocks))
    return (outputs.reshape(CLIPS, PAD, D), input_grads.reshape(CLIPS, PAD, D), totals[0], totals[1], totals[2], totals[3], totals[4], totals[5], totals[6])
```

```python
import functools
import math

import jax
import jax.numpy as jnp
import numpy as np
from jax import lax
from jax.experimental import pallas as pl
from jax.experimental.pallas import tpu as pltpu
from jax.sharding import Mesh
from jax.sharding import PartitionSpec as P

HEADS = 16
WINDOW = 128


NORM_EPS = 1e-05
MASKED = -1e30


def norm_forward(values, gain_col, shift_col):
    row_mean = jnp.mean(values, axis=-1, keepdims=True)
    centred = values - row_mean
    inverse = lax.rsqrt(jnp.mean(centred * centred, axis=-1, keepdims=True) + NORM_EPS)
    normal = centred * inverse
    return (normal * gain_col + shift_col, normal, inverse)


def norm_backward(upstream, normal, inverse, gain_col):
    scaled = upstream * gain_col
    inner_term = (
        scaled
        - jnp.mean(scaled, axis=-1, keepdims=True)
        - normal * jnp.mean(scaled * normal, axis=-1, keepdims=True)
    )
    return (inverse * inner_term, jnp.sum(upstream * normal, axis=0), jnp.sum(upstream, axis=0))


def rotary_tables(places, head_dim):
    pair_count = head_dim // 2
    freq_rates = jnp.exp(
        jnp.arange(pair_count).astype(jnp.float32) * (-2.0 * math.log(10000.0) / head_dim)
    )
    angles = places.astype(jnp.float32)[:, None] * freq_rates[None, :]
    return (jnp.cos(angles), jnp.sin(angles))


def rotate(values, cosine, sine_table, direction):
    pair_count = values.shape[-1] // 2
    leading = values[..., :pair_count]
    trailing = values[..., pair_count:]
    cos_wide = cosine[:, None, :]
    sin_wide = sine_table[:, None, :] * direction
    return jnp.concatenate(
        [leading * cos_wide - trailing * sin_wide, trailing * cos_wide + leading * sin_wide],
        axis=-1,
    )


def inner_rows(left_op, right_op):
    return lax.dot_general(
        left_op, right_op, (((0,), (0,)), ((), ())), preferred_element_type=jnp.float32
    )


def times_transposed(left_op, right_op):
    return lax.dot_general(
        left_op, right_op, (((1,), (1,)), ((), ())), preferred_element_type=jnp.float32
    )


def body(
    frames,
    cotangent,
    lengths,
    qkv_weight,
    out_weight,
    gate_weight,
    up_weight,
    down_weight,
    gain_table,
    bias_table,
):
    seq_parts = lax.axis_size("seq")
    seq_index = lax.axis_index("seq")
    model_width = frames.shape[2]
    clip_len = frames.shape[1] * seq_parts
    head_dim = model_width // HEADS
    score_scale = 1.0 / math.sqrt(head_dim)
    frames_here, tangent_here = (frames, cotangent)
    places = seq_index * frames.shape[1] + jnp.arange(frames.shape[1])
    heads_here = HEADS // seq_parts
    groups, row_len = (frames_here.shape[0], frames_here.shape[1])
    row_count = groups * row_len
    width_here = heads_here * head_dim
    valid_rows = (places[None, :] < lengths[:, None]).astype(jnp.float32).reshape(row_count, 1)
    cosine, sine_table = rotary_tables(places, head_dim)
    full_cosine, full_sine = rotary_tables(jnp.arange(clip_len), head_dim)
    source = frames_here.astype(jnp.float32).reshape(row_count, model_width)
    normed_one, normal_one, inverse_one = norm_forward(source, gain_table[:, 0], bias_table[:, 0])
    normed_one = normed_one.astype(jnp.bfloat16)
    mixed_rows = jnp.dot(normed_one, qkv_weight, preferred_element_type=jnp.float32)
    shaped = mixed_rows.reshape(groups, row_len, 3, HEADS, head_dim)
    queries = (
        rotate(shaped[:, :, 0], cosine, sine_table, 1.0)
        .astype(jnp.bfloat16)
        .reshape(groups, row_len, model_width)
    )
    key_rows = (
        rotate(shaped[:, :, 1], cosine, sine_table, 1.0)
        .astype(jnp.bfloat16)
        .reshape(groups, row_len, model_width)
    )
    values = shaped[:, :, 2].astype(jnp.bfloat16).reshape(groups, row_len, model_width)
    head_queries, head_keys, head_values = (
        lax.all_to_all(queries, "seq", split_axis=2, concat_axis=1, tiled=True),
        lax.all_to_all(key_rows, "seq", split_axis=2, concat_axis=1, tiled=True),
        lax.all_to_all(values, "seq", split_axis=2, concat_axis=1, tiled=True),
    )
    head_queries = head_queries.reshape(groups, clip_len, heads_here, head_dim)
    head_keys = head_keys.reshape(groups, clip_len, heads_here, head_dim)
    head_values = head_values.reshape(groups, clip_len, heads_here, head_dim)
    query_pos = jnp.arange(clip_len)[:, None]
    key_pos = jnp.arange(clip_len)[None, :]
    window_mask = (key_pos <= query_pos) & (key_pos > query_pos - WINDOW)

    def clip_scores(clip_queries, clip_keys, length):
        products = jnp.einsum(
            "qhd,khd->hqk", clip_queries, clip_keys, preferred_element_type=jnp.float32
        )
        allowed = window_mask & (key_pos < length)
        return (jnp.where(allowed[None], products * score_scale, MASKED), allowed)

    def attend(block_item):
        clip_queries, clip_keys, clip_values, length = block_item
        scores, allowed = clip_scores(clip_queries, clip_keys, length)
        top_score = jnp.max(scores, axis=-1, keepdims=True)
        exponent = jnp.exp(scores - top_score)
        row_total = jnp.sum(exponent, axis=-1, keepdims=True)
        weights_low = (exponent / row_total).astype(jnp.bfloat16)
        context = jnp.einsum(
            "hqk,khd->qhd", weights_low, clip_values, preferred_element_type=jnp.float32
        )
        return (context.astype(jnp.bfloat16), top_score + jnp.log(row_total))

    context_heads, log_totals = lax.map(attend, (head_queries, head_keys, head_values, lengths))
    context_heads = context_heads.reshape(groups, clip_len, width_here)
    context = lax.all_to_all(context_heads, "seq", split_axis=1, concat_axis=2, tiled=True).reshape(
        row_count, model_width
    )
    attended = jnp.dot(context, out_weight, preferred_element_type=jnp.float32)
    middle = source + gain_table[:, 2] * attended
    normed_two, normal_two, inverse_two = norm_forward(middle, gain_table[:, 1], bias_table[:, 1])
    normed_two = normed_two.astype(jnp.bfloat16)
    gate_rows = jnp.dot(normed_two, gate_weight, preferred_element_type=jnp.float32)
    upward = jnp.dot(normed_two, up_weight, preferred_element_type=jnp.float32)
    sigmoid_gate = jax.nn.sigmoid(gate_rows)
    activated = gate_rows * sigmoid_gate
    hidden = (activated * upward).astype(jnp.bfloat16)
    branch = jnp.dot(hidden, down_weight, preferred_element_type=jnp.float32)
    output = (
        ((middle + gain_table[:, 3] * branch) * valid_rows)
        .astype(jnp.bfloat16)
        .reshape(groups, row_len, model_width)
    )
    output_delta = tangent_here.astype(jnp.float32).reshape(row_count, model_width) * valid_rows
    branch_delta = (output_delta * gain_table[:, 3]).astype(jnp.bfloat16)
    scale_mlp = jnp.sum(output_delta * branch, axis=0)
    down_grad = inner_rows(hidden, branch_delta)
    hidden_delta = times_transposed(branch_delta, down_weight)
    up_delta = (hidden_delta * activated).astype(jnp.bfloat16)
    gate_delta = (
        hidden_delta * upward * sigmoid_gate * (1.0 + gate_rows * (1.0 - sigmoid_gate))
    ).astype(jnp.bfloat16)
    gate_grad = inner_rows(normed_two, gate_delta)
    up_grad = inner_rows(normed_two, up_delta)
    second_delta = times_transposed(gate_delta, gate_weight) + times_transposed(up_delta, up_weight)
    back_two, gain_two, bias_two = norm_backward(
        second_delta, normal_two, inverse_two, gain_table[:, 1]
    )
    middle_delta = output_delta + back_two
    attended_delta = (middle_delta * gain_table[:, 2]).astype(jnp.bfloat16)
    scale_attn = jnp.sum(middle_delta * attended, axis=0)
    out_grad = inner_rows(context, attended_delta)
    context_delta = (
        times_transposed(attended_delta, out_weight)
        .astype(jnp.bfloat16)
        .reshape(groups, row_len, model_width)
    )
    context_heads_delta = lax.all_to_all(
        context_delta, "seq", split_axis=2, concat_axis=1, tiled=True
    )
    context_heads_delta = context_heads_delta.reshape(groups, clip_len, heads_here, head_dim)

    def attend_back(block_item):
        clip_queries, clip_keys, clip_values, length, log_total, clip_delta = block_item
        scores, allowed = clip_scores(clip_queries, clip_keys, length)
        weights = jnp.exp(scores - log_total)
        weights_low = weights.astype(jnp.bfloat16)
        weight_delta = jnp.einsum(
            "qhd,khd->hqk", clip_delta, clip_values, preferred_element_type=jnp.float32
        )
        row_inner = jnp.sum(weight_delta * weights, axis=-1, keepdims=True)
        product_delta = jnp.where(
            allowed[None], weights * (weight_delta - row_inner) * score_scale, 0.0
        ).astype(jnp.bfloat16)
        query_delta = jnp.einsum(
            "hqk,khd->qhd", product_delta, clip_keys, preferred_element_type=jnp.float32
        )
        key_delta = jnp.einsum(
            "hqk,qhd->khd", product_delta, clip_queries, preferred_element_type=jnp.float32
        )
        value_delta = jnp.einsum(
            "hqk,qhd->khd", weights_low, clip_delta, preferred_element_type=jnp.float32
        )
        query_delta = rotate(query_delta, full_cosine, full_sine, -1.0).astype(jnp.bfloat16)
        key_delta = rotate(key_delta, full_cosine, full_sine, -1.0).astype(jnp.bfloat16)
        return (query_delta, key_delta, value_delta.astype(jnp.bfloat16))

    query_delta, key_delta, value_delta = lax.map(
        attend_back,
        (head_queries, head_keys, head_values, lengths, log_totals, context_heads_delta),
    )
    query_delta = query_delta.reshape(groups, clip_len, width_here)
    key_delta = key_delta.reshape(groups, clip_len, width_here)
    value_delta = value_delta.reshape(groups, clip_len, width_here)
    query_back, key_back, value_back = (
        lax.all_to_all(query_delta, "seq", split_axis=1, concat_axis=2, tiled=True),
        lax.all_to_all(key_delta, "seq", split_axis=1, concat_axis=2, tiled=True),
        lax.all_to_all(value_delta, "seq", split_axis=1, concat_axis=2, tiled=True),
    )
    mixed_delta = jnp.concatenate(
        [
            query_back.reshape(row_count, model_width),
            key_back.reshape(row_count, model_width),
            value_back.reshape(row_count, model_width),
        ],
        axis=1,
    )
    qkv_grad = inner_rows(normed_one, mixed_delta)
    first_delta = times_transposed(mixed_delta, qkv_weight)
    back_one, gain_one, bias_one = norm_backward(
        first_delta, normal_one, inverse_one, gain_table[:, 0]
    )
    input_grad = (
        (middle_delta + back_one).astype(jnp.bfloat16).reshape(groups, row_len, model_width)
    )
    gain_grad = jnp.stack([gain_one, gain_two, scale_attn, scale_mlp], axis=1)
    bias_grad = jnp.stack([bias_one, bias_two], axis=1)
    over_clips = (
        lax.psum_scatter(qkv_grad, "dp", scatter_dimension=0, tiled=True),
        lax.psum_scatter(out_grad, "dp", scatter_dimension=0, tiled=True),
        lax.psum_scatter(gate_grad, "dp", scatter_dimension=0, tiled=True),
        lax.psum_scatter(up_grad, "dp", scatter_dimension=0, tiled=True),
        lax.psum_scatter(down_grad, "dp", scatter_dimension=0, tiled=True),
        lax.psum_scatter(gain_grad, "dp", scatter_dimension=0, tiled=True),
        lax.psum_scatter(bias_grad, "dp", scatter_dimension=0, tiled=True),
    )
    summed = (
        lax.psum_scatter(
            over_clips[0].astype(jnp.bfloat16), "seq", scatter_dimension=1, tiled=True
        ).astype(jnp.float32),
        lax.psum_scatter(
            over_clips[1].astype(jnp.bfloat16), "seq", scatter_dimension=1, tiled=True
        ).astype(jnp.float32),
        lax.psum_scatter(
            over_clips[2].astype(jnp.bfloat16), "seq", scatter_dimension=1, tiled=True
        ).astype(jnp.float32),
        lax.psum_scatter(
            over_clips[3].astype(jnp.bfloat16), "seq", scatter_dimension=1, tiled=True
        ).astype(jnp.float32),
        lax.psum_scatter(
            over_clips[4].astype(jnp.bfloat16), "seq", scatter_dimension=1, tiled=True
        ).astype(jnp.float32),
        lax.psum_scatter(
            over_clips[5].astype(jnp.bfloat16), "seq", scatter_dimension=1, tiled=True
        ).astype(jnp.float32),
        lax.psum_scatter(
            over_clips[6].astype(jnp.bfloat16), "seq", scatter_dimension=1, tiled=True
        ).astype(jnp.float32),
    )
    return (
        output,
        input_grad,
        summed[0],
        summed[1],
        summed[2],
        summed[3],
        summed[4],
        summed[5],
        summed[6],
    )


BF = jnp.bfloat16
F32 = jnp.float32
TILE = 128
MIB = 1024 * 1024


def mm(left, right):
    return lax.dot_general(left, right, (((1,), (0,)), ((), ())), preferred_element_type=F32)


def mm_t(left, right):
    return lax.dot_general(left, right, (((1,), (1,)), ((), ())), preferred_element_type=F32)


def t_mm(left, right):
    return lax.dot_general(left, right, (((0,), (0,)), ((), ())), preferred_element_type=F32)


def call_kernel(
    kernel, info, args, *, name, grid, ins, outs, shapes, scratch=(), vmem=48, cost=None, after=()
):
    flops, moved = cost
    count, unread = len(args), len(after)

    def run(info, *refs):
        kernel(info, *refs[:count], *refs[count + unread :])

    args = [*args, *after]
    ins = [*ins] + [pl.BlockSpec(memory_space=pl.ANY)] * unread
    return pl.pallas_call(
        run,
        grid_spec=pltpu.PrefetchScalarGridSpec(
            num_scalar_prefetch=1, grid=grid, in_specs=ins, out_specs=outs, scratch_shapes=scratch
        ),
        out_shape=shapes,
        compiler_params=pltpu.CompilerParams(
            dimension_semantics=("arbitrary",) * len(grid), vmem_limit_bytes=vmem * MIB
        ),
        cost_estimate=pl.CostEstimate(flops=int(flops), bytes_accessed=int(moved), transcendentals=0),
        name=name,
    )(info, *args)


def shape_of(shape, dtype=BF):
    return jax.ShapeDtypeStruct(shape, dtype)


def rows_spec(rows, width, column=0):
    return pl.BlockSpec((rows, width), lambda r, info: (r, column))


def whole_spec(shape):
    return pl.BlockSpec(shape, lambda r, info: (0,) * len(shape))


LEN0 = 5


def norm_stats(values):
    row_mean = jnp.mean(values, axis=-1, keepdims=True)
    centred = values - row_mean
    inverse = lax.rsqrt(jnp.mean(centred * centred, axis=-1, keepdims=True) + NORM_EPS)
    return centred * inverse, inverse


def norm_back(upstream, normal, inverse, gain):
    scaled = upstream * gain
    return inverse * (
        scaled
        - jnp.mean(scaled, axis=-1, keepdims=True)
        - normal * jnp.mean(scaled * normal, axis=-1, keepdims=True)
    )


def turn(values, cosine, sine_a, sine_b):
    return (
        values * cosine
        + pltpu.roll(values, TILE - 32, 1) * sine_a
        + pltpu.roll(values, 32, 1) * sine_b
    )


def column_sum(values):
    return jnp.sum(values, axis=0, keepdims=True)


def qkv_kernel(info, x_ref, w_ref, gb_ref, tab_ref, qkv_ref, n_ref):
    r = pl.program_id(0)
    live = info[3] < info[LEN0 + r]

    @pl.when(live)
    def _():
        normal, _ = norm_stats(x_ref[...].astype(F32))
        normed = (normal * gb_ref[0:1, :] + gb_ref[4:5, :]).astype(BF)
        n_ref[...] = normed
        width = normed.shape[1]
        cosine, sine_a, sine_b = tab_ref[0], tab_ref[1], tab_ref[2]
        for part in range(3):
            mixed = mm(normed, w_ref[:, part * width : (part + 1) * width])
            for t in range(width // TILE):
                piece = mixed[:, t * TILE : (t + 1) * TILE]
                if part < 2:
                    piece = turn(piece, cosine, sine_a, sine_b)
                at = part * width + t * TILE
                qkv_ref[:, at : at + TILE] = piece.astype(BF)

    @pl.when(jnp.logical_not(live))
    def _():
        qkv_ref[...] = jnp.zeros_like(qkv_ref)
        n_ref[...] = jnp.zeros_like(n_ref)


def halo_kernel(info, x_ref, wk_ref, wv_ref, gb_ref, tab_ref, kv_ref, n_ref):
    r = pl.program_id(0)
    live = jnp.logical_and(info[0] > 0, info[3] < info[LEN0 + r])

    @pl.when(live)
    def _():
        normal, _ = norm_stats(x_ref[...].astype(F32))
        normed = (normal * gb_ref[0:1, :] + gb_ref[4:5, :]).astype(BF)
        n_ref[...] = normed
        width = normed.shape[1]
        keys = mm(normed, wk_ref[...])
        for t in range(width // TILE):
            piece = keys[:, t * TILE : (t + 1) * TILE]
            kv_ref[:, t * TILE : (t + 1) * TILE] = turn(
                piece, tab_ref[0], tab_ref[1], tab_ref[2]
            ).astype(BF)
        kv_ref[:, width:] = mm(normed, wv_ref[...]).astype(BF)

    @pl.when(jnp.logical_not(live))
    def _():
        kv_ref[...] = jnp.zeros_like(kv_ref)
        n_ref[...] = jnp.zeros_like(n_ref)


def window_bias(info, clip, block):
    i = lax.broadcasted_iota(jnp.int32, (2 * TILE, 2 * TILE), 0) % TILE
    j = lax.broadcasted_iota(jnp.int32, (2 * TILE, 2 * TILE), 1)
    key = info[3] + (block - 1) * TILE + j
    allowed = (j > i) & (j <= i + TILE) & (key >= 0) & (key < info[LEN0 + clip])
    return jnp.where(allowed, 0.0, MASKED)


def two_heads(values):
    lane = lax.broadcasted_iota(jnp.int32, values.shape, 1)
    nought = jnp.zeros_like(values)
    return jnp.concatenate(
        [jnp.where(lane < 64, values, nought), jnp.where(lane < 64, nought, values)], axis=0
    )


def one_row(values):
    lane = lax.broadcasted_iota(jnp.int32, (TILE, TILE), 1)
    return jnp.where(lane < 64, values[:TILE], values[TILE:])


def key_window(halo_ref, own_ref, block, at, own_at):
    if block == 0:
        return jnp.concatenate(
            [halo_ref[:, at : at + TILE], own_ref[0:TILE, own_at : own_at + TILE]], axis=0
        )
    return own_ref[(block - 1) * TILE : (block + 1) * TILE, own_at : own_at + TILE]


def attend_kernel(scale, info, qkv_ref, kvh_ref, ctx_ref, lse_ref):
    clip = pl.program_id(0)
    rows, width = ctx_ref.shape
    for block in range(rows // TILE):
        live = info[3] + block * TILE < info[LEN0 + clip]
        at_rows = slice(block * TILE, (block + 1) * TILE)

        @pl.when(live)
        def _():
            bias = window_bias(info, clip, block)
            lane = lax.broadcasted_iota(jnp.int32, (TILE, TILE), 1)
            totals = jnp.zeros((TILE, TILE), F32)
            for pair in range(width // TILE):
                at = pair * TILE
                queries = two_heads(qkv_ref[at_rows, at : at + TILE])
                keys = key_window(kvh_ref, qkv_ref, block, at, width + at)
                values = key_window(kvh_ref, qkv_ref, block, width + at, 2 * width + at)
                scores = mm_t(queries, keys) * scale + bias
                top = jnp.max(scores, axis=1, keepdims=True)
                exponent = jnp.exp(scores - top)
                total = jnp.sum(exponent, axis=1, keepdims=True)
                weights = (exponent * (1.0 / total)).astype(BF)
                ctx_ref[at_rows, at : at + TILE] = one_row(mm(weights, values)).astype(BF)
                log_total = top + jnp.log(total)
                totals = jnp.where(lane == 2 * pair, log_total[:TILE], totals)
                totals = jnp.where(lane == 2 * pair + 1, log_total[TILE:], totals)
            lse_ref[at_rows, :] = totals

        @pl.when(jnp.logical_not(live))
        def _():
            ctx_ref[at_rows, :] = jnp.zeros((TILE, width), BF)
            lse_ref[at_rows, :] = jnp.zeros((TILE, TILE), F32)


def attend_back_kernel(
    scale, info, qkv_ref, kvh_ref, dctx_ref, lse_ref, tab_ref, tabh_ref, md_ref, mdh_ref, dk_acc, dv_acc
):
    clip = pl.program_id(0)
    rows, width = dctx_ref.shape
    blocks = rows // TILE
    first_live = info[3] < info[LEN0 + clip]

    @pl.when(jnp.logical_not(first_live))
    def _():
        md_ref[...] = jnp.zeros_like(md_ref)
        mdh_ref[...] = jnp.zeros_like(mdh_ref)

    @pl.when(first_live)
    def _():
        dk_acc[...] = jnp.zeros_like(dk_acc)
        dv_acc[...] = jnp.zeros_like(dv_acc)
        for block in range(blocks):
            at_rows = slice(block * TILE, (block + 1) * TILE)
            key_rows = slice(block * TILE, (block + 2) * TILE)
            live = info[3] + block * TILE < info[LEN0 + clip]

            @pl.when(live)
            def _():
                bias = window_bias(info, clip, block)
                for pair in range(width // TILE):
                    at = pair * TILE
                    queries = two_heads(qkv_ref[at_rows, at : at + TILE])
                    delta = two_heads(dctx_ref[at_rows, at : at + TILE])
                    keys = key_window(kvh_ref, qkv_ref, block, at, width + at)
                    values = key_window(kvh_ref, qkv_ref, block, width + at, 2 * width + at)
                    log_total = jnp.concatenate(
                        [
                            lse_ref[at_rows, 2 * pair : 2 * pair + 1],
                            lse_ref[at_rows, 2 * pair + 1 : 2 * pair + 2],
                        ],
                        axis=0,
                    )
                    weights = jnp.exp(mm_t(queries, keys) * scale + bias - log_total)
                    weight_delta = mm_t(delta, values)
                    inner = jnp.sum(weight_delta * weights, axis=1, keepdims=True)
                    product_delta = (weights * (weight_delta - inner) * scale).astype(BF)
                    query_delta = one_row(mm(product_delta, keys))
                    md_ref[at_rows, at : at + TILE] = turn(
                        query_delta, tab_ref[0, at_rows], -tab_ref[1, at_rows], -tab_ref[2, at_rows]
                    ).astype(BF)
                    dk_acc[key_rows, at : at + TILE] += t_mm(product_delta, queries)
                    dv_acc[key_rows, at : at + TILE] += t_mm(weights.astype(BF), delta)

            @pl.when(jnp.logical_not(live))
            def _():
                md_ref[at_rows, 0:width] = jnp.zeros((TILE, width), BF)

        for pair in range(width // TILE):
            at = pair * TILE
            mdh_ref[:, at : at + TILE] = turn(
                dk_acc[:TILE, at : at + TILE], tabh_ref[0], -tabh_ref[1], -tabh_ref[2]
            ).astype(BF)
            md_ref[:, width + at : width + at + TILE] = turn(
                dk_acc[TILE:, at : at + TILE], tab_ref[0], -tab_ref[1], -tab_ref[2]
            ).astype(BF)
        mdh_ref[:, width:] = dv_acc[0:TILE, :].astype(BF)
        md_ref[:, 2 * width :] = dv_acc[TILE:, :].astype(BF)


def out_kernel(info, ctx_ref, x_ref, w_ref, gb_ref, att_ref, n_ref):
    r = pl.program_id(0)
    live = info[3] < info[LEN0 + r]

    @pl.when(live)
    def _():
        attended = mm(ctx_ref[...], w_ref[...])
        att_ref[...] = attended
        middle = x_ref[...].astype(F32) + gb_ref[2:3, :] * attended
        normal, _ = norm_stats(middle)
        n_ref[...] = (normal * gb_ref[1:2, :] + gb_ref[5:6, :]).astype(BF)

    @pl.when(jnp.logical_not(live))
    def _():
        att_ref[...] = jnp.zeros_like(att_ref)
        n_ref[...] = jnp.zeros_like(n_ref)


def row_valid(info, clip, rows):
    place = info[3] + lax.broadcasted_iota(jnp.int32, (rows, 1), 0)
    return (place < info[LEN0 + clip]).astype(F32)


def output_kernel(info, x_ref, ct_ref, att_ref, ba_ref, bb_ref, gb_ref, out_ref, sum_ref):
    r = pl.program_id(0)
    valid = row_valid(info, r, x_ref.shape[0])
    branch = ba_ref[...].astype(F32) + bb_ref[...].astype(F32)
    middle = x_ref[...].astype(F32) + gb_ref[2:3, :] * att_ref[...]
    out_ref[...] = ((middle + gb_ref[3:4, :] * branch) * valid).astype(BF)
    part = column_sum(ct_ref[...].astype(F32) * valid * branch)

    @pl.when(r == 0)
    def _():
        sum_ref[...] = jnp.zeros_like(sum_ref)

    sum_ref[0:1, :] += part


def out_back_kernel(
    info, sa_ref, sb_ref, att_ref, x_ref, ct_ref, ctx_ref, w_ref, gb_ref,
    delta_ref, dctx_ref, keep_ref, send_ref, sum_ref, acc,
):
    r = pl.program_id(0)
    rows, width = x_ref.shape

    @pl.when(r == 0)
    def _():
        sum_ref[...] = jnp.zeros_like(sum_ref)
        acc[...] = jnp.zeros_like(acc)

    live = info[3] < info[LEN0 + r]

    @pl.when(live)
    def _():
        valid = row_valid(info, r, rows)
        attended = att_ref[...]
        middle = x_ref[...].astype(F32) + gb_ref[2:3, :] * attended
        normal, inverse = norm_stats(middle)
        second = sa_ref[...].astype(F32) + sb_ref[...].astype(F32)
        back = norm_back(second, normal, inverse, gb_ref[1:2, :])
        middle_delta = ct_ref[...].astype(F32) * valid + back
        delta_ref[...] = middle_delta
        attended_delta = (middle_delta * gb_ref[2:3, :]).astype(BF)
        dctx_ref[...] = mm_t(attended_delta, w_ref[...]).astype(BF)
        acc[...] += t_mm(ctx_ref[...], attended_delta)
        sum_ref[0:1, :] += column_sum(second * normal)
        sum_ref[1:2, :] += column_sum(middle_delta * attended)
        sum_ref[2:3, :] += column_sum(second)

    @pl.when(jnp.logical_not(live))
    def _():
        delta_ref[...] = jnp.zeros_like(delta_ref)
        dctx_ref[...] = jnp.zeros_like(dctx_ref)

    @pl.when(r == pl.num_programs(0) - 1)
    def _():
        half = width // 2
        for x in range(2):
            col = pl.multiple_of(((info[0] + x) % 2) * half, TILE)
            for y in range(2):
                for z in range(4):
                    base = z * 256 + ((info[1] + y) % 2) * 128
                    for c, ref in ((0, keep_ref), (1, send_ref)):
                        row = pl.multiple_of(base + ((info[2] + c) % 2) * 64, 64)
                        ref[x, y, z] = acc[pl.ds(row, 64), pl.ds(col, half)].astype(BF)


def qkv_grad_kernel(info, n_ref, md_ref, nh_ref, mdh_ref, keep_ref, send_ref, acc):
    t = pl.program_id(0)
    acc[...] = t_mm(n_ref[...], md_ref[...])

    @pl.when(jnp.logical_and(info[0] > 0, t >= 2))
    def _():
        acc[...] += t_mm(nh_ref[...], mdh_ref[...])

    for y in range(2):
        for z in range(4):
            z_there = (info[4] // 2 + z // 2) % 2 * 2 + (info[4] + z) % 2
            base = z_there * 256 + ((info[1] + y) % 2) * 128
            for c, ref in ((0, keep_ref), (1, send_ref)):
                row = pl.multiple_of(base + ((info[2] + c) % 2) * 64, 64)
                ref[0, y, z] = acc[pl.ds(row, 64), :].astype(BF)


def first_back_kernel(info, md_ref, w_ref, x_ref, delta_ref, gb_ref, out_ref, sum_ref):
    r = pl.program_id(0)

    @pl.when(r == 0)
    def _():
        sum_ref[...] = jnp.zeros_like(sum_ref)

    live = info[3] < info[LEN0 + r]

    @pl.when(live)
    def _():
        first = mm_t(md_ref[...], w_ref[...])
        normal, inverse = norm_stats(x_ref[...].astype(F32))
        out_ref[...] = delta_ref[...] + norm_back(first, normal, inverse, gb_ref[0:1, :])
        sum_ref[0:1, :] += column_sum(first * normal)
        sum_ref[1:2, :] += column_sum(first)

    @pl.when(jnp.logical_not(live))
    def _():
        out_ref[...] = jnp.zeros_like(out_ref)


def first_halo_kernel(info, mdh_ref, wk_ref, wv_ref, x_ref, out_ref, sum_ref):
    r = pl.program_id(0)
    width = x_ref.shape[1]

    @pl.when(r == 0)
    def _():
        sum_ref[...] = jnp.zeros_like(sum_ref)

    live = jnp.logical_and(info[0] > 0, info[3] < info[LEN0 + r])

    @pl.when(live)
    def _():
        first = mm_t(mdh_ref[:, :width], wk_ref[...]) + mm_t(mdh_ref[:, width:], wv_ref[...])
        out_ref[...] = first.astype(BF)
        normal, _ = norm_stats(x_ref[...].astype(F32))
        sum_ref[0:1, :] += column_sum(first * normal)
        sum_ref[1:2, :] += column_sum(first)

    @pl.when(jnp.logical_not(live))
    def _():
        out_ref[...] = jnp.zeros_like(out_ref)


def input_grad_kernel(info, part_ref, halo_ref, x_ref, gb_ref, out_ref):
    rows = part_ref.shape[0]
    split = rows - halo_ref.shape[0]
    out_ref[:split, :] = part_ref[:split, :].astype(BF)

    @pl.when(info[0] == 0)
    def _():
        normal, inverse = norm_stats(x_ref[split:, :].astype(F32))
        back = norm_back(halo_ref[...].astype(F32), normal, inverse, gb_ref[0:1, :])
        out_ref[split:, :] = (part_ref[split:, :] + back).astype(BF)

    @pl.when(info[0] > 0)
    def _():
        out_ref[split:, :] = part_ref[split:, :].astype(BF)


def ffn_kernel(c, z0, first, x_leads, half, info, n_own, n_other, b_own, b_other, *rest):
    if not first:
        br_in, se_in, *rest = rest
    wg_hbm, wu_hbm, wd_hbm, br_ref, se_ref, keep_ref, send_ref, wg, wu, wd, ag, au, ad, sems = rest
    r = pl.program_id(0)

    def copies():
        for x in range(2):
            for q in range(2):
                k = x * 2 + q
                d = ((info[0] + x) % 2 * 2 + z0) * 4 + (info[1] + q) % 2 * 2 + info[2]
                src = pl.ds(pl.multiple_of(d * 256 + c * TILE, TILE), TILE)
                dst = pl.ds(k * TILE, TILE)
                yield pltpu.make_async_copy(wg_hbm.at[:, src], wg.at[:, dst], sems.at[0, k])
                yield pltpu.make_async_copy(wu_hbm.at[:, src], wu.at[:, dst], sems.at[1, k])
                yield pltpu.make_async_copy(wd_hbm.at[src, :], wd.at[dst, :], sems.at[2, k])

    @pl.when(r == 0)
    def _():
        for copy in copies():
            copy.start()
        for copy in copies():
            copy.wait()

    own = r < half
    normed = jnp.where(own, n_own[...], n_other[...])
    delta = jnp.where(own, b_own[...], b_other[...])
    gate = mm(normed, wg[...])
    upward = mm(normed, wu[...])
    hidden_delta = mm_t(delta, wd[...])
    sigmoid = jax.nn.sigmoid(gate)
    active = gate * sigmoid
    hidden = (active * upward).astype(BF)
    up_delta = (hidden_delta * active).astype(BF)
    gate_delta = (hidden_delta * upward * (sigmoid + active * (1.0 - sigmoid))).astype(BF)
    branch = mm(hidden, wd[...])
    second = mm_t(gate_delta, wg[...]) + mm_t(up_delta, wu[...])
    if not first:
        branch = branch + br_in[...].astype(F32)
        second = second + se_in[...].astype(F32)
    br_ref[...] = branch.astype(BF)
    se_ref[...] = second.astype(BF)
    grads = (t_mm(normed, gate_delta), t_mm(normed, up_delta), t_mm(delta, hidden))

    @pl.when(r == 0)
    def _():
        for acc, grad in zip((ag, au, ad), grads):
            acc[...] = grad

    @pl.when(r > 0)
    def _():
        for acc, grad in zip((ag, au, ad), grads):
            acc[...] += grad

    @pl.when(r == pl.num_programs(0) - 1)
    def _():
        def put(x, y, tile, value):
            lead, other = (x, y) if x_leads else (y, x)
            ref = send_ref if lead else keep_ref
            ref[other, tile * TILE : (tile + 1) * TILE, :] = value.astype(BF)

        def block(i, n=1):
            return slice(i * TILE, (i + n) * TILE)

        for x in range(2):
            for y in range(2):
                for z in range(4):
                    here, there = block(z * 2 + y), block(z * 2 + 1 - y)
                    for q in range(2):
                        cols, turned = block(x * 2 + q), block(x * 2 + 1 - q)
                        for i, acc in enumerate((ag, au)):
                            value = jnp.where(info[1] == 0, acc[here, cols], acc[there, turned])
                            put(x, y, 8 * i + z * 2 + q, value)
                for z1 in range(2):
                    for dq in range(4):
                        value = jnp.where(
                            info[0] == 0,
                            ad[block(x * 4 + dq), block(z1 * 2 + y)],
                            ad[block((1 - x) * 4 + dq), block((1 - z1) * 2 + y)],
                        )
                        put(x, y, 16 + z1 * 4 + dq, value)


def ffn_call(c, z0, x_leads, info, pieces, weights, previous, after=(), block_rows=512):
    rows, width = pieces[0].shape
    half = rows // block_rows
    first = previous is None
    hidden = 4 * TILE

    def spec(index):
        return pl.BlockSpec((block_rows, width), index)

    own = spec(lambda r, info: (jnp.minimum(r, half - 1), 0))
    other = spec(lambda r, info: (jnp.maximum(r - half, 0), 0))
    every = spec(lambda r, info: (r, 0))
    packed = (2, 24 * TILE, TILE)
    extra = [] if first else list(previous)
    return call_kernel(
        functools.partial(ffn_kernel, c, z0, first, x_leads, half),
        info,
        [*pieces, *extra, *weights],
        name="feed_forward",
        grid=(2 * half,),
        ins=[own, other, own, other]
        + [every] * len(extra)
        + [pl.BlockSpec(memory_space=pl.ANY)] * 3,
        outs=[every, every, whole_spec(packed), whole_spec(packed)],
        shapes=[shape_of((2 * rows, width))] * 2 + [shape_of(packed)] * 2,
        scratch=[
            pltpu.VMEM((width, hidden), BF),
            pltpu.VMEM((width, hidden), BF),
            pltpu.VMEM((hidden, width), BF),
            pltpu.VMEM((width, hidden), F32),
            pltpu.VMEM((width, hidden), F32),
            pltpu.VMEM((width, hidden), F32),
            pltpu.SemaphoreType.DMA((3, 4)),
        ],
        vmem=56,
        cost=(18 * 2 * rows * width * hidden, 30 * MIB),
        after=after,
    )


SWAP = [(0, 1), (1, 0)]
Z_NEAR = [(0, 1), (1, 0), (2, 3), (3, 2)]
Z_FAR = [(0, 2), (2, 0), (1, 3), (3, 1)]


def swap(values, axis):
    return lax.ppermute(values, axis, SWAP)


def plus(left, right):
    return (left.astype(F32) + right.astype(F32)).astype(BF)


def fold(keep, send, axis):
    return plus(keep, swap(send, axis))


def fold_two(keep, send, lead, other):
    total = fold(keep, send, lead)
    return fold(total[0], total[1], other)


def scatter_z(values):
    return lax.psum_scatter(values, "z", scatter_dimension=0, tiled=True)[0]


def turn_table(first, last, head_dim):
    pairs = head_dim // 2
    rates = np.exp(np.arange(pairs, dtype=np.float32) * np.float32(-2.0 * math.log(10000.0) / head_dim))
    angles = np.arange(first, last, dtype=np.float32)[:, None] * rates[None, :].astype(np.float32)
    cosine, sine = (np.tile(t(angles), (1, TILE // pairs)) for t in (np.cos, np.sin))
    front = (np.arange(TILE) % head_dim < pairs)[None, :]
    return np.stack([cosine, np.where(front, -sine, 0), np.where(front, 0, sine)]).astype(np.float32)


def fast_body(
    frames, cotangent, lengths, qkv_weight, out_weight, gate_weight, up_weight, down_weight,
    gain_table, bias_table,
):
    clips, rows, width = frames.shape
    count = clips * rows
    head_dim = width // HEADS
    scale = 1.0 / math.sqrt(head_dim)
    x_at, y_at, core_at, z_at = (lax.axis_index(a) for a in ("seq", "y", "core", "z"))
    start = x_at * rows
    info = jnp.concatenate(
        [jnp.stack([x_at, y_at, core_at, start, z_at]).astype(jnp.int32), lengths.astype(jnp.int32)]
    )
    flat = frames.reshape(count, width)
    tangent = cotangent.reshape(count, width)
    halo = lax.ppermute(
        frames[:, rows - TILE :].reshape(clips * TILE, width), "seq", [(0, 1)]
    )
    places = start + jnp.arange(rows)
    valid = (places[None, :] < lengths[:, None]).astype(F32).reshape(count, 1)
    branch_delta = (tangent.astype(F32) * valid * gain_table[:, 3]).astype(BF)
    branch_delta_other = swap(branch_delta, "core")
    table = jnp.concatenate([gain_table, bias_table, jnp.zeros((width, 2), F32)], axis=1).T
    seats = lax.axis_size("seq")
    own_turns = jnp.asarray(turn_table(0, seats * rows, head_dim))
    halo_turns = jnp.asarray(
        np.concatenate([turn_table(i * rows - TILE, i * rows, head_dim) for i in range(seats)], axis=1)
    )
    own_tab = pl.BlockSpec((3, rows, TILE), lambda r, info: (0, info[0], 0))
    halo_tab = pl.BlockSpec((3, TILE, TILE), lambda r, info: (0, info[0], 0))
    gb = whole_spec(table.shape)
    own = rows_spec(rows, width)
    halo_rows = rows_spec(TILE, width)
    qkv_rows = rows_spec(rows, 3 * width)
    kv_rows = rows_spec(TILE, 2 * width)
    w_qkv = whole_spec((width, 3 * width))
    w_key = pl.BlockSpec((width, width), lambda r, info: (0, 1))
    w_value = pl.BlockSpec((width, width), lambda r, info: (0, 2))
    w_out = whole_spec((width, width))
    sums = whole_spec((8, width))
    grid = (clips,)
    mac = 2 * count * width * width

    qkv, normed_one = call_kernel(
        qkv_kernel, info, [flat, qkv_weight, table, own_turns], name="qkv", grid=grid,
        ins=[own, w_qkv, gb, own_tab], outs=[qkv_rows, own],
        shapes=[shape_of((count, 3 * width)), shape_of((count, width))], cost=(3 * mac, 16 * MIB),
    )
    kv_halo, normed_halo = call_kernel(
        halo_kernel, info, [halo, qkv_weight, qkv_weight, table, halo_turns], name="halo",
        grid=grid, ins=[halo_rows, w_key, w_value, gb, halo_tab],
        outs=[kv_rows, halo_rows],
        shapes=[shape_of((clips * TILE, 2 * width)), shape_of((clips * TILE, width))],
        cost=(mac, 8 * MIB),
    )
    context, log_totals = call_kernel(
        functools.partial(attend_kernel, scale), info, [qkv, kv_halo], name="attend", grid=grid,
        ins=[qkv_rows, kv_rows], outs=[own, rows_spec(rows, TILE)],
        shapes=[shape_of((count, width)), shape_of((count, TILE), F32)], cost=(4 * mac, 12 * MIB),
    )
    attended, normed_two = call_kernel(
        out_kernel, info, [context, flat, out_weight, table], name="project", grid=grid,
        ins=[own, own, w_out, gb], outs=[own, own],
        shapes=[shape_of((count, width), F32), shape_of((count, width))], cost=(mac, 12 * MIB),
    )
    normed_two_other = swap(normed_two, "core")

    pieces = (normed_two, normed_two_other, branch_delta, branch_delta_other)
    weights = (gate_weight, up_weight, down_weight)
    units = [(0, 0), (0, 1), (1, 0), (1, 1)]
    axes = [("seq", "y"), ("y", "seq")] * 2
    previous, first_sums = None, []

    def run_ffn(i, after):
        c, z0 = units[i]
        *state, keep, send = ffn_call(
            c, z0, axes[i][0] == "seq", info, pieces, weights, previous, after
        )
        return state, keep, swap(send, axes[i][0])

    def last_sum(total, i):
        return plus(total[0], swap(total[1], axes[i][1])).reshape(24, TILE, TILE)

    def z_sum(parts):
        gates = [
            part[8 * i : 8 * i + 8].reshape(4, 2, TILE, TILE) for part in parts for i in range(2)
        ]
        downs = jnp.stack([part[16:].reshape(2, 4, TILE, TILE) for part in parts], axis=1)
        return scatter_z(jnp.concatenate([*gates, downs.reshape(4, 4, TILE, TILE)], axis=1))

    previous, keep_0, came_0 = run_ffn(0, ())
    previous, keep_1, came_1 = run_ffn(1, ())
    previous, keep_2, came_2 = run_ffn(2, (came_0,))
    total_0 = plus(keep_0, came_0)
    previous, keep_3, came_3 = run_ffn(3, (total_0, came_1))
    total_1 = plus(keep_1, came_1)
    part_0 = last_sum(total_0, 0)
    branch, second = previous
    second_other = swap(second[count:], "core")
    branch_other = swap(branch[count:], "core")

    packed = (2, 2, 4, 64, width // 2)
    middle_delta, context_delta, out_keep, out_send, sums_two = call_kernel(
        out_back_kernel, info,
        [second, second_other, attended, flat, tangent, context, out_weight, table],
        name="project_back", grid=grid,
        ins=[own, own, own, own, own, own, w_out, gb],
        outs=[own, own, whole_spec(packed), whole_spec(packed), sums],
        shapes=[
            shape_of((count, width), F32), shape_of((count, width)), shape_of(packed),
            shape_of(packed), shape_of((8, width), F32),
        ],
        scratch=[pltpu.VMEM((width, width), F32)], cost=(2 * mac, 24 * MIB),
        after=(total_1, came_2),
    )
    total_2 = plus(keep_2, came_2)
    part_1 = last_sum(total_1, 1)
    out_came = swap(out_send, "core")

    output, sums_out = call_kernel(
        output_kernel, info, [flat, tangent, attended, branch, branch_other, table],
        name="output", grid=grid, ins=[own, own, own, own, own, gb], outs=[own, sums],
        shapes=[shape_of((count, width)), shape_of((8, width), F32)], cost=(0, 14 * MIB),
        after=(part_0, total_2, came_3),
    )
    total_3 = plus(keep_3, came_3)
    z_0 = z_sum((part_0, part_1))
    out_total = plus(out_keep, out_came)
    out_came = swap(out_total[1], "seq")

    mixed_delta, mixed_halo = call_kernel(
        functools.partial(attend_back_kernel, scale), info,
        [qkv, kv_halo, context_delta, log_totals, own_turns, halo_turns], name="attend_back", grid=grid,
        ins=[qkv_rows, kv_rows, own, rows_spec(rows, TILE), own_tab, halo_tab],
        outs=[qkv_rows, kv_rows],
        shapes=[shape_of((count, 3 * width)), shape_of((clips * TILE, 2 * width))],
        scratch=[pltpu.VMEM((rows + TILE, width), F32), pltpu.VMEM((rows + TILE, width), F32)],
        cost=(10 * mac, 24 * MIB), after=(total_3, out_total, part_1, sums_out),
    )
    part_2, part_3 = last_sum(total_2, 2), last_sum(total_3, 3)
    out_total = plus(out_total[0], out_came)
    out_grad = scatter_z(plus(out_total[0], swap(out_total[1], "y"))).astype(F32)
    first_halo, sums_halo = call_kernel(
        first_halo_kernel, info, [mixed_halo, qkv_weight, qkv_weight, halo], name="first_halo",
        grid=grid, ins=[kv_rows, w_key, w_value, halo_rows], outs=[halo_rows, sums],
        shapes=[shape_of((clips * TILE, width)), shape_of((8, width), F32)], cost=(mac, 8 * MIB),
    )
    first_back = lax.ppermute(first_halo, "seq", [(1, 0)])

    cut = 3 * width // 6
    packed = (2, 2, 4, 64, 3 * cut)
    out_spec = pl.BlockSpec(
        (1, 2, 4, 64, cut), lambda t, info: ((t // 3 + info[0]) % 2, 0, 0, 0, t % 3)
    )
    qkv_keep, qkv_send = call_kernel(
        qkv_grad_kernel, info, [normed_one, mixed_delta, normed_halo, mixed_halo],
        name="qkv_grad", grid=(6,),
        ins=[
            whole_spec((count, width)),
            pl.BlockSpec((count, cut), lambda t, info: (0, t)),
            whole_spec((clips * TILE, width)),
            pl.BlockSpec((clips * TILE, cut), lambda t, info: (0, jnp.maximum(t - 2, 0))),
        ],
        outs=[out_spec, out_spec], shapes=[shape_of(packed)] * 2,
        scratch=[pltpu.VMEM((width, cut), F32)], cost=(4 * mac, 16 * MIB), after=(first_halo, part_2, part_3),
    )
    z_1 = z_sum((part_2, part_3))
    qkv_total = fold(qkv_keep, qkv_send, "core")
    half = 32
    left, right = qkv_total[:, :, :, :half], qkv_total[:, :, :, half:]
    left = fold_two(left[0], left[1], "seq", "y")
    right = fold_two(right[:, 0], right[:, 1], "y", "seq")
    qkv_total = jnp.concatenate([left, right], axis=1).reshape(2, 2, 64, -1)
    for step, pairs in ((1, Z_NEAR), (2, Z_FAR)):
        keep, send = (qkv_total[:, 0], qkv_total[:, 1]) if step == 1 else (qkv_total[0], qkv_total[1])
        qkv_total = plus(keep, lax.ppermute(send, "z", pairs))
    qkv_grad = qkv_total.astype(F32)

    part_grad, sums_one = call_kernel(
        first_back_kernel, info, [mixed_delta, qkv_weight, flat, middle_delta, table],
        name="first_back", grid=grid, ins=[qkv_rows, w_qkv, own, own, gb], outs=[own, sums],
        shapes=[shape_of((count, width), F32), shape_of((8, width), F32)],
        cost=(3 * mac, 24 * MIB),
    )
    input_grad = call_kernel(
        input_grad_kernel, info, [part_grad, first_back, flat, table], name="input_grad",
        grid=grid, ins=[own, halo_rows, own, gb], outs=own, shapes=shape_of((count, width)),
        cost=(0, 8 * MIB),
    )

    ones = sums_one + sums_halo
    vectors = jnp.stack(
        [ones[0], sums_two[0], sums_two[1], sums_out[0], ones[1], sums_two[2], ones[2], ones[3]]
    )
    for axis, pairs in (("core", SWAP), ("seq", SWAP), ("y", SWAP), ("z", Z_NEAR), ("z", Z_FAR)):
        vectors = vectors + lax.ppermute(vectors, axis, pairs)
    vectors = vectors.T
    dp_at = (z_at * 2 + y_at) * 2 + core_at
    share = width // 16
    mine = lax.dynamic_slice_in_dim(vectors, dp_at * share, share, axis=0)
    gain_grad = lax.dynamic_slice_in_dim(mine[:, :4], x_at * 2, 2, axis=1)
    bias_grad = lax.dynamic_slice_in_dim(mine[:, 4:6], x_at, 1, axis=1)

    tiles = jnp.stack([z_0, z_1])
    gates = tiles[:, :8].reshape(2, 2, 2, 2, 2, share, TILE)
    kept = lax.dynamic_index_in_dim(gates, core_at, axis=4, keepdims=False)
    sent = lax.dynamic_index_in_dim(gates, 1 - core_at, axis=4, keepdims=False)
    came = swap(sent, "core")
    both = jnp.where(core_at == 0, jnp.stack([kept, came], 4), jnp.stack([came, kept], 4))
    both = both.transpose(2, 5, 1, 3, 4, 0, 6).astype(F32)
    gate_grad = both[0].reshape(share, -1)
    up_grad = both[1].reshape(share, -1)
    down_grad = tiles[:, 8:].reshape(2, width // 2, TILE).transpose(0, 2, 1).astype(F32)
    down_grad = down_grad.reshape(2 * TILE, width // 2)
    shape = (clips, rows, width)
    return (
        output.reshape(shape), input_grad.reshape(shape), qkv_grad, out_grad, gate_grad, up_grad,
        down_grad, gain_grad, bias_grad,
    )


def solution(mesh):
    placed = (("dp", "seq", None),) * 2 + (("dp",),) + ((),) * 7
    given = (("dp", "seq", None),) * 2 + (("dp", "seq"),) * 7
    fast = mesh.shape["dp"] == 16 and mesh.shape["seq"] == 2
    dp_axes = ("z", "y", "core") if fast else "dp"

    def specs(entries):
        return tuple(P(*(dp_axes if a == "dp" else a for a in entry)) for entry in entries)

    if fast:
        mesh = Mesh(mesh.devices.reshape(4, 2, 2, 2), ("z", "y", "core", "seq"))
    return jax.shard_map(
        fast_body if fast else body,
        mesh=mesh,
        in_specs=specs(placed),
        out_specs=specs(given),
        check_vma=False,
    )
```

```python
import functools
import math

import jax
import jax.numpy as jnp
import numpy as np
from jax import lax
from jax.experimental import pallas as pl
from jax.experimental.pallas import tpu as pltpu
from jax.sharding import Mesh
from jax.sharding import PartitionSpec as P

HEADS = 16
WINDOW = 128


NORM_EPS = 1e-05
MASKED = -1e30


def norm_forward(values, gain_col, shift_col):
    row_mean = jnp.mean(values, axis=-1, keepdims=True)
    centred = values - row_mean
    inverse = lax.rsqrt(jnp.mean(centred * centred, axis=-1, keepdims=True) + NORM_EPS)
    normal = centred * inverse
    return (normal * gain_col + shift_col, normal, inverse)


def norm_backward(upstream, normal, inverse, gain_col):
    scaled = upstream * gain_col
    inner_term = (
        scaled
        - jnp.mean(scaled, axis=-1, keepdims=True)
        - normal * jnp.mean(scaled * normal, axis=-1, keepdims=True)
    )
    return (inverse * inner_term, jnp.sum(upstream * normal, axis=0), jnp.sum(upstream, axis=0))


def rotary_tables(places, head_dim):
    pair_count = head_dim // 2
    freq_rates = jnp.exp(
        jnp.arange(pair_count).astype(jnp.float32) * (-2.0 * math.log(10000.0) / head_dim)
    )
    angles = places.astype(jnp.float32)[:, None] * freq_rates[None, :]
    return (jnp.cos(angles), jnp.sin(angles))


def rotate(values, cosine, sine_table, direction):
    pair_count = values.shape[-1] // 2
    leading = values[..., :pair_count]
    trailing = values[..., pair_count:]
    cos_wide = cosine[:, None, :]
    sin_wide = sine_table[:, None, :] * direction
    return jnp.concatenate(
        [leading * cos_wide - trailing * sin_wide, trailing * cos_wide + leading * sin_wide],
        axis=-1,
    )


def inner_rows(left_op, right_op):
    return lax.dot_general(
        left_op, right_op, (((0,), (0,)), ((), ())), preferred_element_type=jnp.float32
    )


def times_transposed(left_op, right_op):
    return lax.dot_general(
        left_op, right_op, (((1,), (1,)), ((), ())), preferred_element_type=jnp.float32
    )


def body(
    frames,
    cotangent,
    lengths,
    qkv_weight,
    out_weight,
    gate_weight,
    up_weight,
    down_weight,
    gain_table,
    bias_table,
):
    seq_parts = lax.axis_size("seq")
    seq_index = lax.axis_index("seq")
    model_width = frames.shape[2]
    clip_len = frames.shape[1] * seq_parts
    head_dim = model_width // HEADS
    score_scale = 1.0 / math.sqrt(head_dim)
    frames_here, tangent_here = (frames, cotangent)
    places = seq_index * frames.shape[1] + jnp.arange(frames.shape[1])
    heads_here = HEADS // seq_parts
    groups, row_len = (frames_here.shape[0], frames_here.shape[1])
    row_count = groups * row_len
    width_here = heads_here * head_dim
    valid_rows = (places[None, :] < lengths[:, None]).astype(jnp.float32).reshape(row_count, 1)
    cosine, sine_table = rotary_tables(places, head_dim)
    full_cosine, full_sine = rotary_tables(jnp.arange(clip_len), head_dim)
    source = frames_here.astype(jnp.float32).reshape(row_count, model_width)
    normed_one, normal_one, inverse_one = norm_forward(source, gain_table[:, 0], bias_table[:, 0])
    normed_one = normed_one.astype(jnp.bfloat16)
    mixed_rows = jnp.dot(normed_one, qkv_weight, preferred_element_type=jnp.float32)
    shaped = mixed_rows.reshape(groups, row_len, 3, HEADS, head_dim)
    queries = (
        rotate(shaped[:, :, 0], cosine, sine_table, 1.0)
        .astype(jnp.bfloat16)
        .reshape(groups, row_len, model_width)
    )
    key_rows = (
        rotate(shaped[:, :, 1], cosine, sine_table, 1.0)
        .astype(jnp.bfloat16)
        .reshape(groups, row_len, model_width)
    )
    values = shaped[:, :, 2].astype(jnp.bfloat16).reshape(groups, row_len, model_width)
    head_queries, head_keys, head_values = (
        lax.all_to_all(queries, "seq", split_axis=2, concat_axis=1, tiled=True),
        lax.all_to_all(key_rows, "seq", split_axis=2, concat_axis=1, tiled=True),
        lax.all_to_all(values, "seq", split_axis=2, concat_axis=1, tiled=True),
    )
    head_queries = head_queries.reshape(groups, clip_len, heads_here, head_dim)
    head_keys = head_keys.reshape(groups, clip_len, heads_here, head_dim)
    head_values = head_values.reshape(groups, clip_len, heads_here, head_dim)
    query_pos = jnp.arange(clip_len)[:, None]
    key_pos = jnp.arange(clip_len)[None, :]
    window_mask = (key_pos <= query_pos) & (key_pos > query_pos - WINDOW)

    def clip_scores(clip_queries, clip_keys, length):
        products = jnp.einsum(
            "qhd,khd->hqk", clip_queries, clip_keys, preferred_element_type=jnp.float32
        )
        allowed = window_mask & (key_pos < length)
        return (jnp.where(allowed[None], products * score_scale, MASKED), allowed)

    def attend(block_item):
        clip_queries, clip_keys, clip_values, length = block_item
        scores, allowed = clip_scores(clip_queries, clip_keys, length)
        top_score = jnp.max(scores, axis=-1, keepdims=True)
        exponent = jnp.exp(scores - top_score)
        row_total = jnp.sum(exponent, axis=-1, keepdims=True)
        weights_low = (exponent / row_total).astype(jnp.bfloat16)
        context = jnp.einsum(
            "hqk,khd->qhd", weights_low, clip_values, preferred_element_type=jnp.float32
        )
        return (context.astype(jnp.bfloat16), top_score + jnp.log(row_total))

    context_heads, log_totals = lax.map(attend, (head_queries, head_keys, head_values, lengths))
    context_heads = context_heads.reshape(groups, clip_len, width_here)
    context = lax.all_to_all(context_heads, "seq", split_axis=1, concat_axis=2, tiled=True).reshape(
        row_count, model_width
    )
    attended = jnp.dot(context, out_weight, preferred_element_type=jnp.float32)
    middle = source + gain_table[:, 2] * attended
    normed_two, normal_two, inverse_two = norm_forward(middle, gain_table[:, 1], bias_table[:, 1])
    normed_two = normed_two.astype(jnp.bfloat16)
    gate_rows = jnp.dot(normed_two, gate_weight, preferred_element_type=jnp.float32)
    upward = jnp.dot(normed_two, up_weight, preferred_element_type=jnp.float32)
    sigmoid_gate = jax.nn.sigmoid(gate_rows)
    activated = gate_rows * sigmoid_gate
    hidden = (activated * upward).astype(jnp.bfloat16)
    branch = jnp.dot(hidden, down_weight, preferred_element_type=jnp.float32)
    output = (
        ((middle + gain_table[:, 3] * branch) * valid_rows)
        .astype(jnp.bfloat16)
        .reshape(groups, row_len, model_width)
    )
    output_delta = tangent_here.astype(jnp.float32).reshape(row_count, model_width) * valid_rows
    branch_delta = (output_delta * gain_table[:, 3]).astype(jnp.bfloat16)
    scale_mlp = jnp.sum(output_delta * branch, axis=0)
    down_grad = inner_rows(hidden, branch_delta)
    hidden_delta = times_transposed(branch_delta, down_weight)
    up_delta = (hidden_delta * activated).astype(jnp.bfloat16)
    gate_delta = (
        hidden_delta * upward * sigmoid_gate * (1.0 + gate_rows * (1.0 - sigmoid_gate))
    ).astype(jnp.bfloat16)
    gate_grad = inner_rows(normed_two, gate_delta)
    up_grad = inner_rows(normed_two, up_delta)
    second_delta = times_transposed(gate_delta, gate_weight) + times_transposed(up_delta, up_weight)
    back_two, gain_two, bias_two = norm_backward(
        second_delta, normal_two, inverse_two, gain_table[:, 1]
    )
    middle_delta = output_delta + back_two
    attended_delta = (middle_delta * gain_table[:, 2]).astype(jnp.bfloat16)
    scale_attn = jnp.sum(middle_delta * attended, axis=0)
    out_grad = inner_rows(context, attended_delta)
    context_delta = (
        times_transposed(attended_delta, out_weight)
        .astype(jnp.bfloat16)
        .reshape(groups, row_len, model_width)
    )
    context_heads_delta = lax.all_to_all(
        context_delta, "seq", split_axis=2, concat_axis=1, tiled=True
    )
    context_heads_delta = context_heads_delta.reshape(groups, clip_len, heads_here, head_dim)

    def attend_back(block_item):
        clip_queries, clip_keys, clip_values, length, log_total, clip_delta = block_item
        scores, allowed = clip_scores(clip_queries, clip_keys, length)
        weights = jnp.exp(scores - log_total)
        weights_low = weights.astype(jnp.bfloat16)
        weight_delta = jnp.einsum(
            "qhd,khd->hqk", clip_delta, clip_values, preferred_element_type=jnp.float32
        )
        row_inner = jnp.sum(weight_delta * weights, axis=-1, keepdims=True)
        product_delta = jnp.where(
            allowed[None], weights * (weight_delta - row_inner) * score_scale, 0.0
        ).astype(jnp.bfloat16)
        query_delta = jnp.einsum(
            "hqk,khd->qhd", product_delta, clip_keys, preferred_element_type=jnp.float32
        )
        key_delta = jnp.einsum(
            "hqk,qhd->khd", product_delta, clip_queries, preferred_element_type=jnp.float32
        )
        value_delta = jnp.einsum(
            "hqk,qhd->khd", weights_low, clip_delta, preferred_element_type=jnp.float32
        )
        query_delta = rotate(query_delta, full_cosine, full_sine, -1.0).astype(jnp.bfloat16)
        key_delta = rotate(key_delta, full_cosine, full_sine, -1.0).astype(jnp.bfloat16)
        return (query_delta, key_delta, value_delta.astype(jnp.bfloat16))

    query_delta, key_delta, value_delta = lax.map(
        attend_back,
        (head_queries, head_keys, head_values, lengths, log_totals, context_heads_delta),
    )
    query_delta = query_delta.reshape(groups, clip_len, width_here)
    key_delta = key_delta.reshape(groups, clip_len, width_here)
    value_delta = value_delta.reshape(groups, clip_len, width_here)
    query_back, key_back, value_back = (
        lax.all_to_all(query_delta, "seq", split_axis=1, concat_axis=2, tiled=True),
        lax.all_to_all(key_delta, "seq", split_axis=1, concat_axis=2, tiled=True),
        lax.all_to_all(value_delta, "seq", split_axis=1, concat_axis=2, tiled=True),
    )
    mixed_delta = jnp.concatenate(
        [
            query_back.reshape(row_count, model_width),
            key_back.reshape(row_count, model_width),
            value_back.reshape(row_count, model_width),
        ],
        axis=1,
    )
    qkv_grad = inner_rows(normed_one, mixed_delta)
    first_delta = times_transposed(mixed_delta, qkv_weight)
    back_one, gain_one, bias_one = norm_backward(
        first_delta, normal_one, inverse_one, gain_table[:, 0]
    )
    input_grad = (
        (middle_delta + back_one).astype(jnp.bfloat16).reshape(groups, row_len, model_width)
    )
    gain_grad = jnp.stack([gain_one, gain_two, scale_attn, scale_mlp], axis=1)
    bias_grad = jnp.stack([bias_one, bias_two], axis=1)
    over_clips = (
        lax.psum_scatter(qkv_grad, "dp", scatter_dimension=0, tiled=True),
        lax.psum_scatter(out_grad, "dp", scatter_dimension=0, tiled=True),
        lax.psum_scatter(gate_grad, "dp", scatter_dimension=0, tiled=True),
        lax.psum_scatter(up_grad, "dp", scatter_dimension=0, tiled=True),
        lax.psum_scatter(down_grad, "dp", scatter_dimension=0, tiled=True),
        lax.psum_scatter(gain_grad, "dp", scatter_dimension=0, tiled=True),
        lax.psum_scatter(bias_grad, "dp", scatter_dimension=0, tiled=True),
    )
    summed = (
        lax.psum_scatter(
            over_clips[0].astype(jnp.bfloat16), "seq", scatter_dimension=1, tiled=True
        ).astype(jnp.float32),
        lax.psum_scatter(
            over_clips[1].astype(jnp.bfloat16), "seq", scatter_dimension=1, tiled=True
        ).astype(jnp.float32),
        lax.psum_scatter(
            over_clips[2].astype(jnp.bfloat16), "seq", scatter_dimension=1, tiled=True
        ).astype(jnp.float32),
        lax.psum_scatter(
            over_clips[3].astype(jnp.bfloat16), "seq", scatter_dimension=1, tiled=True
        ).astype(jnp.float32),
        lax.psum_scatter(
            over_clips[4].astype(jnp.bfloat16), "seq", scatter_dimension=1, tiled=True
        ).astype(jnp.float32),
        lax.psum_scatter(
            over_clips[5].astype(jnp.bfloat16), "seq", scatter_dimension=1, tiled=True
        ).astype(jnp.float32),
        lax.psum_scatter(
            over_clips[6].astype(jnp.bfloat16), "seq", scatter_dimension=1, tiled=True
        ).astype(jnp.float32),
    )
    return (
        output,
        input_grad,
        summed[0],
        summed[1],
        summed[2],
        summed[3],
        summed[4],
        summed[5],
        summed[6],
    )


BF = jnp.bfloat16
F32 = jnp.float32
TILE = 128
MIB = 1024 * 1024
HINT = 0.25


def mm(left, right):
    return lax.dot_general(left, right, (((1,), (0,)), ((), ())), preferred_element_type=F32)


def mm_t(left, right):
    return lax.dot_general(left, right, (((1,), (1,)), ((), ())), preferred_element_type=F32)


def t_mm(left, right):
    return lax.dot_general(left, right, (((0,), (0,)), ((), ())), preferred_element_type=F32)


def call_kernel(
    kernel, info, args, *, name, grid, ins, outs, shapes, scratch=(), vmem=60, cost=None, after=(),
    onto=(),
):
    flops, moved = cost
    aliases = {1 + len(args) + len(after) + k: k for k in range(len(onto))}
    after = (*after, *onto)
    count, unread = len(args), len(after)

    def run(info, *refs):
        kernel(info, *refs[:count], *refs[count + unread :])

    args = [*args, *after]
    ins = [*ins] + [pl.BlockSpec(memory_space=pl.ANY)] * unread
    return pl.pallas_call(
        run,
        grid_spec=pltpu.PrefetchScalarGridSpec(
            num_scalar_prefetch=1, grid=grid, in_specs=ins, out_specs=outs, scratch_shapes=scratch
        ),
        out_shape=shapes,
        input_output_aliases=aliases,
        compiler_params=pltpu.CompilerParams(
            dimension_semantics=("arbitrary",) * len(grid), vmem_limit_bytes=vmem * MIB
        ),
        cost_estimate=pl.CostEstimate(
            flops=int(flops * HINT), bytes_accessed=int(moved * HINT), transcendentals=0
        ),
        name=name,
    )(info, *args)


def shape_of(shape, dtype=BF):
    return jax.ShapeDtypeStruct(shape, dtype)


def rows_spec(rows, width, column=0):
    return pl.BlockSpec((rows, width), lambda r, info: (r, column))


def whole_spec(shape):
    return pl.BlockSpec(shape, lambda r, info: (0,) * len(shape))


LEN0 = 5


def norm_stats(values):
    row_mean = jnp.mean(values, axis=-1, keepdims=True)
    centred = values - row_mean
    inverse = lax.rsqrt(jnp.mean(centred * centred, axis=-1, keepdims=True) + NORM_EPS)
    return centred * inverse, inverse


def norm_back(upstream, normal, inverse, gain):
    scaled = upstream * gain
    return inverse * (
        scaled
        - jnp.mean(scaled, axis=-1, keepdims=True)
        - normal * jnp.mean(scaled * normal, axis=-1, keepdims=True)
    )


def turn(values, cosine, sine_a, sine_b):
    return (
        values * cosine
        + pltpu.roll(values, TILE - 32, 1) * sine_a
        + pltpu.roll(values, 32, 1) * sine_b
    )


def column_sum(values):
    return jnp.sum(values, axis=0, keepdims=True)


def qkv_kernel(info, x_ref, w_ref, gb_ref, tab_ref, qkv_ref, n_ref):
    r = pl.program_id(0)
    live = info[3] < info[LEN0 + r]

    @pl.when(live)
    def _():
        normal, _ = norm_stats(x_ref[...].astype(F32))
        normed = (normal * gb_ref[0:1, :] + gb_ref[4:5, :]).astype(BF)
        n_ref[...] = normed
        width = normed.shape[1]
        cosine, sine_a, sine_b = tab_ref[0], tab_ref[1], tab_ref[2]
        for part in range(3):
            mixed = mm(normed, w_ref[:, part * width : (part + 1) * width])
            for t in range(width // TILE):
                piece = mixed[:, t * TILE : (t + 1) * TILE]
                if part < 2:
                    piece = turn(piece, cosine, sine_a, sine_b)
                at = part * width + t * TILE
                qkv_ref[:, at : at + TILE] = piece.astype(BF)

    @pl.when(jnp.logical_not(live))
    def _():
        qkv_ref[...] = jnp.zeros_like(qkv_ref)
        n_ref[...] = jnp.zeros_like(n_ref)


def halo_kernel(info, x_ref, wk_ref, wv_ref, gb_ref, tab_ref, kv_ref, n_ref):
    r = pl.program_id(0)
    live = jnp.logical_and(info[0] > 0, info[3] < info[LEN0 + r])

    @pl.when(live)
    def _():
        normal, _ = norm_stats(x_ref[...].astype(F32))
        normed = (normal * gb_ref[0:1, :] + gb_ref[4:5, :]).astype(BF)
        n_ref[...] = normed
        width = normed.shape[1]
        keys = mm(normed, wk_ref[...])
        for t in range(width // TILE):
            piece = keys[:, t * TILE : (t + 1) * TILE]
            kv_ref[:, t * TILE : (t + 1) * TILE] = turn(
                piece, tab_ref[0], tab_ref[1], tab_ref[2]
            ).astype(BF)
        kv_ref[:, width:] = mm(normed, wv_ref[...]).astype(BF)

    @pl.when(jnp.logical_not(live))
    def _():
        kv_ref[...] = jnp.zeros_like(kv_ref)
        n_ref[...] = jnp.zeros_like(n_ref)


def window_bias(info, clip, block):
    i = lax.broadcasted_iota(jnp.int32, (2 * TILE, 2 * TILE), 0) % TILE
    j = lax.broadcasted_iota(jnp.int32, (2 * TILE, 2 * TILE), 1)
    key = info[3] + (block - 1) * TILE + j
    allowed = (j > i) & (j <= i + TILE) & (key >= 0) & (key < info[LEN0 + clip])
    return jnp.where(allowed, 0.0, MASKED)


def two_heads(values):
    lane = lax.broadcasted_iota(jnp.int32, values.shape, 1)
    nought = jnp.zeros_like(values)
    return jnp.concatenate(
        [jnp.where(lane < 64, values, nought), jnp.where(lane < 64, nought, values)], axis=0
    )


def one_row(values):
    lane = lax.broadcasted_iota(jnp.int32, (TILE, TILE), 1)
    return jnp.where(lane < 64, values[:TILE], values[TILE:])


def key_window(halo_ref, own_ref, block, at, own_at):
    if block == 0:
        return jnp.concatenate(
            [halo_ref[:, at : at + TILE], own_ref[0:TILE, own_at : own_at + TILE]], axis=0
        )
    return own_ref[(block - 1) * TILE : (block + 1) * TILE, own_at : own_at + TILE]


def attend_kernel(scale, block, info, qkv_ref, kvh_ref, ctx_ref, lse_ref):
    clip = pl.program_id(0)
    width = ctx_ref.shape[1]
    at_rows = slice(block * TILE, (block + 1) * TILE)
    live = info[3] + block * TILE < info[LEN0 + clip]

    @pl.when(live)
    def _():
        bias = window_bias(info, clip, block)
        lane = lax.broadcasted_iota(jnp.int32, (TILE, TILE), 1)
        totals = jnp.zeros((TILE, TILE), F32)
        for pair in range(width // TILE):
            at = pair * TILE
            queries = two_heads(qkv_ref[at_rows, at : at + TILE])
            keys = key_window(kvh_ref, qkv_ref, block, at, width + at)
            values = key_window(kvh_ref, qkv_ref, block, width + at, 2 * width + at)
            scores = mm_t(queries, keys) * scale + bias
            top = jnp.max(scores, axis=1, keepdims=True)
            exponent = jnp.exp(scores - top)
            total = jnp.sum(exponent, axis=1, keepdims=True)
            weights = (exponent * (1.0 / total)).astype(BF)
            ctx_ref[:, at : at + TILE] = one_row(mm(weights, values)).astype(BF)
            log_total = top + jnp.log(total)
            totals = jnp.where(lane == 2 * pair, log_total[:TILE], totals)
            totals = jnp.where(lane == 2 * pair + 1, log_total[TILE:], totals)
        lse_ref[...] = totals

    @pl.when(jnp.logical_not(live))
    def _():
        ctx_ref[...] = jnp.zeros_like(ctx_ref)
        lse_ref[...] = jnp.zeros_like(lse_ref)


def attend_late_kernel(scale, info, qkv_ref, ctx_ref, lse_ref):
    attend_kernel(scale, 1, info, qkv_ref, None, ctx_ref, lse_ref)


def attend_back_kernel(
    scale, first_clip, info, qkv_ref, kvh_ref, dctx_ref, lse_ref, tab_ref, tabh_ref, md_ref, mdh_ref, dk_acc, dv_acc
):
    clip = pl.program_id(0) + first_clip
    rows, width = dctx_ref.shape
    blocks = rows // TILE
    first_live = info[3] < info[LEN0 + clip]

    @pl.when(jnp.logical_not(first_live))
    def _():
        md_ref[...] = jnp.zeros_like(md_ref)
        mdh_ref[...] = jnp.zeros_like(mdh_ref)

    @pl.when(first_live)
    def _():
        dk_acc[...] = jnp.zeros_like(dk_acc)
        dv_acc[...] = jnp.zeros_like(dv_acc)
        for block in range(blocks):
            at_rows = slice(block * TILE, (block + 1) * TILE)
            key_rows = slice(block * TILE, (block + 2) * TILE)
            live = info[3] + block * TILE < info[LEN0 + clip]

            @pl.when(live)
            def _():
                bias = window_bias(info, clip, block)
                for pair in range(width // TILE):
                    at = pair * TILE
                    queries = two_heads(qkv_ref[at_rows, at : at + TILE])
                    delta = two_heads(dctx_ref[at_rows, at : at + TILE])
                    keys = key_window(kvh_ref, qkv_ref, block, at, width + at)
                    values = key_window(kvh_ref, qkv_ref, block, width + at, 2 * width + at)
                    log_total = jnp.concatenate(
                        [
                            lse_ref[at_rows, 2 * pair : 2 * pair + 1],
                            lse_ref[at_rows, 2 * pair + 1 : 2 * pair + 2],
                        ],
                        axis=0,
                    )
                    weights = jnp.exp(mm_t(queries, keys) * scale + bias - log_total)
                    weight_delta = mm_t(delta, values)
                    inner = jnp.sum(weight_delta * weights, axis=1, keepdims=True)
                    product_delta = (weights * (weight_delta - inner) * scale).astype(BF)
                    query_delta = one_row(mm(product_delta, keys))
                    md_ref[at_rows, at : at + TILE] = turn(
                        query_delta, tab_ref[0, at_rows], -tab_ref[1, at_rows], -tab_ref[2, at_rows]
                    ).astype(BF)
                    dk_acc[key_rows, at : at + TILE] += t_mm(product_delta, queries)
                    dv_acc[key_rows, at : at + TILE] += t_mm(weights.astype(BF), delta)

            @pl.when(jnp.logical_not(live))
            def _():
                md_ref[at_rows, 0:width] = jnp.zeros((TILE, width), BF)

        for pair in range(width // TILE):
            at = pair * TILE
            mdh_ref[:, at : at + TILE] = turn(
                dk_acc[:TILE, at : at + TILE], tabh_ref[0], -tabh_ref[1], -tabh_ref[2]
            ).astype(BF)
            md_ref[:, width + at : width + at + TILE] = turn(
                dk_acc[TILE:, at : at + TILE], tab_ref[0], -tab_ref[1], -tab_ref[2]
            ).astype(BF)
        mdh_ref[:, width:] = dv_acc[0:TILE, :].astype(BF)
        md_ref[:, 2 * width :] = dv_acc[TILE:, :].astype(BF)


def out_kernel(info, ctx_ref, x_ref, w_ref, gb_ref, att_ref, n_ref):
    r = pl.program_id(0)
    live = info[3] < info[LEN0 + r]

    @pl.when(live)
    def _():
        attended = mm(ctx_ref[...], w_ref[...])
        att_ref[...] = attended
        middle = x_ref[...].astype(F32) + gb_ref[2:3, :] * attended
        normal, _ = norm_stats(middle)
        n_ref[...] = (normal * gb_ref[1:2, :] + gb_ref[5:6, :]).astype(BF)

    @pl.when(jnp.logical_not(live))
    def _():
        att_ref[...] = jnp.zeros_like(att_ref)
        n_ref[...] = jnp.zeros_like(n_ref)


def row_valid(info, clip, rows):
    place = info[3] + lax.broadcasted_iota(jnp.int32, (rows, 1), 0)
    return (place < info[LEN0 + clip]).astype(F32)


def output_kernel(info, x_ref, att_ref, ba_ref, bb_ref, gb_ref, out_ref):
    r = pl.program_id(0)
    valid = row_valid(info, r, x_ref.shape[0])
    branch = ba_ref[...].astype(F32) + bb_ref[0].astype(F32)
    middle = x_ref[...].astype(F32) + gb_ref[2:3, :] * att_ref[...]
    out_ref[...] = ((middle + gb_ref[3:4, :] * branch) * valid).astype(BF)


def out_back_kernel(
    info, sa_ref, sb_ref, ba_ref, bb_ref, att_ref, x_ref, ct_ref, ctx_ref, w_ref, gb_ref,
    delta_ref, dctx_ref, out_ref, sum_ref, acc,
):
    r = pl.program_id(0)
    rows, width = x_ref.shape

    @pl.when(r == 0)
    def _():
        sum_ref[...] = jnp.zeros_like(sum_ref)
        acc[...] = jnp.zeros_like(acc)

    live = info[3] < info[LEN0 + r]

    @pl.when(live)
    def _():
        valid = row_valid(info, r, rows)
        attended = att_ref[...]
        middle = x_ref[...].astype(F32) + gb_ref[2:3, :] * attended
        normal, inverse = norm_stats(middle)
        second = sa_ref[...].astype(F32) + sb_ref[0].astype(F32)
        back = norm_back(second, normal, inverse, gb_ref[1:2, :])
        output_delta = ct_ref[...].astype(F32) * valid
        branch = ba_ref[...].astype(F32) + bb_ref[0].astype(F32)
        sum_ref[3:4, :] += column_sum(output_delta * branch)
        middle_delta = output_delta + back
        delta_ref[...] = middle_delta
        attended_delta = (middle_delta * gb_ref[2:3, :]).astype(BF)
        dctx_ref[...] = mm_t(attended_delta, w_ref[...]).astype(BF)
        acc[...] += t_mm(ctx_ref[...], attended_delta)
        sum_ref[0:1, :] += column_sum(second * normal)
        sum_ref[1:2, :] += column_sum(middle_delta * attended)
        sum_ref[2:3, :] += column_sum(second)

    @pl.when(jnp.logical_not(live))
    def _():
        delta_ref[...] = jnp.zeros_like(delta_ref)
        dctx_ref[...] = jnp.zeros_like(dctx_ref)

    @pl.when(r == pl.num_programs(0) - 1)
    def _():
        out_ref[...] = acc[...].astype(BF)


def qkv_grad_kernel(info, n_ref, md_ref, nh_ref, mdh_ref, *refs):
    t = pl.program_id(0)
    acc = refs[4]
    acc[...] = t_mm(n_ref[...], md_ref[...])

    @pl.when(jnp.logical_and(info[0] > 0, t >= 2))
    def _():
        acc[...] += t_mm(nh_ref[...], mdh_ref[...])

    def put(left):
        for y in range(2):
            for z in range(4):
                z_there = (info[4] // 2 + z // 2) % 2 * 2 + (info[4] + z) % 2
                base = z_there * 256 + ((info[1] + y) % 2) * 128
                for c in range(2):
                    row = pl.multiple_of(base + ((info[2] + c) % 2) * 64, 64)
                    value = acc[pl.ds(row, 64), :].astype(BF)
                    if left:
                        refs[2 * c][0, y, z] = value
                    else:
                        refs[2 * c + 1][y, 0, 0, z] = value

    pl.when(t % 3 == 0)(functools.partial(put, True))
    pl.when(t % 3 > 0)(functools.partial(put, False))


def first_back_kernel(info, md_ref, w_ref, x_ref, delta_ref, gb_ref, out_ref, sum_ref):
    r = pl.program_id(0)

    @pl.when(r == 0)
    def _():
        sum_ref[...] = jnp.zeros_like(sum_ref)

    live = info[3] < info[LEN0 + r]

    @pl.when(live)
    def _():
        first = mm_t(md_ref[...], w_ref[...])
        normal, inverse = norm_stats(x_ref[...].astype(F32))
        out_ref[...] = delta_ref[...] + norm_back(first, normal, inverse, gb_ref[0:1, :])
        sum_ref[0:1, :] += column_sum(first * normal)
        sum_ref[1:2, :] += column_sum(first)

    @pl.when(jnp.logical_not(live))
    def _():
        out_ref[...] = jnp.zeros_like(out_ref)


def first_halo_kernel(first_clip, info, mdh_ref, wk_ref, wv_ref, x_ref, out_ref, sum_ref):
    r = pl.program_id(0)
    width = x_ref.shape[1]

    @pl.when(r == 0)
    def _():
        sum_ref[...] = jnp.zeros_like(sum_ref)

    live = jnp.logical_and(info[0] > 0, info[3] < info[LEN0 + first_clip + r])

    @pl.when(live)
    def _():
        first = mm_t(mdh_ref[:, :width], wk_ref[...]) + mm_t(mdh_ref[:, width:], wv_ref[...])
        out_ref[...] = first.astype(BF)
        normal, _ = norm_stats(x_ref[...].astype(F32))
        sum_ref[0:1, :] += column_sum(first * normal)
        sum_ref[1:2, :] += column_sum(first)

    @pl.when(jnp.logical_not(live))
    def _():
        out_ref[...] = jnp.zeros_like(out_ref)


def input_grad_kernel(first_clips, info, part_ref, halo_a, halo_b, x_ref, gb_ref, out_ref):
    r = pl.program_id(0)
    rows = part_ref.shape[0]
    split = rows - halo_a.shape[0]
    out_ref[:split, :] = part_ref[:split, :].astype(BF)

    @pl.when(info[0] == 0)
    def _():
        normal, inverse = norm_stats(x_ref[split:, :].astype(F32))
        halo = jnp.where(r < first_clips, halo_a[...], halo_b[...])
        back = norm_back(halo.astype(F32), normal, inverse, gb_ref[0:1, :])
        out_ref[split:, :] = (part_ref[split:, :] + back).astype(BF)

    @pl.when(info[0] > 0)
    def _():
        out_ref[split:, :] = part_ref[split:, :].astype(BF)


def ffn_kernel(c, first, half, info, n_own, n_other, b_own, b_other, *rest):
    if not first:
        earlier, rest = rest[:3], rest[3:]
    wg_hbm, wu_hbm, wd_hbm, *rest = rest
    sums, rest = rest[:3], rest[3:]
    packs, rest = (rest[0:2], rest[2:4]), rest[4:]
    wg, wu, wd, ag, au, ad, n_buf, b_buf, sems, row_sems = rest
    r = pl.program_id(0)
    steps = pl.num_programs(0)
    block_rows = n_buf.shape[1]

    def weight_copies(kind):
        hbm, vmem = ((wg_hbm, wg), (wu_hbm, wu), (wd_hbm, wd))[kind]
        for k in range(8):
            z0, x, q = k // 4, k // 2 % 2, k % 2
            d = ((info[0] + x) % 2 * 2 + z0) * 4 + (info[1] + q) % 2 * 2 + info[2]
            src = pl.ds(pl.multiple_of(d * 256 + c * TILE, TILE), TILE)
            dst = pl.ds(k * TILE, TILE)
            if kind < 2:
                yield pltpu.make_async_copy(hbm.at[:, src], vmem.at[:, dst], sems.at[kind, k])
            else:
                yield pltpu.make_async_copy(hbm.at[src, :], vmem.at[dst, :], sems.at[kind, k])

    def row_copies(step, sources):
        src = pl.ds(pl.multiple_of(step % half * block_rows, block_rows), block_rows)
        for i, (hbm, vmem) in enumerate(zip(sources, (n_buf, b_buf))):
            yield pltpu.make_async_copy(
                hbm.at[src, :], vmem.at[step % 2], row_sems.at[i, step % 2]
            )

    def start_rows(step):
        @pl.when(step < half)
        def _():
            for copy in row_copies(step, (n_own, b_own)):
                copy.start()

        @pl.when(step >= half)
        def _():
            for copy in row_copies(step, (n_other, b_other)):
                copy.start()

    @pl.when(r == 0)
    def _():
        start_rows(r)
        for kind in range(3):
            for copy in weight_copies(kind):
                copy.start()
        for acc in (ag, au, ad):
            acc[...] = jnp.zeros_like(acc)

    @pl.when(r + 1 < steps)
    def _():
        start_rows(r + 1)

    for copy in row_copies(r, (n_own, b_own)):
        copy.wait()

    @pl.when(r == 0)
    def _():
        for kind in range(3):
            for copy in weight_copies(kind):
                copy.wait()

    normed, delta = n_buf.at[r % 2], b_buf.at[r % 2]
    gate = mm(normed[...], wg[...])
    upward = mm(normed[...], wu[...])
    hidden_delta = mm_t(delta[...], wd[...])
    sigmoid = jax.nn.sigmoid(gate)
    active = gate * sigmoid
    hidden = (active * upward).astype(BF)
    up_delta = (hidden_delta * active).astype(BF)
    gate_delta = (hidden_delta * upward * (sigmoid + active * (1.0 - sigmoid))).astype(BF)
    branch = mm(hidden, wd[...])
    second = mm_t(gate_delta, wg[...]) + mm_t(up_delta, wu[...])
    if not first:
        branch = branch + jnp.where(r < half, earlier[0][...], earlier[2][0]).astype(F32)
        second = second + jnp.where(r < half, earlier[1][...], earlier[2][1]).astype(F32)
    branch, second = branch.astype(BF), second.astype(BF)
    sums[0][...] = branch
    sums[1][...] = second
    sums[2][0] = branch
    sums[2][1] = second
    ag[...] += t_mm(normed[...], gate_delta)
    au[...] += t_mm(normed[...], up_delta)
    ad[...] += t_mm(delta[...], hidden)

    @pl.when(r == pl.num_programs(0) - 1)
    def _():
        def flip(bit, own):
            return (bit + own) % 2

        def tile(acc, row, col):
            row = pl.multiple_of(row * TILE, TILE)
            col = pl.multiple_of(col * TILE, TILE)
            return acc[pl.ds(row, TILE), pl.ds(col, TILE)].astype(BF)

        x_own, y_own, z1_own, z0_own = info[0], info[1], info[4] // 2, info[4] % 2
        for u in range(2):
            for x in range(2):
                for y in range(2):
                    lead, other = (x, y) if u == 0 else (y, x)
                    ref = packs[u][lead]

                    def put(at, value):
                        ref[other, at * TILE : (at + 1) * TILE, :] = value

                    for z1 in range(2):
                        for z0 in range(2):
                            z = flip(z1, z1_own) * 2 + flip(z0, z0_own)
                            at = 4 * z1 if z0 == 0 else 16 + 4 * z1
                            for i, acc in enumerate((ag, au)):
                                for q in range(2):
                                    col = u * 4 + x * 2 + flip(q, y_own)
                                    put(at + 2 * i + q, tile(acc, z * 2 + flip(y, y_own), col))
                        col = flip(u, z0_own) * 4 + flip(flip(z1, z1_own), x_own) * 2 + y
                        for dq in range(4):
                            put(8 + 4 * z1 + dq, tile(ad, flip(x, x_own) * 4 + dq, col))


def ffn_call(c, info, pieces, weights, previous, after=(), block_rows=256):
    rows, width = pieces[0].shape
    half = rows // block_rows
    first = previous is None
    hidden = 8 * TILE
    own = pl.BlockSpec((block_rows, width), lambda r, info: (jnp.minimum(r, half), 0))
    other = pl.BlockSpec((2, block_rows, width), lambda r, info: (0, jnp.maximum(r - half, 0), 0))
    packed = (2, 24 * TILE, TILE)
    pack = pl.BlockSpec(packed, lambda r, info: (0, 0, 0), pipeline_mode=pl.Buffered(1))
    extra = [] if first else list(previous)
    anywhere = pl.BlockSpec(memory_space=pl.ANY)
    return call_kernel(
        functools.partial(ffn_kernel, c, first, half),
        info,
        [*pieces, *extra, *weights],
        name="feed_forward",
        grid=(2 * half,),
        ins=[anywhere] * 4 + [own, own, other] * (len(extra) // 3) + [anywhere] * 3,
        outs=[own, own, other] + [pack] * 4,
        shapes=[shape_of((rows + block_rows, width))] * 2 + [shape_of((2, rows, width))] + [shape_of(packed)] * 4,
        scratch=[
            pltpu.VMEM((width, hidden), BF),
            pltpu.VMEM((width, hidden), BF),
            pltpu.VMEM((hidden, width), BF),
            pltpu.VMEM((width, hidden), F32),
            pltpu.VMEM((width, hidden), F32),
            pltpu.VMEM((width, hidden), F32),
            pltpu.VMEM((2, block_rows, width), BF),
            pltpu.VMEM((2, block_rows, width), BF),
            pltpu.SemaphoreType.DMA((3, 8)),
            pltpu.SemaphoreType.DMA((2, 2)),
        ],
        vmem=60,
        cost=(18 * 2 * rows * width * hidden, 30 * MIB),
        after=after,
    )


SWAP = [(0, 1), (1, 0)]
Z_NEAR = [(0, 1), (1, 0), (2, 3), (3, 2)]
Z_FAR = [(0, 2), (2, 0), (1, 3), (3, 1)]


def meet(*values):
    return lax.optimization_barrier(values)


def later(values, *needed):
    return lax.optimization_barrier((values, needed))[0]


def swap(values, axis):
    return lax.ppermute(values, axis, SWAP)


def plus(left, right):
    return (left.astype(F32) + right.astype(F32)).astype(BF)


def fold(keep, send, axis):
    return plus(keep, swap(send, axis))


def fold_two(keep, send, lead, other):
    total = fold(keep, send, lead)
    return fold(total[0], total[1], other)


def scatter_z(values):
    return lax.psum_scatter(values, "z", scatter_dimension=0, tiled=True)[0]


def turn_table(first, last, head_dim):
    pairs = head_dim // 2
    rates = np.exp(np.arange(pairs, dtype=np.float32) * np.float32(-2.0 * math.log(10000.0) / head_dim))
    angles = np.arange(first, last, dtype=np.float32)[:, None] * rates[None, :].astype(np.float32)
    cosine, sine = (np.tile(t(angles), (1, TILE // pairs)) for t in (np.cos, np.sin))
    front = (np.arange(TILE) % head_dim < pairs)[None, :]
    return np.stack([cosine, np.where(front, -sine, 0), np.where(front, 0, sine)]).astype(np.float32)


def fast_body(
    frames, cotangent, lengths, qkv_weight, out_weight, gate_weight, up_weight, down_weight,
    gain_table, bias_table,
):
    clips, rows, width = frames.shape
    count = clips * rows
    head_dim = width // HEADS
    scale = 1.0 / math.sqrt(head_dim)
    x_at, y_at, core_at, z_at = (lax.axis_index(a) for a in ("seq", "y", "core", "z"))
    start = x_at * rows
    info = jnp.concatenate(
        [jnp.stack([x_at, y_at, core_at, start, z_at]).astype(jnp.int32), lengths.astype(jnp.int32)]
    )
    flat = frames.reshape(count, width)
    tangent = cotangent.reshape(count, width)
    halo = lax.ppermute(
        frames[:, rows - TILE :].reshape(clips * TILE, width), "seq", [(0, 1)]
    )
    places = start + jnp.arange(rows)
    valid = (places[None, :] < lengths[:, None]).astype(F32).reshape(count, 1)
    branch_delta = (tangent.astype(F32) * valid * gain_table[:, 3]).astype(BF)
    table = jnp.concatenate([gain_table, bias_table, jnp.zeros((width, 2), F32)], axis=1).T
    seats = lax.axis_size("seq")
    own_turns = jnp.asarray(turn_table(0, seats * rows, head_dim))
    halo_turns = jnp.asarray(
        np.concatenate([turn_table(i * rows - TILE, i * rows, head_dim) for i in range(seats)], axis=1)
    )
    own_tab = pl.BlockSpec((3, rows, TILE), lambda r, info: (0, info[0], 0))
    halo_tab = pl.BlockSpec((3, TILE, TILE), lambda r, info: (0, info[0], 0))
    gb = whole_spec(table.shape)
    own = rows_spec(rows, width)
    halo_rows = rows_spec(TILE, width)
    qkv_rows = rows_spec(rows, 3 * width)
    kv_rows = rows_spec(TILE, 2 * width)
    w_qkv = whole_spec((width, 3 * width))
    w_key = pl.BlockSpec((width, width), lambda r, info: (0, 1))
    w_value = pl.BlockSpec((width, width), lambda r, info: (0, 2))
    w_out = whole_spec((width, width))
    sums = whole_spec((8, width))

    def half_sums(part):
        return pl.BlockSpec((1, rows, width), lambda r, info: (part, r, 0))

    grid = (clips,)
    mac = 2 * count * width * width

    qkv, normed_one = call_kernel(
        qkv_kernel, info, [flat, qkv_weight, table, own_turns], name="qkv", grid=grid,
        ins=[own, w_qkv, gb, own_tab], outs=[qkv_rows, own],
        shapes=[shape_of((count, 3 * width)), shape_of((count, width))], cost=(3 * mac, 16 * MIB),
    )
    def half_rows(width, part):
        return pl.BlockSpec((TILE, width), lambda r, info: (2 * r + part, 0))

    seen = [shape_of((count, width)), shape_of((count, TILE), F32)]
    late = call_kernel(
        functools.partial(attend_late_kernel, scale), info, [qkv], name="attend_late", grid=grid,
        ins=[qkv_rows], outs=[half_rows(width, 1), half_rows(TILE, 1)], shapes=seen,
        cost=(2 * mac, 8 * MIB),
    )
    halo, branch_delta = lax.optimization_barrier((halo, branch_delta))
    branch_delta_other = swap(branch_delta, "core")
    kv_halo, normed_halo = call_kernel(
        halo_kernel, info, [halo, qkv_weight, qkv_weight, table, halo_turns], name="halo",
        grid=grid, ins=[halo_rows, w_key, w_value, gb, halo_tab],
        outs=[kv_rows, halo_rows],
        shapes=[shape_of((clips * TILE, 2 * width)), shape_of((clips * TILE, width))],
        cost=(mac, 8 * MIB), after=late,
    )
    context, log_totals = call_kernel(
        functools.partial(attend_kernel, scale, 0), info, [qkv, kv_halo], name="attend_early",
        grid=grid, ins=[half_rows(3 * width, 0), kv_rows],
        outs=[half_rows(width, 0), half_rows(TILE, 0)], shapes=seen,
        cost=(2 * mac, 12 * MIB), onto=late,
    )
    attended, normed_two = call_kernel(
        out_kernel, info, [context, flat, out_weight, table], name="project", grid=grid,
        ins=[own, own, w_out, gb], outs=[own, own],
        shapes=[shape_of((count, width), F32), shape_of((count, width))], cost=(mac, 12 * MIB),
    )
    normed_two_other = swap(normed_two, "core")

    pieces = (normed_two, normed_two_other, branch_delta, branch_delta_other)
    weights = (gate_weight, up_weight, down_weight)
    def start_pair(keeps):
        (keep_a, send_a), (keep_b, send_b) = keeps
        return (keep_a, swap(send_a, "seq")), (keep_b, swap(send_b, "y"))

    def second_pair(totals):
        (stay_a, go_a), (stay_b, go_b) = totals
        return (stay_a, swap(go_a, "y")), (stay_b, swap(go_b, "seq"))

    def halves(pairs):
        return [tuple(plus(keep[k], came[k]) for k in range(2)) for keep, came in pairs]

    def near_pair(pairs):
        a, b = (plus(stay, came).reshape(24, TILE, TILE) for stay, came in pairs)
        keep, send = jnp.concatenate([a[:16], b[:8]]), jnp.concatenate([a[16:], b[8:]])
        return keep, lax.ppermute(send, "z", Z_NEAR)

    def far_pair(pair):
        total = plus(*pair).reshape(3, 2, 4, TILE, TILE)
        return total[:, 0], lax.ppermute(total[:, 1], "z", Z_FAR)

    def run_ffn(c, previous, after):
        *state, keep_a, send_a, keep_b, send_b = ffn_call(
            c, info, pieces, weights, previous, after
        )
        return state, ((keep_a, send_a), (keep_b, send_b))

    previous, grads_0 = run_ffn(0, None, ())
    moved_0 = start_pair(grads_0)
    (branch, second, sums_sent), grads_1 = run_ffn(1, previous, ())
    branch, second, sums_sent, grads_1, moved_0 = meet(branch, second, sums_sent, grads_1, moved_0)
    sums_other = swap(sums_sent, "core")
    grads_1, sums_other = meet(grads_1, sums_other)
    totals_0 = halves(moved_0)
    moved_0 = second_pair(totals_0)
    moved_1 = start_pair(grads_1)

    middle_delta, context_delta, out_grad, sums_two = call_kernel(
        out_back_kernel, info,
        [second, sums_other, branch, sums_other, attended, flat, tangent, context, out_weight, table],
        name="project_back", grid=grid,
        ins=[own, half_sums(1), own, half_sums(0), own, own, own, own, w_out, gb],
        outs=[own, own, w_out, sums],
        shapes=[
            shape_of((count, width), F32), shape_of((count, width)), shape_of((width, width)),
            shape_of((8, width), F32),
        ],
        scratch=[pltpu.VMEM((width, width), F32)], cost=(2 * mac, 24 * MIB), after=tuple(t for pair in totals_0 for t in pair),
    )
    out_grad = lax.psum_scatter(out_grad, ("z", "y", "core"), scatter_dimension=0, tiled=True)

    def attend_back(first_clip, onto, after, taken):
        def at(rows, width):
            return pl.BlockSpec((rows, width), lambda r, info: (r + first_clip, 0))

        return call_kernel(
            functools.partial(attend_back_kernel, scale, first_clip), info,
            [qkv, kv_halo, context_delta, log_totals, own_turns, halo_turns],
            name="attend_back", grid=(taken,),
            ins=[
                at(rows, 3 * width), at(TILE, 2 * width), at(rows, width), at(rows, TILE),
                own_tab, halo_tab,
            ],
            outs=[at(rows, 3 * width), at(TILE, 2 * width)],
            shapes=[shape_of((count, 3 * width)), shape_of((clips * TILE, 2 * width))],
            scratch=[pltpu.VMEM((rows + TILE, width), F32), pltpu.VMEM((rows + TILE, width), F32)],
            cost=(2.5 * mac * taken, 6 * MIB * taken), after=after, onto=onto,
        )

    some = clips - 1

    def first_halo(first_clip, mixed_halo, after, taken):
        def at(width):
            return pl.BlockSpec((TILE, width), lambda r, info: (r + first_clip, 0))

        return call_kernel(
            functools.partial(first_halo_kernel, first_clip), info,
            [mixed_halo, qkv_weight, qkv_weight, halo], name="first_halo", grid=(taken,),
            ins=[at(2 * width), w_key, w_value, at(width)], outs=[halo_rows, sums],
            shapes=[shape_of((taken * TILE, width)), shape_of((8, width), F32)],
            cost=(mac // 4 * taken, 6 * MIB), after=after,
        )

    mixed = attend_back(0, (), (), some)
    mixed, moved_0, moved_1 = meet(mixed, moved_0, moved_1)
    totals_1 = halves(moved_1)
    moved_1 = second_pair(totals_1)
    near_0 = near_pair(moved_0)
    ready = (*(t for pair in totals_1 for t in pair), near_0[0])
    back_a, sums_a = first_halo(0, mixed[1], ready, some)
    mixed_delta, mixed_halo = attend_back(some, mixed, (back_a,), clips - some)
    mixed_delta, mixed_halo, back_a, moved_1, near_0 = meet(
        mixed_delta, mixed_halo, back_a, moved_1, near_0
    )
    came_a = lax.ppermute(back_a, "seq", [(1, 0)])
    far_0 = far_pair(near_0)

    cut = 3 * width // 6
    def x_seat(t, info):
        return (t // 3 + info[0]) % 2

    left_spec = pl.BlockSpec((1, 2, 4, 64, cut), lambda t, info: (x_seat(t, info), 0, 0, 0, 0))
    right_spec = pl.BlockSpec(
        (2, 1, 1, 4, 64, cut),
        lambda t, info: (0, x_seat(t, info), jnp.maximum(t % 3 - 1, 0), 0, 0, 0),
    )
    packed = [shape_of((2, 2, 4, 64, cut)), shape_of((2, 2, 2, 4, 64, cut))]
    keep_l, keep_r, send_l, send_r = call_kernel(
        qkv_grad_kernel, info, [normed_one, mixed_delta, normed_halo, mixed_halo],
        name="qkv_grad", grid=(6,),
        ins=[
            whole_spec((count, width)),
            pl.BlockSpec((count, cut), lambda t, info: (0, t)),
            whole_spec((clips * TILE, width)),
            pl.BlockSpec((clips * TILE, cut), lambda t, info: (0, jnp.maximum(t - 2, 0))),
        ],
        outs=[left_spec, right_spec] * 2, shapes=packed * 2,
        scratch=[pltpu.VMEM((width, cut), F32)], cost=(4 * mac, 16 * MIB),
        after=(far_0[0],),
    )
    came_a, far_0, keep_l, keep_r, send_l, send_r = meet(
        came_a, far_0, keep_l, keep_r, send_l, send_r
    )
    qkv_came = swap(send_l, "core"), swap(send_r, "core")
    back_b, sums_b = first_halo(some, mixed_halo, (keep_l,), clips - some)
    qkv_came, back_b = meet(qkv_came, back_b)
    came_b = lax.ppermute(back_b, "seq", [(1, 0)])
    came_l, came_r = qkv_came
    stay_l, go_l = (plus(keep_l[k], came_l[k]) for k in range(2))
    stay_r, go_r = (plus(keep_r[k], came_r[k]) for k in range(2))
    go_l, go_r = swap(go_l, "seq"), swap(go_r, "y")
    near_1 = near_pair(later(moved_1, stay_l, stay_r, back_b))
    part_grad, sums_one = call_kernel(
        first_back_kernel, info, [mixed_delta, qkv_weight, flat, middle_delta, table],
        name="first_back", grid=grid, ins=[qkv_rows, w_qkv, own, own, gb], outs=[own, sums],
        shapes=[shape_of((count, width), F32), shape_of((8, width), F32)],
        cost=(3 * mac, 24 * MIB), after=(stay_l, stay_r, near_1[0]),
    )
    go_l, go_r, near_1, came_b, part_grad, sums_one = meet(
        go_l, go_r, near_1, came_b, part_grad, sums_one
    )
    share = width // 16
    ones = sums_one + sums_a + sums_b
    nought = jnp.zeros((width,), F32)
    vectors = jnp.stack(
        [ones[0], sums_two[0], ones[1], nought, sums_two[1], sums_two[3], sums_two[2], nought]
    )
    vectors = vectors.reshape(2, 4, 16, share).transpose(2, 0, 1, 3).reshape(32, 4, share)
    vectors = lax.all_to_all(vectors, ("z", "y", "core", "seq"), 0, 0, tiled=True)
    left, right = plus(stay_l, go_l), plus(stay_r, go_r)
    vectors, left, right, near_1 = meet(vectors, left, right, near_1)
    go_l, go_r = swap(left[1], "y"), swap(right[1], "seq")
    far_1 = far_pair(near_1)
    output = call_kernel(
        output_kernel, info, [flat, attended, branch, sums_other, table],
        name="output", grid=grid, ins=[own, own, own, half_sums(0), gb], outs=own,
        shapes=shape_of((count, width)), cost=(0, 14 * MIB),
        after=(left, right, far_1[0], came_b),
    )
    go_l, go_r, output = meet(go_l, go_r, output)
    left, right = plus(left[0], go_l), plus(right[0], go_r)
    qkv_total = jnp.concatenate([left[None], right]).reshape(3, 2, 2, 64, cut)
    qkv_near = qkv_total[:, :, 1]
    go = lax.ppermute(qkv_near, "z", Z_NEAR)
    input_grad = call_kernel(
        functools.partial(input_grad_kernel, some), info, [part_grad, came_a, came_b, flat, table],
        name="input_grad", grid=grid,
        ins=[
            own,
            pl.BlockSpec((TILE, width), lambda r, info: (jnp.minimum(r, some - 1), 0)),
            pl.BlockSpec((TILE, width), lambda r, info: (jnp.maximum(r - some, 0), 0)),
            own, gb,
        ],
        outs=own, shapes=shape_of((count, width)), cost=(0, 8 * MIB),
        after=(left, right, output, qkv_total),
    )
    go, far_1, input_grad = meet(go, far_1, input_grad)
    qkv_total = plus(qkv_total[:, :, 0], go)
    qkv_total = plus(qkv_total[:, 0], lax.ppermute(qkv_total[:, 1], "z", Z_FAR))
    qkv_grad = qkv_total.transpose(1, 0, 2).reshape(-1, 3 * cut).astype(F32)
    out_halves = later(out_grad, input_grad).reshape(-1, 2, width // 2)
    out_kept = lax.dynamic_index_in_dim(out_halves, x_at, axis=1, keepdims=False)
    out_sent = lax.dynamic_index_in_dim(out_halves, 1 - x_at, axis=1, keepdims=False)
    out_grad = out_kept.astype(F32) + swap(out_sent, "seq").astype(F32)

    vectors = jnp.sum(vectors, axis=0).T
    gain_grad, bias_grad = vectors[:, :2], vectors[:, 2:3]

    tiles = jnp.stack([plus(*far_0), plus(*far_1)])
    gates = tiles[:, ::2].reshape(2, 2, 2, 2, 2, share, TILE)
    kept = lax.dynamic_index_in_dim(gates, core_at, axis=4, keepdims=False)
    sent = lax.dynamic_index_in_dim(gates, 1 - core_at, axis=4, keepdims=False)
    came = swap(sent, "core")
    both = jnp.where(core_at == 0, jnp.stack([kept, came], 4), jnp.stack([came, kept], 4))
    both = both.transpose(2, 5, 1, 3, 4, 0, 6).astype(F32)
    gate_grad = both[0].reshape(share, -1)
    up_grad = both[1].reshape(share, -1)
    down_grad = tiles[:, 1].reshape(2, width // 2, TILE).transpose(0, 2, 1).astype(F32)
    down_grad = down_grad.reshape(2 * TILE, width // 2)
    shape = (clips, rows, width)
    return (
        output.reshape(shape), input_grad.reshape(shape), qkv_grad, out_grad, gate_grad, up_grad,
        down_grad, gain_grad, bias_grad,
    )


def solution(mesh):
    placed = (("dp", "seq", None),) * 2 + (("dp",),) + ((),) * 7
    given = (("dp", "seq", None),) * 2 + (("dp", "seq"),) * 7
    fast = mesh.shape["dp"] == 16 and mesh.shape["seq"] == 2
    dp_axes = ("z", "y", "core") if fast else "dp"

    def specs(entries):
        return tuple(P(*(dp_axes if a == "dp" else a for a in entry)) for entry in entries)

    if fast:
        mesh = Mesh(mesh.devices.reshape(4, 2, 2, 2), ("z", "y", "core", "seq"))
    return jax.shard_map(
        fast_body if fast else body,
        mesh=mesh,
        in_specs=specs(placed),
        out_specs=specs(given),
        check_vma=False,
    )
```

```python
import functools
import math

import jax
import jax.numpy as jnp
import numpy as np
from jax import lax
from jax.experimental import pallas as pl
from jax.experimental.pallas import tpu as pltpu
from jax.sharding import Mesh
from jax.sharding import PartitionSpec as P

HEADS = 16
WINDOW = 128


NORM_EPS = 1e-05
MASKED = -1e30


def norm_forward(values, gain_col, shift_col):
    row_mean = jnp.mean(values, axis=-1, keepdims=True)
    centred = values - row_mean
    inverse = lax.rsqrt(jnp.mean(centred * centred, axis=-1, keepdims=True) + NORM_EPS)
    normal = centred * inverse
    return (normal * gain_col + shift_col, normal, inverse)


def norm_backward(upstream, normal, inverse, gain_col):
    scaled = upstream * gain_col
    inner_term = (
        scaled
        - jnp.mean(scaled, axis=-1, keepdims=True)
        - normal * jnp.mean(scaled * normal, axis=-1, keepdims=True)
    )
    return (inverse * inner_term, jnp.sum(upstream * normal, axis=0), jnp.sum(upstream, axis=0))


def rotary_tables(places, head_dim):
    pair_count = head_dim // 2
    freq_rates = jnp.exp(
        jnp.arange(pair_count).astype(jnp.float32) * (-2.0 * math.log(10000.0) / head_dim)
    )
    angles = places.astype(jnp.float32)[:, None] * freq_rates[None, :]
    return (jnp.cos(angles), jnp.sin(angles))


def rotate(values, cosine, sine_table, direction):
    pair_count = values.shape[-1] // 2
    leading = values[..., :pair_count]
    trailing = values[..., pair_count:]
    cos_wide = cosine[:, None, :]
    sin_wide = sine_table[:, None, :] * direction
    return jnp.concatenate(
        [leading * cos_wide - trailing * sin_wide, trailing * cos_wide + leading * sin_wide],
        axis=-1,
    )


def inner_rows(left_op, right_op):
    return lax.dot_general(
        left_op, right_op, (((0,), (0,)), ((), ())), preferred_element_type=jnp.float32
    )


def times_transposed(left_op, right_op):
    return lax.dot_general(
        left_op, right_op, (((1,), (1,)), ((), ())), preferred_element_type=jnp.float32
    )


def body(
    frames,
    cotangent,
    lengths,
    qkv_weight,
    out_weight,
    gate_weight,
    up_weight,
    down_weight,
    gain_table,
    bias_table,
):
    seq_parts = lax.axis_size("seq")
    seq_index = lax.axis_index("seq")
    model_width = frames.shape[2]
    clip_len = frames.shape[1] * seq_parts
    head_dim = model_width // HEADS
    score_scale = 1.0 / math.sqrt(head_dim)
    frames_here, tangent_here = (frames, cotangent)
    places = seq_index * frames.shape[1] + jnp.arange(frames.shape[1])
    heads_here = HEADS // seq_parts
    groups, row_len = (frames_here.shape[0], frames_here.shape[1])
    row_count = groups * row_len
    width_here = heads_here * head_dim
    valid_rows = (places[None, :] < lengths[:, None]).astype(jnp.float32).reshape(row_count, 1)
    cosine, sine_table = rotary_tables(places, head_dim)
    full_cosine, full_sine = rotary_tables(jnp.arange(clip_len), head_dim)
    source = frames_here.astype(jnp.float32).reshape(row_count, model_width)
    normed_one, normal_one, inverse_one = norm_forward(source, gain_table[:, 0], bias_table[:, 0])
    normed_one = normed_one.astype(jnp.bfloat16)
    mixed_rows = jnp.dot(normed_one, qkv_weight, preferred_element_type=jnp.float32)
    shaped = mixed_rows.reshape(groups, row_len, 3, HEADS, head_dim)
    queries = (
        rotate(shaped[:, :, 0], cosine, sine_table, 1.0)
        .astype(jnp.bfloat16)
        .reshape(groups, row_len, model_width)
    )
    key_rows = (
        rotate(shaped[:, :, 1], cosine, sine_table, 1.0)
        .astype(jnp.bfloat16)
        .reshape(groups, row_len, model_width)
    )
    values = shaped[:, :, 2].astype(jnp.bfloat16).reshape(groups, row_len, model_width)
    head_queries, head_keys, head_values = (
        lax.all_to_all(queries, "seq", split_axis=2, concat_axis=1, tiled=True),
        lax.all_to_all(key_rows, "seq", split_axis=2, concat_axis=1, tiled=True),
        lax.all_to_all(values, "seq", split_axis=2, concat_axis=1, tiled=True),
    )
    head_queries = head_queries.reshape(groups, clip_len, heads_here, head_dim)
    head_keys = head_keys.reshape(groups, clip_len, heads_here, head_dim)
    head_values = head_values.reshape(groups, clip_len, heads_here, head_dim)
    query_pos = jnp.arange(clip_len)[:, None]
    key_pos = jnp.arange(clip_len)[None, :]
    window_mask = (key_pos <= query_pos) & (key_pos > query_pos - WINDOW)

    def clip_scores(clip_queries, clip_keys, length):
        products = jnp.einsum(
            "qhd,khd->hqk", clip_queries, clip_keys, preferred_element_type=jnp.float32
        )
        allowed = window_mask & (key_pos < length)
        return (jnp.where(allowed[None], products * score_scale, MASKED), allowed)

    def attend(block_item):
        clip_queries, clip_keys, clip_values, length = block_item
        scores, allowed = clip_scores(clip_queries, clip_keys, length)
        top_score = jnp.max(scores, axis=-1, keepdims=True)
        exponent = jnp.exp(scores - top_score)
        row_total = jnp.sum(exponent, axis=-1, keepdims=True)
        weights_low = (exponent / row_total).astype(jnp.bfloat16)
        context = jnp.einsum(
            "hqk,khd->qhd", weights_low, clip_values, preferred_element_type=jnp.float32
        )
        return (context.astype(jnp.bfloat16), top_score + jnp.log(row_total))

    context_heads, log_totals = lax.map(attend, (head_queries, head_keys, head_values, lengths))
    context_heads = context_heads.reshape(groups, clip_len, width_here)
    context = lax.all_to_all(context_heads, "seq", split_axis=1, concat_axis=2, tiled=True).reshape(
        row_count, model_width
    )
    attended = jnp.dot(context, out_weight, preferred_element_type=jnp.float32)
    middle = source + gain_table[:, 2] * attended
    normed_two, normal_two, inverse_two = norm_forward(middle, gain_table[:, 1], bias_table[:, 1])
    normed_two = normed_two.astype(jnp.bfloat16)
    gate_rows = jnp.dot(normed_two, gate_weight, preferred_element_type=jnp.float32)
    upward = jnp.dot(normed_two, up_weight, preferred_element_type=jnp.float32)
    sigmoid_gate = jax.nn.sigmoid(gate_rows)
    activated = gate_rows * sigmoid_gate
    hidden = (activated * upward).astype(jnp.bfloat16)
    branch = jnp.dot(hidden, down_weight, preferred_element_type=jnp.float32)
    output = (
        ((middle + gain_table[:, 3] * branch) * valid_rows)
        .astype(jnp.bfloat16)
        .reshape(groups, row_len, model_width)
    )
    output_delta = tangent_here.astype(jnp.float32).reshape(row_count, model_width) * valid_rows
    branch_delta = (output_delta * gain_table[:, 3]).astype(jnp.bfloat16)
    scale_mlp = jnp.sum(output_delta * branch, axis=0)
    down_grad = inner_rows(hidden, branch_delta)
    hidden_delta = times_transposed(branch_delta, down_weight)
    up_delta = (hidden_delta * activated).astype(jnp.bfloat16)
    gate_delta = (
        hidden_delta * upward * sigmoid_gate * (1.0 + gate_rows * (1.0 - sigmoid_gate))
    ).astype(jnp.bfloat16)
    gate_grad = inner_rows(normed_two, gate_delta)
    up_grad = inner_rows(normed_two, up_delta)
    second_delta = times_transposed(gate_delta, gate_weight) + times_transposed(up_delta, up_weight)
    back_two, gain_two, bias_two = norm_backward(
        second_delta, normal_two, inverse_two, gain_table[:, 1]
    )
    middle_delta = output_delta + back_two
    attended_delta = (middle_delta * gain_table[:, 2]).astype(jnp.bfloat16)
    scale_attn = jnp.sum(middle_delta * attended, axis=0)
    out_grad = inner_rows(context, attended_delta)
    context_delta = (
        times_transposed(attended_delta, out_weight)
        .astype(jnp.bfloat16)
        .reshape(groups, row_len, model_width)
    )
    context_heads_delta = lax.all_to_all(
        context_delta, "seq", split_axis=2, concat_axis=1, tiled=True
    )
    context_heads_delta = context_heads_delta.reshape(groups, clip_len, heads_here, head_dim)

    def attend_back(block_item):
        clip_queries, clip_keys, clip_values, length, log_total, clip_delta = block_item
        scores, allowed = clip_scores(clip_queries, clip_keys, length)
        weights = jnp.exp(scores - log_total)
        weights_low = weights.astype(jnp.bfloat16)
        weight_delta = jnp.einsum(
            "qhd,khd->hqk", clip_delta, clip_values, preferred_element_type=jnp.float32
        )
        row_inner = jnp.sum(weight_delta * weights, axis=-1, keepdims=True)
        product_delta = jnp.where(
            allowed[None], weights * (weight_delta - row_inner) * score_scale, 0.0
        ).astype(jnp.bfloat16)
        query_delta = jnp.einsum(
            "hqk,khd->qhd", product_delta, clip_keys, preferred_element_type=jnp.float32
        )
        key_delta = jnp.einsum(
            "hqk,qhd->khd", product_delta, clip_queries, preferred_element_type=jnp.float32
        )
        value_delta = jnp.einsum(
            "hqk,qhd->khd", weights_low, clip_delta, preferred_element_type=jnp.float32
        )
        query_delta = rotate(query_delta, full_cosine, full_sine, -1.0).astype(jnp.bfloat16)
        key_delta = rotate(key_delta, full_cosine, full_sine, -1.0).astype(jnp.bfloat16)
        return (query_delta, key_delta, value_delta.astype(jnp.bfloat16))

    query_delta, key_delta, value_delta = lax.map(
        attend_back,
        (head_queries, head_keys, head_values, lengths, log_totals, context_heads_delta),
    )
    query_delta = query_delta.reshape(groups, clip_len, width_here)
    key_delta = key_delta.reshape(groups, clip_len, width_here)
    value_delta = value_delta.reshape(groups, clip_len, width_here)
    query_back, key_back, value_back = (
        lax.all_to_all(query_delta, "seq", split_axis=1, concat_axis=2, tiled=True),
        lax.all_to_all(key_delta, "seq", split_axis=1, concat_axis=2, tiled=True),
        lax.all_to_all(value_delta, "seq", split_axis=1, concat_axis=2, tiled=True),
    )
    mixed_delta = jnp.concatenate(
        [
            query_back.reshape(row_count, model_width),
            key_back.reshape(row_count, model_width),
            value_back.reshape(row_count, model_width),
        ],
        axis=1,
    )
    qkv_grad = inner_rows(normed_one, mixed_delta)
    first_delta = times_transposed(mixed_delta, qkv_weight)
    back_one, gain_one, bias_one = norm_backward(
        first_delta, normal_one, inverse_one, gain_table[:, 0]
    )
    input_grad = (
        (middle_delta + back_one).astype(jnp.bfloat16).reshape(groups, row_len, model_width)
    )
    gain_grad = jnp.stack([gain_one, gain_two, scale_attn, scale_mlp], axis=1)
    bias_grad = jnp.stack([bias_one, bias_two], axis=1)
    over_clips = (
        lax.psum_scatter(qkv_grad, "dp", scatter_dimension=0, tiled=True),
        lax.psum_scatter(out_grad, "dp", scatter_dimension=0, tiled=True),
        lax.psum_scatter(gate_grad, "dp", scatter_dimension=0, tiled=True),
        lax.psum_scatter(up_grad, "dp", scatter_dimension=0, tiled=True),
        lax.psum_scatter(down_grad, "dp", scatter_dimension=0, tiled=True),
        lax.psum_scatter(gain_grad, "dp", scatter_dimension=0, tiled=True),
        lax.psum_scatter(bias_grad, "dp", scatter_dimension=0, tiled=True),
    )
    summed = (
        lax.psum_scatter(
            over_clips[0].astype(jnp.bfloat16), "seq", scatter_dimension=1, tiled=True
        ).astype(jnp.float32),
        lax.psum_scatter(
            over_clips[1].astype(jnp.bfloat16), "seq", scatter_dimension=1, tiled=True
        ).astype(jnp.float32),
        lax.psum_scatter(
            over_clips[2].astype(jnp.bfloat16), "seq", scatter_dimension=1, tiled=True
        ).astype(jnp.float32),
        lax.psum_scatter(
            over_clips[3].astype(jnp.bfloat16), "seq", scatter_dimension=1, tiled=True
        ).astype(jnp.float32),
        lax.psum_scatter(
            over_clips[4].astype(jnp.bfloat16), "seq", scatter_dimension=1, tiled=True
        ).astype(jnp.float32),
        lax.psum_scatter(
            over_clips[5].astype(jnp.bfloat16), "seq", scatter_dimension=1, tiled=True
        ).astype(jnp.float32),
        lax.psum_scatter(
            over_clips[6].astype(jnp.bfloat16), "seq", scatter_dimension=1, tiled=True
        ).astype(jnp.float32),
    )
    return (
        output,
        input_grad,
        summed[0],
        summed[1],
        summed[2],
        summed[3],
        summed[4],
        summed[5],
        summed[6],
    )


BF = jnp.bfloat16
F32 = jnp.float32
TILE = 128
MIB = 1024 * 1024
HINT = 0.25


def mm(left, right):
    return lax.dot_general(left, right, (((1,), (0,)), ((), ())), preferred_element_type=F32)


def mm_t(left, right):
    return lax.dot_general(left, right, (((1,), (1,)), ((), ())), preferred_element_type=F32)


def t_mm(left, right):
    return lax.dot_general(left, right, (((0,), (0,)), ((), ())), preferred_element_type=F32)


def call_kernel(
    kernel, info, args, *, name, grid, ins, outs, shapes, scratch=(), vmem=60, cost=None, after=(),
    onto=(),
):
    flops, moved = cost
    aliases = {1 + len(args) + len(after) + k: k for k in range(len(onto))}
    after = (*after, *onto)
    count, unread = len(args), len(after)

    def run(info, *refs):
        kernel(info, *refs[:count], *refs[count + unread :])

    args = [*args, *after]
    ins = [*ins] + [pl.BlockSpec(memory_space=pl.ANY)] * unread
    return pl.pallas_call(
        run,
        grid_spec=pltpu.PrefetchScalarGridSpec(
            num_scalar_prefetch=1, grid=grid, in_specs=ins, out_specs=outs, scratch_shapes=scratch
        ),
        out_shape=shapes,
        input_output_aliases=aliases,
        compiler_params=pltpu.CompilerParams(
            dimension_semantics=("arbitrary",) * len(grid), vmem_limit_bytes=vmem * MIB
        ),
        cost_estimate=pl.CostEstimate(
            flops=int(flops * HINT), bytes_accessed=int(moved * HINT), transcendentals=0
        ),
        name=name,
    )(info, *args)


def shape_of(shape, dtype=BF):
    return jax.ShapeDtypeStruct(shape, dtype)


def rows_spec(rows, width, column=0):
    return pl.BlockSpec((rows, width), lambda r, info: (r, column))


def whole_spec(shape):
    return pl.BlockSpec(shape, lambda r, info: (0,) * len(shape))


LEN0 = 5


def norm_stats(values):
    row_mean = jnp.mean(values, axis=-1, keepdims=True)
    centred = values - row_mean
    inverse = lax.rsqrt(jnp.mean(centred * centred, axis=-1, keepdims=True) + NORM_EPS)
    return centred * inverse, inverse


def norm_back(upstream, normal, inverse, gain):
    scaled = upstream * gain
    return inverse * (
        scaled
        - jnp.mean(scaled, axis=-1, keepdims=True)
        - normal * jnp.mean(scaled * normal, axis=-1, keepdims=True)
    )


def turn(values, cosine, sine_a, sine_b):
    return (
        values * cosine
        + pltpu.roll(values, TILE - 32, 1) * sine_a
        + pltpu.roll(values, 32, 1) * sine_b
    )


def column_sum(values):
    return jnp.sum(values, axis=0, keepdims=True)


def qkv_kernel(info, x_ref, w_ref, gb_ref, tab_ref, qkv_ref, n_ref):
    r = pl.program_id(0)
    live = info[3] < info[LEN0 + r]

    @pl.when(live)
    def _():
        normal, _ = norm_stats(x_ref[...].astype(F32))
        normed = (normal * gb_ref[0:1, :] + gb_ref[4:5, :]).astype(BF)
        n_ref[...] = normed
        width = normed.shape[1]
        cosine, sine_a, sine_b = tab_ref[0], tab_ref[1], tab_ref[2]
        for part in range(3):
            mixed = mm(normed, w_ref[:, part * width : (part + 1) * width])
            for t in range(width // TILE):
                piece = mixed[:, t * TILE : (t + 1) * TILE]
                if part < 2:
                    piece = turn(piece, cosine, sine_a, sine_b)
                at = part * width + t * TILE
                qkv_ref[:, at : at + TILE] = piece.astype(BF)

    @pl.when(jnp.logical_not(live))
    def _():
        qkv_ref[...] = jnp.zeros_like(qkv_ref)
        n_ref[...] = jnp.zeros_like(n_ref)


def halo_kernel(info, x_ref, wk_ref, wv_ref, gb_ref, tab_ref, kv_ref, n_ref):
    r = pl.program_id(0)
    live = jnp.logical_and(info[0] > 0, info[3] < info[LEN0 + r])

    @pl.when(live)
    def _():
        normal, _ = norm_stats(x_ref[...].astype(F32))
        normed = (normal * gb_ref[0:1, :] + gb_ref[4:5, :]).astype(BF)
        n_ref[...] = normed
        width = normed.shape[1]
        keys = mm(normed, wk_ref[...])
        for t in range(width // TILE):
            piece = keys[:, t * TILE : (t + 1) * TILE]
            kv_ref[:, t * TILE : (t + 1) * TILE] = turn(
                piece, tab_ref[0], tab_ref[1], tab_ref[2]
            ).astype(BF)
        kv_ref[:, width:] = mm(normed, wv_ref[...]).astype(BF)

    @pl.when(jnp.logical_not(live))
    def _():
        kv_ref[...] = jnp.zeros_like(kv_ref)
        n_ref[...] = jnp.zeros_like(n_ref)


def staged(count, *stages):
    kept = [{} for _ in stages]
    for step in range(count + len(stages) - 1):
        for k, stage in enumerate(stages):
            i = step - k
            if 0 <= i < count:
                kept[k][i] = stage(i, kept[k - 1].pop(i)) if k else stage(i)


def window_bias(info, clip, block):
    j = lax.broadcasted_iota(jnp.int32, (2 * TILE, 2 * TILE), 0)
    i = lax.broadcasted_iota(jnp.int32, (2 * TILE, 2 * TILE), 1) % TILE
    key = info[3] + (block - 1) * TILE + j
    allowed = (j > i) & (j <= i + TILE) & (key >= 0) & (key < info[LEN0 + clip])
    return jnp.where(allowed, 0.0, MASKED)


def two_heads(values):
    lane = lax.broadcasted_iota(jnp.int32, values.shape, 1)
    nought = jnp.zeros_like(values)
    return jnp.concatenate(
        [jnp.where(lane < 64, values, nought), jnp.where(lane < 64, nought, values)], axis=0
    )


def one_row(turned):
    return jnp.concatenate([turned[:64, :TILE], turned[64:, TILE:]], axis=0).T


def key_window(halo_ref, own_ref, block, at, own_at):
    if block == 0:
        return jnp.concatenate(
            [halo_ref[:, at : at + TILE], own_ref[0:TILE, own_at : own_at + TILE]], axis=0
        )
    return own_ref[(block - 1) * TILE : (block + 1) * TILE, own_at : own_at + TILE]


def attend_kernel(scale, block, info, qkv_ref, kvh_ref, ctx_ref, lse_ref):
    clip = pl.program_id(0)
    width = ctx_ref.shape[1]
    at_rows = slice(block * TILE, (block + 1) * TILE)
    live = info[3] < info[LEN0 + clip]

    @pl.when(live)
    def _():
        bias = window_bias(info, clip, block)

        def score(pair):
            at = pair * TILE
            queries = two_heads(qkv_ref[at_rows, at : at + TILE] * BF(scale))
            return mm_t(key_window(kvh_ref, qkv_ref, block, at, width + at), queries)

        def weigh(pair, scores):
            scores = scores + bias
            top = jnp.max(scores, axis=0, keepdims=True)
            exponent = jnp.exp(scores - top)
            total = jnp.sum(exponent, axis=0, keepdims=True)
            lse_ref[0, pair : pair + 1, :] = top + jnp.log(total)
            return (exponent * (1.0 / total)).astype(BF)

        def gather(pair, weights):
            at = pair * TILE
            values = key_window(kvh_ref, qkv_ref, block, width + at, 2 * width + at)
            return t_mm(values, weights)

        def put(pair, turned):
            ctx_ref[:, pair * TILE : (pair + 1) * TILE] = one_row(turned).astype(BF)

        staged(width // TILE, score, weigh, gather, put)

    @pl.when(jnp.logical_not(live))
    def _():
        ctx_ref[...] = jnp.zeros_like(ctx_ref)
        lse_ref[...] = jnp.zeros_like(lse_ref)


def attend_late_kernel(scale, info, qkv_ref, ctx_ref, lse_ref):
    attend_kernel(scale, 1, info, qkv_ref, None, ctx_ref, lse_ref)


def attend_back_kernel(
    scale, first_clip, info, qkv_ref, kvh_ref, dctx_ref, lse_ref, tab_ref, tabh_ref, md_ref, mdh_ref
):
    clip = pl.program_id(0) + first_clip
    rows, width = dctx_ref.shape
    live = info[3] < info[LEN0 + clip]

    @pl.when(jnp.logical_not(live))
    def _():
        md_ref[...] = jnp.zeros_like(md_ref)
        mdh_ref[...] = jnp.zeros_like(mdh_ref)

    @pl.when(live)
    def _():
        biases = [window_bias(info, clip, block) for block in range(2)]

        def place(item):
            pair, block = divmod(item, 2)
            return pair, block, pair * TILE, slice(block * TILE, (block + 1) * TILE)

        def score(item):
            pair, block, at, at_rows = place(item)
            queries = two_heads(qkv_ref[at_rows, at : at + TILE] * BF(scale))
            delta = two_heads(dctx_ref[at_rows, at : at + TILE])
            keys = key_window(kvh_ref, qkv_ref, block, at, width + at)
            values = key_window(kvh_ref, qkv_ref, block, width + at, 2 * width + at)
            return mm_t(keys, queries), mm_t(values, delta)

        def weigh(item, scores):
            pair, block, at, at_rows = place(item)
            products, weight_delta = scores
            weights = jnp.exp(products + biases[block] - lse_ref[block, pair : pair + 1, :])
            inner = jnp.sum(weight_delta * weights, axis=0, keepdims=True)
            return weights.astype(BF), (weights * (weight_delta - inner)).astype(BF)

        def gather(item, weighed):
            pair, block, at, at_rows = place(item)
            weights, score_delta = weighed
            queries = two_heads(qkv_ref[at_rows, at : at + TILE] * BF(scale))
            delta = two_heads(dctx_ref[at_rows, at : at + TILE])
            keys = key_window(kvh_ref, qkv_ref, block, at, width + at)
            return t_mm(keys, score_delta), mm(score_delta, queries), mm(weights, delta)

        before = {}
        early, late = slice(0, TILE), slice(TILE, 2 * TILE)

        def put_key(where, at, delta):
            md_ref[where, width + at : width + at + TILE] = turn(
                delta, tab_ref[0, where], -tab_ref[1, where], -tab_ref[2, where]
            ).astype(BF)

        def put(item, deltas):
            pair, block, at, at_rows = place(item)
            turned, key_delta, value_delta = deltas
            md_ref[at_rows, at : at + TILE] = turn(
                one_row(turned) * scale,
                tab_ref[0, at_rows], -tab_ref[1, at_rows], -tab_ref[2, at_rows],
            ).astype(BF)
            value_at = slice(2 * width + at, 2 * width + at + TILE)
            if block == 0:
                mdh_ref[:, at : at + TILE] = turn(
                    key_delta[early], tabh_ref[0], -tabh_ref[1], -tabh_ref[2]
                ).astype(BF)
                mdh_ref[:, width + at : width + at + TILE] = value_delta[early].astype(BF)
                before[pair] = key_delta[late], value_delta[late]
            else:
                key_before, value_before = before.pop(pair)
                put_key(early, at, key_before + key_delta[early])
                put_key(late, at, key_delta[late])
                md_ref[early, value_at] = (value_before + value_delta[early]).astype(BF)
                md_ref[late, value_at] = value_delta[late].astype(BF)

        staged(2 * (width // TILE), score, weigh, gather, put)


def out_kernel(info, ctx_ref, x_ref, w_ref, gb_ref, att_ref, n_ref):
    r = pl.program_id(0)
    live = info[3] < info[LEN0 + r]

    @pl.when(live)
    def _():
        attended = mm(ctx_ref[...], w_ref[...])
        att_ref[...] = attended
        middle = x_ref[...].astype(F32) + gb_ref[2:3, :] * attended
        normal, _ = norm_stats(middle)
        n_ref[...] = (normal * gb_ref[1:2, :] + gb_ref[5:6, :]).astype(BF)

    @pl.when(jnp.logical_not(live))
    def _():
        att_ref[...] = jnp.zeros_like(att_ref)
        n_ref[...] = jnp.zeros_like(n_ref)


def row_valid(info, clip, rows):
    place = info[3] + lax.broadcasted_iota(jnp.int32, (rows, 1), 0)
    return (place < info[LEN0 + clip]).astype(F32)


def output_kernel(info, x_ref, att_ref, ba_ref, bb_ref, gb_ref, out_ref):
    r = pl.program_id(0)
    valid = row_valid(info, r, x_ref.shape[0])
    branch = ba_ref[...].astype(F32) + bb_ref[...].astype(F32)
    middle = x_ref[...].astype(F32) + gb_ref[2:3, :] * att_ref[...]
    out_ref[...] = ((middle + gb_ref[3:4, :] * branch) * valid).astype(BF)


def out_back_kernel(
    info, sa_ref, sb_ref, att_ref, x_ref, ct_ref, ctx_ref, w_ref, gb_ref,
    delta_ref, dctx_ref, out_ref, sum_ref, acc,
):
    r = pl.program_id(0)
    rows, width = x_ref.shape

    @pl.when(r == 0)
    def _():
        sum_ref[...] = jnp.zeros_like(sum_ref)
        acc[...] = jnp.zeros_like(acc)

    live = info[3] < info[LEN0 + r]

    @pl.when(live)
    def _():
        valid = row_valid(info, r, rows)
        attended = att_ref[...]
        middle = x_ref[...].astype(F32) + gb_ref[2:3, :] * attended
        normal, inverse = norm_stats(middle)
        second = sa_ref[...].astype(F32) + sb_ref[...].astype(F32)
        back = norm_back(second, normal, inverse, gb_ref[1:2, :])
        output_delta = ct_ref[...].astype(F32) * valid
        middle_delta = output_delta + back
        delta_ref[...] = middle_delta
        attended_delta = (middle_delta * gb_ref[2:3, :]).astype(BF)
        dctx_ref[...] = mm_t(attended_delta, w_ref[...]).astype(BF)
        acc[...] += t_mm(ctx_ref[...], attended_delta)
        sum_ref[0:1, :] += column_sum(second * normal)
        sum_ref[1:2, :] += column_sum(middle_delta * attended)
        sum_ref[2:3, :] += column_sum(second)

    @pl.when(jnp.logical_not(live))
    def _():
        delta_ref[...] = jnp.zeros_like(delta_ref)
        dctx_ref[...] = jnp.zeros_like(dctx_ref)

    @pl.when(r == pl.num_programs(0) - 1)
    def _():
        out_ref[...] = acc[...].astype(BF)


def qkv_grad_kernel(info, n_ref, md_ref, nh_ref, mdh_ref, *refs):
    t = pl.program_id(0)
    acc = refs[4]
    acc[...] = t_mm(n_ref[...], md_ref[...])

    @pl.when(jnp.logical_and(info[0] > 0, t >= 2))
    def _():
        acc[...] += t_mm(nh_ref[...], mdh_ref[...])

    def put(left):
        for y in range(2):
            for z in range(4):
                z_there = (info[4] // 2 + z // 2) % 2 * 2 + (info[4] + z) % 2
                base = z_there * 256 + ((info[1] + y) % 2) * 128
                for c in range(2):
                    row = pl.multiple_of(base + ((info[2] + c) % 2) * 64, 64)
                    value = acc[pl.ds(row, 64), :].astype(BF)
                    if left:
                        refs[2 * c][0, y, z] = value
                    else:
                        refs[2 * c + 1][y, 0, 0, z] = value

    pl.when(t % 3 == 0)(functools.partial(put, True))
    pl.when(t % 3 > 0)(functools.partial(put, False))


def first_back_kernel(info, md_ref, w_ref, x_ref, delta_ref, gb_ref, out_ref, sum_ref):
    r = pl.program_id(0)

    @pl.when(r == 0)
    def _():
        sum_ref[...] = jnp.zeros_like(sum_ref)

    live = info[3] < info[LEN0 + r]

    @pl.when(live)
    def _():
        first = mm_t(md_ref[...], w_ref[...])
        normal, inverse = norm_stats(x_ref[...].astype(F32))
        out_ref[...] = delta_ref[...] + norm_back(first, normal, inverse, gb_ref[0:1, :])
        sum_ref[0:1, :] += column_sum(first * normal)
        sum_ref[1:2, :] += column_sum(first)

    @pl.when(jnp.logical_not(live))
    def _():
        out_ref[...] = jnp.zeros_like(out_ref)


def first_halo_kernel(first_clip, info, mdh_ref, wk_ref, wv_ref, x_ref, out_ref, sum_ref):
    r = pl.program_id(0)
    width = x_ref.shape[1]

    @pl.when(r == 0)
    def _():
        sum_ref[...] = jnp.zeros_like(sum_ref)

    live = jnp.logical_and(info[0] > 0, info[3] < info[LEN0 + first_clip + r])

    @pl.when(live)
    def _():
        first = mm_t(mdh_ref[:, :width], wk_ref[...]) + mm_t(mdh_ref[:, width:], wv_ref[...])
        out_ref[...] = first.astype(BF)
        normal, _ = norm_stats(x_ref[...].astype(F32))
        sum_ref[0:1, :] += column_sum(first * normal)
        sum_ref[1:2, :] += column_sum(first)

    @pl.when(jnp.logical_not(live))
    def _():
        out_ref[...] = jnp.zeros_like(out_ref)


def input_grad_kernel(first_clips, info, part_ref, halo_a, halo_b, x_ref, gb_ref, out_ref):
    r = pl.program_id(0)
    rows = part_ref.shape[0]
    split = rows - halo_a.shape[0]
    out_ref[:split, :] = part_ref[:split, :].astype(BF)

    @pl.when(info[0] == 0)
    def _():
        normal, inverse = norm_stats(x_ref[split:, :].astype(F32))
        halo = jnp.where(r < first_clips, halo_a[...], halo_b[...])
        back = norm_back(halo.astype(F32), normal, inverse, gb_ref[0:1, :])
        out_ref[split:, :] = (part_ref[split:, :] + back).astype(BF)

    @pl.when(info[0] > 0)
    def _():
        out_ref[split:, :] = part_ref[split:, :].astype(BF)


def hidden_block(info, c, k):
    z0, x, q = k // 4, k // 2 % 2, k % 2
    d = ((info[0] + x) % 2 * 2 + z0) * 4 + (info[1] + q) % 2 * 2 + info[2]
    return pl.ds(pl.multiple_of(d * 256 + c * TILE, TILE), TILE)


def ffn_kernel(c, first, half, info, n_own, n_other, b_own, b_other, *rest):
    if not first:
        earlier, rest = rest[:2], rest[2:]
    wg_hbm, wu_hbm, wd_hbm, hidden_ref, *rest = rest
    sums, rest = rest[:2], rest[2:]
    packs, rest = (rest[0:2], rest[2:4]), rest[4:]
    wg, wu, wd, ag, au, ad, n_buf, b_buf, sems, row_sems = rest
    r = pl.program_id(0)
    steps = pl.num_programs(0)
    block_rows = n_buf.shape[1]

    def weight_copies(kind):
        hbm, vmem = ((wg_hbm, wg), (wu_hbm, wu), (wd_hbm, wd))[kind]
        for k in range(8):
            src, dst = hidden_block(info, c, k), pl.ds(k * TILE, TILE)
            if kind < 2:
                yield pltpu.make_async_copy(hbm.at[:, src], vmem.at[:, dst], sems.at[kind, k])
            else:
                yield pltpu.make_async_copy(hbm.at[src, :], vmem.at[dst, :], sems.at[kind, k])

    def row_copies(step, sources):
        src = pl.ds(pl.multiple_of(step % half * block_rows, block_rows), block_rows)
        for i, (hbm, vmem) in enumerate(zip(sources, (n_buf, b_buf))):
            yield pltpu.make_async_copy(
                hbm.at[src, :], vmem.at[step % 2], row_sems.at[i, step % 2]
            )

    def start_rows(step):
        @pl.when(step < half)
        def _():
            for copy in row_copies(step, (n_own, b_own)):
                copy.start()

        @pl.when(step >= half)
        def _():
            for copy in row_copies(step, (n_other, b_other)):
                copy.start()

    @pl.when(r == 0)
    def _():
        start_rows(r)
        for kind in range(3):
            for copy in weight_copies(kind):
                copy.start()
        for acc in (ag, au, ad):
            acc[...] = jnp.zeros_like(acc)

    @pl.when(r + 1 < steps)
    def _():
        start_rows(r + 1)

    for copy in row_copies(r, (n_own, b_own)):
        copy.wait()

    @pl.when(r == 0)
    def _():
        for kind in range(3):
            for copy in weight_copies(kind):
                copy.wait()

    normed, delta = n_buf.at[r % 2], b_buf.at[r % 2]
    gate = mm(normed[...], wg[...])
    upward = mm(normed[...], wu[...])
    hidden_delta = mm_t(delta[...], wd[...])
    sigmoid = jax.nn.sigmoid(gate)
    active = gate * sigmoid
    hidden = (active * upward).astype(BF)
    up_delta = (hidden_delta * active).astype(BF)
    gate_delta = (hidden_delta * upward * (sigmoid + active * (1.0 - sigmoid))).astype(BF)
    hidden_ref[...] = hidden
    second = mm_t(gate_delta, wg[...]) + mm_t(up_delta, wu[...])
    if not first:
        second = second + jnp.where(r < half, earlier[0][...], earlier[1][...]).astype(F32)
    second = second.astype(BF)
    sums[0][...] = second
    sums[1][...] = second
    ag[...] += t_mm(normed[...], gate_delta)
    au[...] += t_mm(normed[...], up_delta)
    ad[...] += t_mm(delta[...], hidden)

    @pl.when(r == pl.num_programs(0) - 1)
    def _():
        def flip(bit, own):
            return (bit + own) % 2

        def tile(acc, row, col):
            row = pl.multiple_of(row * TILE, TILE)
            col = pl.multiple_of(col * TILE, TILE)
            return acc[pl.ds(row, TILE), pl.ds(col, TILE)].astype(BF)

        x_own, y_own, z1_own, z0_own = info[0], info[1], info[4] // 2, info[4] % 2
        for u in range(2):
            for x in range(2):
                for y in range(2):
                    lead, other = (x, y) if u == 0 else (y, x)
                    ref = packs[u][lead]

                    def put(at, value):
                        ref[other, at * TILE : (at + 1) * TILE, :] = value

                    for z1 in range(2):
                        for z0 in range(2):
                            z = flip(z1, z1_own) * 2 + flip(z0, z0_own)
                            at = 4 * z1 if z0 == 0 else 16 + 4 * z1
                            for i, acc in enumerate((ag, au)):
                                for q in range(2):
                                    col = u * 4 + x * 2 + flip(q, y_own)
                                    put(at + 2 * i + q, tile(acc, z * 2 + flip(y, y_own), col))
                        col = flip(u, z0_own) * 4 + flip(flip(z1, z1_own), x_own) * 2 + y
                        for dq in range(4):
                            put(8 + 4 * z1 + dq, tile(ad, flip(x, x_own) * 4 + dq, col))


def ffn_call(c, info, pieces, weights, previous, after=(), block_rows=256):
    rows, width = pieces[0].shape
    half = rows // block_rows
    first = previous is None
    hidden = 8 * TILE
    own = pl.BlockSpec((block_rows, width), lambda r, info: (jnp.minimum(r, half), 0))
    other = pl.BlockSpec((block_rows, width), lambda r, info: (jnp.maximum(r - half, 0), 0))
    every = pl.BlockSpec((block_rows, hidden), lambda r, info: (r, 0))
    packed = (2, 24 * TILE, TILE)
    pack = pl.BlockSpec(packed, lambda r, info: (0, 0, 0), pipeline_mode=pl.Buffered(1))
    extra = [] if first else list(previous)
    anywhere = pl.BlockSpec(memory_space=pl.ANY)
    return call_kernel(
        functools.partial(ffn_kernel, c, first, half),
        info,
        [*pieces, *extra, *weights],
        name="feed_forward",
        grid=(2 * half,),
        ins=[anywhere] * 4 + [own, other] * (len(extra) // 2) + [anywhere] * 3,
        outs=[every, own, other] + [pack] * 4,
        shapes=[
            shape_of((2 * rows, hidden)), shape_of((rows + block_rows, width)), shape_of((rows, width))
        ] + [shape_of(packed)] * 4,
        scratch=[
            pltpu.VMEM((width, hidden), BF),
            pltpu.VMEM((width, hidden), BF),
            pltpu.VMEM((hidden, width), BF),
            pltpu.VMEM((width, hidden), F32),
            pltpu.VMEM((width, hidden), F32),
            pltpu.VMEM((width, hidden), F32),
            pltpu.VMEM((2, block_rows, width), BF),
            pltpu.VMEM((2, block_rows, width), BF),
            pltpu.SemaphoreType.DMA((3, 8)),
            pltpu.SemaphoreType.DMA((2, 2)),
        ],
        vmem=60,
        cost=(18 * 2 * rows * width * hidden, 30 * MIB),
        after=after,
    )


def branch_kernel(half, info, ha, hb, b_own, b_other, wd_hbm, own_ref, other_ref, sum_ref, wd, sems):
    r = pl.program_id(0)

    def copies():
        for c in range(2):
            for k in range(8):
                dst = wd.at[c, pl.ds(k * TILE, TILE), :]
                yield pltpu.make_async_copy(wd_hbm.at[hidden_block(info, c, k), :], dst, sems.at[c, k])

    @pl.when(r == 0)
    def _():
        for copy in copies():
            copy.start()
        sum_ref[...] = jnp.zeros_like(sum_ref)
        for copy in copies():
            copy.wait()

    branch = mm(ha[...], wd[0]) + mm(hb[...], wd[1])
    delta = jnp.where(r < half, b_own[...], b_other[...]).astype(F32)
    sum_ref[0:1, :] += column_sum(delta * branch)
    branch = branch.astype(BF)
    own_ref[...] = branch
    other_ref[...] = branch


def branch_call(info, hiddens, deltas, down_weight, after, block_rows=512):
    rows, width = deltas[0].shape
    half = rows // block_rows
    hidden = hiddens[0].shape[1]
    every = pl.BlockSpec((block_rows, hidden), lambda r, info: (r, 0))
    own = pl.BlockSpec((block_rows, width), lambda r, info: (jnp.minimum(r, half), 0))
    own_in = pl.BlockSpec((block_rows, width), lambda r, info: (jnp.minimum(r, half - 1), 0))
    other = pl.BlockSpec((block_rows, width), lambda r, info: (jnp.maximum(r - half, 0), 0))
    return call_kernel(
        functools.partial(branch_kernel, half), info, [*hiddens, *deltas, down_weight],
        name="branch", grid=(2 * half,),
        ins=[every, every, own_in, other, pl.BlockSpec(memory_space=pl.ANY)],
        outs=[own, other, whole_spec((8, width))],
        shapes=[
            shape_of((rows + block_rows, width)), shape_of((rows, width)), shape_of((8, width), F32)
        ],
        scratch=[pltpu.VMEM((2, hidden, width), BF), pltpu.SemaphoreType.DMA((2, 8))],
        cost=(4 * 2 * rows * width * hidden, 16 * MIB), after=after,
    )


SWAP = [(0, 1), (1, 0)]
Z_NEAR = [(0, 1), (1, 0), (2, 3), (3, 2)]
Z_FAR = [(0, 2), (2, 0), (1, 3), (3, 1)]


def meet(*values):
    return lax.optimization_barrier(values)


def later(values, *needed):
    return lax.optimization_barrier((values, needed))[0]


def swap(values, axis):
    return lax.ppermute(values, axis, SWAP)


def plus(left, right):
    return (left.astype(F32) + right.astype(F32)).astype(BF)


def fold(keep, send, axis):
    return plus(keep, swap(send, axis))


def fold_two(keep, send, lead, other):
    total = fold(keep, send, lead)
    return fold(total[0], total[1], other)


def scatter_z(values):
    return lax.psum_scatter(values, "z", scatter_dimension=0, tiled=True)[0]


def turn_table(first, last, head_dim):
    pairs = head_dim // 2
    rates = np.exp(np.arange(pairs, dtype=np.float32) * np.float32(-2.0 * math.log(10000.0) / head_dim))
    angles = np.arange(first, last, dtype=np.float32)[:, None] * rates[None, :].astype(np.float32)
    cosine, sine = (np.tile(t(angles), (1, TILE // pairs)) for t in (np.cos, np.sin))
    front = (np.arange(TILE) % head_dim < pairs)[None, :]
    return np.stack([cosine, np.where(front, -sine, 0), np.where(front, 0, sine)]).astype(np.float32)


def fast_body(
    frames, cotangent, lengths, qkv_weight, out_weight, gate_weight, up_weight, down_weight,
    gain_table, bias_table,
):
    clips, rows, width = frames.shape
    count = clips * rows
    head_dim = width // HEADS
    scale = 1.0 / math.sqrt(head_dim)
    x_at, y_at, core_at, z_at = (lax.axis_index(a) for a in ("seq", "y", "core", "z"))
    start = x_at * rows
    info = jnp.concatenate(
        [jnp.stack([x_at, y_at, core_at, start, z_at]).astype(jnp.int32), lengths.astype(jnp.int32)]
    )
    flat = frames.reshape(count, width)
    tangent = cotangent.reshape(count, width)
    halo = lax.ppermute(
        frames[:, rows - TILE :].reshape(clips * TILE, width), "seq", [(0, 1)]
    )
    places = start + jnp.arange(rows)
    valid = (places[None, :] < lengths[:, None]).astype(F32).reshape(count, 1)
    branch_delta = (tangent.astype(F32) * valid * gain_table[:, 3]).astype(BF)
    table = jnp.concatenate([gain_table, bias_table, jnp.zeros((width, 2), F32)], axis=1).T
    seats = lax.axis_size("seq")
    own_turns = jnp.asarray(turn_table(0, seats * rows, head_dim))
    halo_turns = jnp.asarray(
        np.concatenate([turn_table(i * rows - TILE, i * rows, head_dim) for i in range(seats)], axis=1)
    )
    own_tab = pl.BlockSpec((3, rows, TILE), lambda r, info: (0, info[0], 0))
    halo_tab = pl.BlockSpec((3, TILE, TILE), lambda r, info: (0, info[0], 0))
    gb = whole_spec(table.shape)
    own = rows_spec(rows, width)
    halo_rows = rows_spec(TILE, width)
    qkv_rows = rows_spec(rows, 3 * width)
    kv_rows = rows_spec(TILE, 2 * width)
    w_qkv = whole_spec((width, 3 * width))
    w_key = pl.BlockSpec((width, width), lambda r, info: (0, 1))
    w_value = pl.BlockSpec((width, width), lambda r, info: (0, 2))
    w_out = whole_spec((width, width))
    sums = whole_spec((8, width))

    grid = (clips,)
    mac = 2 * count * width * width

    qkv, normed_one = call_kernel(
        qkv_kernel, info, [flat, qkv_weight, table, own_turns], name="qkv", grid=grid,
        ins=[own, w_qkv, gb, own_tab], outs=[qkv_rows, own],
        shapes=[shape_of((count, 3 * width)), shape_of((count, width))], cost=(3 * mac, 16 * MIB),
    )
    def half_rows(width, part):
        return pl.BlockSpec((TILE, width), lambda r, info: (2 * r + part, 0))

    totals_of = (2 * clips, width // TILE, 2 * TILE)
    seen = [shape_of((count, width)), shape_of(totals_of, F32)]

    def half_totals(part):
        return pl.BlockSpec((1, *totals_of[1:]), lambda r, info: (2 * r + part, 0, 0))

    late = call_kernel(
        functools.partial(attend_late_kernel, scale), info, [qkv], name="attend_late", grid=grid,
        ins=[qkv_rows], outs=[half_rows(width, 1), half_totals(1)], shapes=seen,
        cost=(2 * mac, 8 * MIB),
    )
    halo, branch_delta = lax.optimization_barrier((halo, branch_delta))
    branch_delta_other = swap(branch_delta, "core")
    kv_halo, normed_halo = call_kernel(
        halo_kernel, info, [halo, qkv_weight, qkv_weight, table, halo_turns], name="halo",
        grid=grid, ins=[halo_rows, w_key, w_value, gb, halo_tab],
        outs=[kv_rows, halo_rows],
        shapes=[shape_of((clips * TILE, 2 * width)), shape_of((clips * TILE, width))],
        cost=(mac, 8 * MIB), after=late,
    )
    context, log_totals = call_kernel(
        functools.partial(attend_kernel, scale, 0), info, [qkv, kv_halo], name="attend_early",
        grid=grid, ins=[half_rows(3 * width, 0), kv_rows],
        outs=[half_rows(width, 0), half_totals(0)], shapes=seen,
        cost=(2 * mac, 12 * MIB), onto=late,
    )
    attended, normed_two = call_kernel(
        out_kernel, info, [context, flat, out_weight, table], name="project", grid=grid,
        ins=[own, own, w_out, gb], outs=[own, own],
        shapes=[shape_of((count, width), F32), shape_of((count, width))], cost=(mac, 12 * MIB),
    )
    normed_two_other = swap(normed_two, "core")

    pieces = (normed_two, normed_two_other, branch_delta, branch_delta_other)
    weights = (gate_weight, up_weight, down_weight)
    def start_pair(keeps):
        (keep_a, send_a), (keep_b, send_b) = keeps
        return (keep_a, swap(send_a, "seq")), (keep_b, swap(send_b, "y"))

    def second_pair(totals):
        (stay_a, go_a), (stay_b, go_b) = totals
        return (stay_a, swap(go_a, "y")), (stay_b, swap(go_b, "seq"))

    def halves(pairs):
        return [tuple(plus(keep[k], came[k]) for k in range(2)) for keep, came in pairs]

    def near_pair(pairs):
        a, b = (plus(stay, came).reshape(24, TILE, TILE) for stay, came in pairs)
        keep, send = jnp.concatenate([a[:16], b[:8]]), jnp.concatenate([a[16:], b[8:]])
        return keep, lax.ppermute(send, "z", Z_NEAR)

    def far_pair(pair):
        total = plus(*pair).reshape(3, 2, 4, TILE, TILE)
        return total[:, 0], lax.ppermute(total[:, 1], "z", Z_FAR)

    def run_ffn(c, previous, after):
        *state, keep_a, send_a, keep_b, send_b = ffn_call(
            c, info, pieces, weights, previous, after
        )
        return state, ((keep_a, send_a), (keep_b, send_b))

    (hidden_0, *previous), grads_0 = run_ffn(0, None, ())
    moved_0 = start_pair(grads_0)
    (hidden_1, second, second_sent), grads_1 = run_ffn(1, previous, ())
    second, second_sent, grads_1, moved_0 = meet(second, second_sent, grads_1, moved_0)
    second_other = swap(second_sent, "core")
    totals_0 = halves(moved_0)
    grads_1, second_other, totals_0 = meet(grads_1, second_other, totals_0)
    moved_0 = second_pair(totals_0)
    moved_1 = start_pair(grads_1)

    middle_delta, context_delta, out_grad, sums_two = call_kernel(
        out_back_kernel, info,
        [second, second_other, attended, flat, tangent, context, out_weight, table],
        name="project_back", grid=grid,
        ins=[own, own, own, own, own, own, w_out, gb],
        outs=[own, own, w_out, sums],
        shapes=[
            shape_of((count, width), F32), shape_of((count, width)), shape_of((width, width)),
            shape_of((8, width), F32),
        ],
        scratch=[pltpu.VMEM((width, width), F32)], cost=(2 * mac, 24 * MIB), after=tuple(t for pair in totals_0 for t in pair),
    )
    out_grad = lax.psum_scatter(out_grad, ("z", "y", "core"), scatter_dimension=0, tiled=True)

    def attend_back(first_clip, onto, after, taken):
        def at(rows, width):
            return pl.BlockSpec((rows, width), lambda r, info: (r + first_clip, 0))

        return call_kernel(
            functools.partial(attend_back_kernel, scale, first_clip), info,
            [qkv, kv_halo, context_delta, log_totals, own_turns, halo_turns],
            name="attend_back", grid=(taken,),
            ins=[
                at(rows, 3 * width), at(TILE, 2 * width), at(rows, width),
                pl.BlockSpec((2, *totals_of[1:]), lambda r, info: (r + first_clip, 0, 0)),
                own_tab, halo_tab,
            ],
            outs=[at(rows, 3 * width), at(TILE, 2 * width)],
            shapes=[shape_of((count, 3 * width)), shape_of((clips * TILE, 2 * width))],
            cost=(2.5 * mac * taken, 6 * MIB * taken), after=after, onto=onto,
        )

    some = clips - 1

    def first_halo(first_clip, mixed_halo, after, taken):
        def at(width):
            return pl.BlockSpec((TILE, width), lambda r, info: (r + first_clip, 0))

        return call_kernel(
            functools.partial(first_halo_kernel, first_clip), info,
            [mixed_halo, qkv_weight, qkv_weight, halo], name="first_halo", grid=(taken,),
            ins=[at(2 * width), w_key, w_value, at(width)], outs=[halo_rows, sums],
            shapes=[shape_of((taken * TILE, width)), shape_of((8, width), F32)],
            cost=(mac // 4 * taken, 6 * MIB), after=after,
        )

    mixed = attend_back(0, (), (), some)
    branch, branch_sent, sums_branch = branch_call(
        info, (hidden_0, hidden_1), (branch_delta, branch_delta_other), down_weight, (mixed[1],)
    )
    mixed, moved_0, moved_1, branch_sent = meet(mixed, moved_0, moved_1, branch_sent)
    totals_1 = halves(moved_1)
    moved_1 = second_pair(totals_1)
    near_0 = near_pair(moved_0)
    branch_other = swap(branch_sent, "core")
    ready = (*(t for pair in totals_1 for t in pair), near_0[0])
    back_a, sums_a = first_halo(0, mixed[1], ready, some)
    mixed_delta, mixed_halo = attend_back(some, mixed, (back_a,), clips - some)
    mixed_delta, mixed_halo, back_a, moved_1, near_0, branch_other = meet(
        mixed_delta, mixed_halo, back_a, moved_1, near_0, branch_other
    )
    came_a = lax.ppermute(back_a, "seq", [(1, 0)])
    far_0 = far_pair(near_0)

    cut = 3 * width // 6
    def x_seat(t, info):
        return (t // 3 + info[0]) % 2

    left_spec = pl.BlockSpec((1, 2, 4, 64, cut), lambda t, info: (x_seat(t, info), 0, 0, 0, 0))
    right_spec = pl.BlockSpec(
        (2, 1, 1, 4, 64, cut),
        lambda t, info: (0, x_seat(t, info), jnp.maximum(t % 3 - 1, 0), 0, 0, 0),
    )
    packed = [shape_of((2, 2, 4, 64, cut)), shape_of((2, 2, 2, 4, 64, cut))]
    keep_l, keep_r, send_l, send_r = call_kernel(
        qkv_grad_kernel, info, [normed_one, mixed_delta, normed_halo, mixed_halo],
        name="qkv_grad", grid=(6,),
        ins=[
            whole_spec((count, width)),
            pl.BlockSpec((count, cut), lambda t, info: (0, t)),
            whole_spec((clips * TILE, width)),
            pl.BlockSpec((clips * TILE, cut), lambda t, info: (0, jnp.maximum(t - 2, 0))),
        ],
        outs=[left_spec, right_spec] * 2, shapes=packed * 2,
        scratch=[pltpu.VMEM((width, cut), F32)], cost=(4 * mac, 16 * MIB),
        after=(far_0[0],),
    )
    came_a, far_0, keep_l, keep_r, send_l, send_r = meet(
        came_a, far_0, keep_l, keep_r, send_l, send_r
    )
    qkv_came = swap(send_l, "core"), swap(send_r, "core")
    back_b, sums_b = first_halo(some, mixed_halo, (keep_l,), clips - some)
    qkv_came, back_b = meet(qkv_came, back_b)
    came_b = lax.ppermute(back_b, "seq", [(1, 0)])
    came_l, came_r = qkv_came
    stay_l, go_l = (plus(keep_l[k], came_l[k]) for k in range(2))
    stay_r, go_r = (plus(keep_r[k], came_r[k]) for k in range(2))
    go_l, go_r = swap(go_l, "seq"), swap(go_r, "y")
    near_1 = near_pair(later(moved_1, stay_l, stay_r, back_b))
    part_grad, sums_one = call_kernel(
        first_back_kernel, info, [mixed_delta, qkv_weight, flat, middle_delta, table],
        name="first_back", grid=grid, ins=[qkv_rows, w_qkv, own, own, gb], outs=[own, sums],
        shapes=[shape_of((count, width), F32), shape_of((8, width), F32)],
        cost=(3 * mac, 24 * MIB), after=(stay_l, stay_r, near_1[0]),
    )
    go_l, go_r, near_1, came_b, part_grad, sums_one = meet(
        go_l, go_r, near_1, came_b, part_grad, sums_one
    )
    share = width // 16
    ones = sums_one + sums_a + sums_b
    nought = jnp.zeros((width,), F32)
    scale_mlp = sums_branch[0] / gain_table[:, 3]
    vectors = jnp.stack(
        [ones[0], sums_two[0], ones[1], nought, sums_two[1], scale_mlp, sums_two[2], nought]
    )
    left, right = plus(stay_l, go_l), plus(stay_r, go_r)
    go_l, go_r = swap(left[1], "y"), swap(right[1], "seq")
    vectors_core = swap(vectors, "core")
    far_1 = far_pair(near_1)
    output = call_kernel(
        output_kernel, info, [flat, attended, branch, branch_other, table],
        name="output", grid=grid, ins=[own, own, own, own, gb], outs=own,
        shapes=shape_of((count, width)), cost=(0, 14 * MIB),
        after=(left, right, far_1[0], came_b, vectors),
    )
    go_l, go_r, vectors_core, output = meet(go_l, go_r, vectors_core, output)
    vectors = vectors + vectors_core
    vectors_x = swap(vectors, "seq")
    left, right = plus(left[0], go_l), plus(right[0], go_r)
    qkv_total = jnp.concatenate([left[None], right]).reshape(3, 2, 2, 64, cut)
    qkv_near = qkv_total[:, :, 1]
    go = lax.ppermute(qkv_near, "z", Z_NEAR)
    input_grad = call_kernel(
        functools.partial(input_grad_kernel, some), info, [part_grad, came_a, came_b, flat, table],
        name="input_grad", grid=grid,
        ins=[
            own,
            pl.BlockSpec((TILE, width), lambda r, info: (jnp.minimum(r, some - 1), 0)),
            pl.BlockSpec((TILE, width), lambda r, info: (jnp.maximum(r - some, 0), 0)),
            own, gb,
        ],
        outs=own, shapes=shape_of((count, width)), cost=(0, 8 * MIB),
        after=(left, right, output, qkv_total, vectors),
    )
    go, far_1, vectors_x, input_grad = meet(go, far_1, vectors_x, input_grad)
    vectors = vectors + vectors_x
    vectors = vectors + swap(vectors, "y")
    vectors = vectors + lax.ppermute(vectors, "z", Z_NEAR)
    vectors = vectors + lax.ppermute(vectors, "z", Z_FAR)
    qkv_total = plus(qkv_total[:, :, 0], go)
    qkv_total = plus(qkv_total[:, 0], lax.ppermute(qkv_total[:, 1], "z", Z_FAR))
    qkv_grad = qkv_total.transpose(1, 0, 2).reshape(-1, 3 * cut).astype(F32)
    out_halves = later(out_grad, qkv_total).reshape(-1, 2, width // 2)
    out_kept = lax.dynamic_index_in_dim(out_halves, x_at, axis=1, keepdims=False)
    out_sent = lax.dynamic_index_in_dim(out_halves, 1 - x_at, axis=1, keepdims=False)
    out_grad = out_kept.astype(F32) + swap(out_sent, "seq").astype(F32)

    vectors = vectors.reshape(2, 4, 16, share).transpose(2, 0, 1, 3).reshape(32, 4, share)
    seat = ((z_at * 2 + y_at) * 2 + core_at) * 2 + x_at
    vectors = lax.dynamic_index_in_dim(vectors, seat, keepdims=False).T
    gain_grad, bias_grad = vectors[:, :2], vectors[:, 2:3]

    tiles = jnp.stack([plus(*far_0), plus(*far_1)])
    gates = tiles[:, ::2].reshape(2, 2, 2, 2, 2, share, TILE)
    kept = lax.dynamic_index_in_dim(gates, core_at, axis=4, keepdims=False)
    sent = lax.dynamic_index_in_dim(gates, 1 - core_at, axis=4, keepdims=False)
    came = swap(sent, "core")
    both = jnp.where(core_at == 0, jnp.stack([kept, came], 4), jnp.stack([came, kept], 4))
    both = both.transpose(2, 5, 1, 3, 4, 0, 6).astype(F32)
    gate_grad = both[0].reshape(share, -1)
    up_grad = both[1].reshape(share, -1)
    down_grad = tiles[:, 1].reshape(2, width // 2, TILE).transpose(0, 2, 1).astype(F32)
    down_grad = down_grad.reshape(2 * TILE, width // 2)
    shape = (clips, rows, width)
    return (
        output.reshape(shape), input_grad.reshape(shape), qkv_grad, out_grad, gate_grad, up_grad,
        down_grad, gain_grad, bias_grad,
    )


def solution(mesh):
    placed = (("dp", "seq", None),) * 2 + (("dp",),) + ((),) * 7
    given = (("dp", "seq", None),) * 2 + (("dp", "seq"),) * 7
    fast = mesh.shape["dp"] == 16 and mesh.shape["seq"] == 2
    dp_axes = ("z", "y", "core") if fast else "dp"

    def specs(entries):
        return tuple(P(*(dp_axes if a == "dp" else a for a in entry)) for entry in entries)

    if fast:
        mesh = Mesh(mesh.devices.reshape(4, 2, 2, 2), ("z", "y", "core", "seq"))
    return jax.shard_map(
        fast_body if fast else body,
        mesh=mesh,
        in_specs=specs(placed),
        out_specs=specs(given),
        check_vma=False,
    )
```

```python
import functools
import math

import jax
import jax.numpy as jnp
import numpy as np
from jax import lax
from jax.experimental import pallas as pl
from jax.experimental.pallas import tpu as pltpu
from jax.sharding import Mesh
from jax.sharding import PartitionSpec as P

HEADS = 16
WINDOW = 128


NORM_EPS = 1e-05
MASKED = -1e30


def norm_forward(values, gain_col, shift_col):
    row_mean = jnp.mean(values, axis=-1, keepdims=True)
    centred = values - row_mean
    inverse = lax.rsqrt(jnp.mean(centred * centred, axis=-1, keepdims=True) + NORM_EPS)
    normal = centred * inverse
    return (normal * gain_col + shift_col, normal, inverse)


def norm_backward(upstream, normal, inverse, gain_col):
    scaled = upstream * gain_col
    inner_term = (
        scaled
        - jnp.mean(scaled, axis=-1, keepdims=True)
        - normal * jnp.mean(scaled * normal, axis=-1, keepdims=True)
    )
    return (inverse * inner_term, jnp.sum(upstream * normal, axis=0), jnp.sum(upstream, axis=0))


def rotary_tables(places, head_dim):
    pair_count = head_dim // 2
    freq_rates = jnp.exp(
        jnp.arange(pair_count).astype(jnp.float32) * (-2.0 * math.log(10000.0) / head_dim)
    )
    angles = places.astype(jnp.float32)[:, None] * freq_rates[None, :]
    return (jnp.cos(angles), jnp.sin(angles))


def rotate(values, cosine, sine_table, direction):
    pair_count = values.shape[-1] // 2
    leading = values[..., :pair_count]
    trailing = values[..., pair_count:]
    cos_wide = cosine[:, None, :]
    sin_wide = sine_table[:, None, :] * direction
    return jnp.concatenate(
        [leading * cos_wide - trailing * sin_wide, trailing * cos_wide + leading * sin_wide],
        axis=-1,
    )


def inner_rows(left_op, right_op):
    return lax.dot_general(
        left_op, right_op, (((0,), (0,)), ((), ())), preferred_element_type=jnp.float32
    )


def times_transposed(left_op, right_op):
    return lax.dot_general(
        left_op, right_op, (((1,), (1,)), ((), ())), preferred_element_type=jnp.float32
    )


def body(
    frames,
    cotangent,
    lengths,
    qkv_weight,
    out_weight,
    gate_weight,
    up_weight,
    down_weight,
    gain_table,
    bias_table,
):
    seq_parts = lax.axis_size("seq")
    seq_index = lax.axis_index("seq")
    model_width = frames.shape[2]
    clip_len = frames.shape[1] * seq_parts
    head_dim = model_width // HEADS
    score_scale = 1.0 / math.sqrt(head_dim)
    frames_here, tangent_here = (frames, cotangent)
    places = seq_index * frames.shape[1] + jnp.arange(frames.shape[1])
    heads_here = HEADS // seq_parts
    groups, row_len = (frames_here.shape[0], frames_here.shape[1])
    row_count = groups * row_len
    width_here = heads_here * head_dim
    valid_rows = (places[None, :] < lengths[:, None]).astype(jnp.float32).reshape(row_count, 1)
    cosine, sine_table = rotary_tables(places, head_dim)
    full_cosine, full_sine = rotary_tables(jnp.arange(clip_len), head_dim)
    source = frames_here.astype(jnp.float32).reshape(row_count, model_width)
    normed_one, normal_one, inverse_one = norm_forward(source, gain_table[:, 0], bias_table[:, 0])
    normed_one = normed_one.astype(jnp.bfloat16)
    mixed_rows = jnp.dot(normed_one, qkv_weight, preferred_element_type=jnp.float32)
    shaped = mixed_rows.reshape(groups, row_len, 3, HEADS, head_dim)
    queries = (
        rotate(shaped[:, :, 0], cosine, sine_table, 1.0)
        .astype(jnp.bfloat16)
        .reshape(groups, row_len, model_width)
    )
    key_rows = (
        rotate(shaped[:, :, 1], cosine, sine_table, 1.0)
        .astype(jnp.bfloat16)
        .reshape(groups, row_len, model_width)
    )
    values = shaped[:, :, 2].astype(jnp.bfloat16).reshape(groups, row_len, model_width)
    head_queries, head_keys, head_values = (
        lax.all_to_all(queries, "seq", split_axis=2, concat_axis=1, tiled=True),
        lax.all_to_all(key_rows, "seq", split_axis=2, concat_axis=1, tiled=True),
        lax.all_to_all(values, "seq", split_axis=2, concat_axis=1, tiled=True),
    )
    head_queries = head_queries.reshape(groups, clip_len, heads_here, head_dim)
    head_keys = head_keys.reshape(groups, clip_len, heads_here, head_dim)
    head_values = head_values.reshape(groups, clip_len, heads_here, head_dim)
    query_pos = jnp.arange(clip_len)[:, None]
    key_pos = jnp.arange(clip_len)[None, :]
    window_mask = (key_pos <= query_pos) & (key_pos > query_pos - WINDOW)

    def clip_scores(clip_queries, clip_keys, length):
        products = jnp.einsum(
            "qhd,khd->hqk", clip_queries, clip_keys, preferred_element_type=jnp.float32
        )
        allowed = window_mask & (key_pos < length)
        return (jnp.where(allowed[None], products * score_scale, MASKED), allowed)

    def attend(block_item):
        clip_queries, clip_keys, clip_values, length = block_item
        scores, allowed = clip_scores(clip_queries, clip_keys, length)
        top_score = jnp.max(scores, axis=-1, keepdims=True)
        exponent = jnp.exp(scores - top_score)
        row_total = jnp.sum(exponent, axis=-1, keepdims=True)
        weights_low = (exponent / row_total).astype(jnp.bfloat16)
        context = jnp.einsum(
            "hqk,khd->qhd", weights_low, clip_values, preferred_element_type=jnp.float32
        )
        return (context.astype(jnp.bfloat16), top_score + jnp.log(row_total))

    context_heads, log_totals = lax.map(attend, (head_queries, head_keys, head_values, lengths))
    context_heads = context_heads.reshape(groups, clip_len, width_here)
    context = lax.all_to_all(context_heads, "seq", split_axis=1, concat_axis=2, tiled=True).reshape(
        row_count, model_width
    )
    attended = jnp.dot(context, out_weight, preferred_element_type=jnp.float32)
    middle = source + gain_table[:, 2] * attended
    normed_two, normal_two, inverse_two = norm_forward(middle, gain_table[:, 1], bias_table[:, 1])
    normed_two = normed_two.astype(jnp.bfloat16)
    gate_rows = jnp.dot(normed_two, gate_weight, preferred_element_type=jnp.float32)
    upward = jnp.dot(normed_two, up_weight, preferred_element_type=jnp.float32)
    sigmoid_gate = jax.nn.sigmoid(gate_rows)
    activated = gate_rows * sigmoid_gate
    hidden = (activated * upward).astype(jnp.bfloat16)
    branch = jnp.dot(hidden, down_weight, preferred_element_type=jnp.float32)
    output = (
        ((middle + gain_table[:, 3] * branch) * valid_rows)
        .astype(jnp.bfloat16)
        .reshape(groups, row_len, model_width)
    )
    output_delta = tangent_here.astype(jnp.float32).reshape(row_count, model_width) * valid_rows
    branch_delta = (output_delta * gain_table[:, 3]).astype(jnp.bfloat16)
    scale_mlp = jnp.sum(output_delta * branch, axis=0)
    down_grad = inner_rows(hidden, branch_delta)
    hidden_delta = times_transposed(branch_delta, down_weight)
    up_delta = (hidden_delta * activated).astype(jnp.bfloat16)
    gate_delta = (
        hidden_delta * upward * sigmoid_gate * (1.0 + gate_rows * (1.0 - sigmoid_gate))
    ).astype(jnp.bfloat16)
    gate_grad = inner_rows(normed_two, gate_delta)
    up_grad = inner_rows(normed_two, up_delta)
    second_delta = times_transposed(gate_delta, gate_weight) + times_transposed(up_delta, up_weight)
    back_two, gain_two, bias_two = norm_backward(
        second_delta, normal_two, inverse_two, gain_table[:, 1]
    )
    middle_delta = output_delta + back_two
    attended_delta = (middle_delta * gain_table[:, 2]).astype(jnp.bfloat16)
    scale_attn = jnp.sum(middle_delta * attended, axis=0)
    out_grad = inner_rows(context, attended_delta)
    context_delta = (
        times_transposed(attended_delta, out_weight)
        .astype(jnp.bfloat16)
        .reshape(groups, row_len, model_width)
    )
    context_heads_delta = lax.all_to_all(
        context_delta, "seq", split_axis=2, concat_axis=1, tiled=True
    )
    context_heads_delta = context_heads_delta.reshape(groups, clip_len, heads_here, head_dim)

    def attend_back(block_item):
        clip_queries, clip_keys, clip_values, length, log_total, clip_delta = block_item
        scores, allowed = clip_scores(clip_queries, clip_keys, length)
        weights = jnp.exp(scores - log_total)
        weights_low = weights.astype(jnp.bfloat16)
        weight_delta = jnp.einsum(
            "qhd,khd->hqk", clip_delta, clip_values, preferred_element_type=jnp.float32
        )
        row_inner = jnp.sum(weight_delta * weights, axis=-1, keepdims=True)
        product_delta = jnp.where(
            allowed[None], weights * (weight_delta - row_inner) * score_scale, 0.0
        ).astype(jnp.bfloat16)
        query_delta = jnp.einsum(
            "hqk,khd->qhd", product_delta, clip_keys, preferred_element_type=jnp.float32
        )
        key_delta = jnp.einsum(
            "hqk,qhd->khd", product_delta, clip_queries, preferred_element_type=jnp.float32
        )
        value_delta = jnp.einsum(
            "hqk,qhd->khd", weights_low, clip_delta, preferred_element_type=jnp.float32
        )
        query_delta = rotate(query_delta, full_cosine, full_sine, -1.0).astype(jnp.bfloat16)
        key_delta = rotate(key_delta, full_cosine, full_sine, -1.0).astype(jnp.bfloat16)
        return (query_delta, key_delta, value_delta.astype(jnp.bfloat16))

    query_delta, key_delta, value_delta = lax.map(
        attend_back,
        (head_queries, head_keys, head_values, lengths, log_totals, context_heads_delta),
    )
    query_delta = query_delta.reshape(groups, clip_len, width_here)
    key_delta = key_delta.reshape(groups, clip_len, width_here)
    value_delta = value_delta.reshape(groups, clip_len, width_here)
    query_back, key_back, value_back = (
        lax.all_to_all(query_delta, "seq", split_axis=1, concat_axis=2, tiled=True),
        lax.all_to_all(key_delta, "seq", split_axis=1, concat_axis=2, tiled=True),
        lax.all_to_all(value_delta, "seq", split_axis=1, concat_axis=2, tiled=True),
    )
    mixed_delta = jnp.concatenate(
        [
            query_back.reshape(row_count, model_width),
            key_back.reshape(row_count, model_width),
            value_back.reshape(row_count, model_width),
        ],
        axis=1,
    )
    qkv_grad = inner_rows(normed_one, mixed_delta)
    first_delta = times_transposed(mixed_delta, qkv_weight)
    back_one, gain_one, bias_one = norm_backward(
        first_delta, normal_one, inverse_one, gain_table[:, 0]
    )
    input_grad = (
        (middle_delta + back_one).astype(jnp.bfloat16).reshape(groups, row_len, model_width)
    )
    gain_grad = jnp.stack([gain_one, gain_two, scale_attn, scale_mlp], axis=1)
    bias_grad = jnp.stack([bias_one, bias_two], axis=1)
    over_clips = (
        lax.psum_scatter(qkv_grad, "dp", scatter_dimension=0, tiled=True),
        lax.psum_scatter(out_grad, "dp", scatter_dimension=0, tiled=True),
        lax.psum_scatter(gate_grad, "dp", scatter_dimension=0, tiled=True),
        lax.psum_scatter(up_grad, "dp", scatter_dimension=0, tiled=True),
        lax.psum_scatter(down_grad, "dp", scatter_dimension=0, tiled=True),
        lax.psum_scatter(gain_grad, "dp", scatter_dimension=0, tiled=True),
        lax.psum_scatter(bias_grad, "dp", scatter_dimension=0, tiled=True),
    )
    summed = (
        lax.psum_scatter(
            over_clips[0].astype(jnp.bfloat16), "seq", scatter_dimension=1, tiled=True
        ).astype(jnp.float32),
        lax.psum_scatter(
            over_clips[1].astype(jnp.bfloat16), "seq", scatter_dimension=1, tiled=True
        ).astype(jnp.float32),
        lax.psum_scatter(
            over_clips[2].astype(jnp.bfloat16), "seq", scatter_dimension=1, tiled=True
        ).astype(jnp.float32),
        lax.psum_scatter(
            over_clips[3].astype(jnp.bfloat16), "seq", scatter_dimension=1, tiled=True
        ).astype(jnp.float32),
        lax.psum_scatter(
            over_clips[4].astype(jnp.bfloat16), "seq", scatter_dimension=1, tiled=True
        ).astype(jnp.float32),
        lax.psum_scatter(
            over_clips[5].astype(jnp.bfloat16), "seq", scatter_dimension=1, tiled=True
        ).astype(jnp.float32),
        lax.psum_scatter(
            over_clips[6].astype(jnp.bfloat16), "seq", scatter_dimension=1, tiled=True
        ).astype(jnp.float32),
    )
    return (
        output,
        input_grad,
        summed[0],
        summed[1],
        summed[2],
        summed[3],
        summed[4],
        summed[5],
        summed[6],
    )


BF = jnp.bfloat16
F32 = jnp.float32
TILE = 128
MIB = 1024 * 1024
HINT = 0.25


def mm(left, right):
    return lax.dot_general(left, right, (((1,), (0,)), ((), ())), preferred_element_type=F32)


def mm_t(left, right):
    return lax.dot_general(left, right, (((1,), (1,)), ((), ())), preferred_element_type=F32)


def t_mm(left, right):
    return lax.dot_general(left, right, (((0,), (0,)), ((), ())), preferred_element_type=F32)


def call_kernel(
    kernel, info, args, *, name, grid, ins, outs, shapes, scratch=(), vmem=60, cost=None, after=(),
    onto=(),
):
    flops, moved = cost
    aliases = {1 + len(args) + len(after) + k: k for k in range(len(onto))}
    after = (*after, *onto)
    count, unread = len(args), len(after)

    def run(info, *refs):
        kernel(info, *refs[:count], *refs[count + unread :])

    args = [*args, *after]
    ins = [*ins] + [pl.BlockSpec(memory_space=pl.ANY)] * unread
    return pl.pallas_call(
        run,
        grid_spec=pltpu.PrefetchScalarGridSpec(
            num_scalar_prefetch=1, grid=grid, in_specs=ins, out_specs=outs, scratch_shapes=scratch
        ),
        out_shape=shapes,
        input_output_aliases=aliases,
        compiler_params=pltpu.CompilerParams(
            dimension_semantics=("arbitrary",) * len(grid), vmem_limit_bytes=vmem * MIB
        ),
        cost_estimate=pl.CostEstimate(
            flops=int(flops * HINT), bytes_accessed=int(moved * HINT), transcendentals=0
        ),
        name=name,
    )(info, *args)


def shape_of(shape, dtype=BF):
    return jax.ShapeDtypeStruct(shape, dtype)


def rows_spec(rows, width, column=0):
    return pl.BlockSpec((rows, width), lambda r, info: (r, column))


def whole_spec(shape):
    return pl.BlockSpec(shape, lambda r, info: (0,) * len(shape))


LEN0 = 5


def norm_stats(values):
    row_mean = jnp.mean(values, axis=-1, keepdims=True)
    centred = values - row_mean
    inverse = lax.rsqrt(jnp.mean(centred * centred, axis=-1, keepdims=True) + NORM_EPS)
    return centred * inverse, inverse


def norm_back(upstream, normal, inverse, gain):
    scaled = upstream * gain
    return inverse * (
        scaled
        - jnp.mean(scaled, axis=-1, keepdims=True)
        - normal * jnp.mean(scaled * normal, axis=-1, keepdims=True)
    )


def turn(values, cosine, sine_a, sine_b):
    return (
        values * cosine
        + pltpu.roll(values, TILE - 32, 1) * sine_a
        + pltpu.roll(values, 32, 1) * sine_b
    )


def column_sum(values):
    return jnp.sum(values, axis=0, keepdims=True)


def staged(count, *stages):
    kept = [{} for _ in stages]
    for step in range(count + len(stages) - 1):
        for k, stage in enumerate(stages):
            i = step - k
            if 0 <= i < count:
                kept[k][i] = stage(i, kept[k - 1].pop(i)) if k else stage(i)


def qkv_kernel(info, x_ref, w_ref, gb_ref, tab_ref, qkv_ref, n_ref):
    r = pl.program_id(0)
    rows = tab_ref.shape[1]
    parts = x_ref.shape[0] // rows
    places = [info[LEN0 + r * parts + p] for p in range(parts)]
    live = functools.reduce(jnp.logical_or, [info[3] < place for place in places])
    width = x_ref.shape[1]
    piece = 2 * TILE
    pieces = 3 * width // piece

    @pl.when(live)
    def _():
        normed = {}

        def product(i):
            p, k = divmod(i, pieces)
            at_rows = slice(p * rows, (p + 1) * rows)
            if k == 0:
                normal, _ = norm_stats(x_ref[at_rows, :].astype(F32))
                normed[p] = (normal * gb_ref[0:1, :] + gb_ref[4:5, :]).astype(BF)
                n_ref[at_rows, :] = normed[p]
            return mm(normed[p], w_ref[:, k * piece : (k + 1) * piece])

        def put(i, mixed):
            p, k = divmod(i, pieces)
            at_rows = slice(p * rows, (p + 1) * rows)
            for t in range(piece // TILE):
                value = mixed[:, t * TILE : (t + 1) * TILE]
                if k * piece < 2 * width:
                    value = turn(value, tab_ref[0], tab_ref[1], tab_ref[2])
                at = k * piece + t * TILE
                qkv_ref[at_rows, at : at + TILE] = value.astype(BF)

        staged(parts * pieces, product, put)

    @pl.when(jnp.logical_not(live))
    def _():
        qkv_ref[...] = jnp.zeros_like(qkv_ref)
        n_ref[...] = jnp.zeros_like(n_ref)


def halo_kernel(info, x_ref, wk_ref, wv_ref, gb_ref, tab_ref, kv_ref, n_ref):
    live = info[0] > 0
    rows, width = x_ref.shape
    piece = 2 * TILE
    pieces = width // piece

    @pl.when(live)
    def _():
        normal, _ = norm_stats(x_ref[...].astype(F32))
        normed = (normal * gb_ref[0:1, :] + gb_ref[4:5, :]).astype(BF)
        n_ref[...] = normed

        def product(i):
            ref, k = (wk_ref, i) if i < pieces else (wv_ref, i - pieces)
            return mm(normed, ref[:, k * piece : (k + 1) * piece])

        def put(i, mixed):
            if i >= pieces:
                kv_ref[:, i * piece : (i + 1) * piece] = mixed.astype(BF)
                return
            for t in range(piece // TILE):
                at = i * piece + t * TILE
                for row in range(0, rows, TILE):
                    value = mixed[row : row + TILE, t * TILE : (t + 1) * TILE]
                    value = turn(value, tab_ref[0], tab_ref[1], tab_ref[2])
                    kv_ref[row : row + TILE, at : at + TILE] = value.astype(BF)

        staged(2 * pieces, product, put)

    @pl.when(jnp.logical_not(live))
    def _():
        kv_ref[...] = jnp.zeros_like(kv_ref)
        n_ref[...] = jnp.zeros_like(n_ref)


def window_bias(info, clip, block):
    j = lax.broadcasted_iota(jnp.int32, (2 * TILE, 2 * TILE), 0)
    i = lax.broadcasted_iota(jnp.int32, (2 * TILE, 2 * TILE), 1) % TILE
    key = info[3] + (block - 1) * TILE + j
    allowed = (j > i) & (j <= i + TILE) & (key >= 0) & (key < info[LEN0 + clip])
    return jnp.where(allowed, 0.0, MASKED)


def two_heads(values):
    lane = lax.broadcasted_iota(jnp.int32, values.shape, 1)
    nought = jnp.zeros_like(values)
    return jnp.concatenate(
        [jnp.where(lane < 64, values, nought), jnp.where(lane < 64, nought, values)], axis=0
    )


def one_row(turned):
    return jnp.concatenate([turned[:64, :TILE], turned[64:, TILE:]], axis=0).T


def key_window(halo_ref, own_ref, block, at, own_at):
    if block == 0:
        return jnp.concatenate(
            [halo_ref[:, at : at + TILE], own_ref[0:TILE, own_at : own_at + TILE]], axis=0
        )
    return own_ref[(block - 1) * TILE : (block + 1) * TILE, own_at : own_at + TILE]


def attend_kernel(scale, block, info, qkv_ref, kvh_ref, ctx_ref, lse_ref):
    clip = pl.program_id(0)
    width = ctx_ref.shape[1]
    at_rows = slice(block * TILE, (block + 1) * TILE)
    live = info[3] < info[LEN0 + clip]

    @pl.when(live)
    def _():
        bias = window_bias(info, clip, block)

        def score(pair):
            at = pair * TILE
            queries = two_heads(qkv_ref[at_rows, at : at + TILE] * BF(scale))
            return mm_t(key_window(kvh_ref, qkv_ref, block, at, width + at), queries)

        def weigh(pair, scores):
            scores = scores + bias
            top = jnp.max(scores, axis=0, keepdims=True)
            exponent = jnp.exp(scores - top)
            total = jnp.sum(exponent, axis=0, keepdims=True)
            lse_ref[0, pair : pair + 1, :] = top + jnp.log(total)
            return (exponent * (1.0 / total)).astype(BF)

        def gather(pair, weights):
            at = pair * TILE
            values = key_window(kvh_ref, qkv_ref, block, width + at, 2 * width + at)
            return t_mm(values, weights)

        def put(pair, turned):
            ctx_ref[:, pair * TILE : (pair + 1) * TILE] = one_row(turned).astype(BF)

        staged(width // TILE, score, weigh, gather, put)

    @pl.when(jnp.logical_not(live))
    def _():
        ctx_ref[...] = jnp.zeros_like(ctx_ref)
        lse_ref[...] = jnp.zeros_like(lse_ref)


def attend_late_kernel(scale, info, qkv_ref, ctx_ref, lse_ref):
    attend_kernel(scale, 1, info, qkv_ref, None, ctx_ref, lse_ref)


def attend_back_kernel(
    scale, info, qkv_ref, kvh_ref, dctx_ref, lse_ref, tab_ref, tabh_ref, md_ref, mdh_ref
):
    clip = pl.program_id(0)
    rows, width = dctx_ref.shape
    live = info[3] < info[LEN0 + clip]

    @pl.when(jnp.logical_not(live))
    def _():
        md_ref[...] = jnp.zeros_like(md_ref)
        mdh_ref[...] = jnp.zeros_like(mdh_ref)

    @pl.when(live)
    def _():
        biases = [window_bias(info, clip, block) for block in range(2)]

        def place(item):
            pair, block = divmod(item, 2)
            return pair, block, pair * TILE, slice(block * TILE, (block + 1) * TILE)

        def score(item):
            pair, block, at, at_rows = place(item)
            queries = two_heads(qkv_ref[at_rows, at : at + TILE] * BF(scale))
            delta = two_heads(dctx_ref[at_rows, at : at + TILE])
            keys = key_window(kvh_ref, qkv_ref, block, at, width + at)
            values = key_window(kvh_ref, qkv_ref, block, width + at, 2 * width + at)
            return mm_t(keys, queries), mm_t(values, delta)

        def weigh(item, scores):
            pair, block, at, at_rows = place(item)
            products, weight_delta = scores
            weights = jnp.exp(products + biases[block] - lse_ref[block, pair : pair + 1, :])
            inner = jnp.sum(weight_delta * weights, axis=0, keepdims=True)
            return weights.astype(BF), (weights * (weight_delta - inner)).astype(BF)

        def gather(item, weighed):
            pair, block, at, at_rows = place(item)
            weights, score_delta = weighed
            queries = two_heads(qkv_ref[at_rows, at : at + TILE] * BF(scale))
            delta = two_heads(dctx_ref[at_rows, at : at + TILE])
            keys = key_window(kvh_ref, qkv_ref, block, at, width + at)
            return t_mm(keys, score_delta), mm(score_delta, queries), mm(weights, delta)

        before = {}
        early, late = slice(0, TILE), slice(TILE, 2 * TILE)

        def put_key(where, at, delta):
            md_ref[where, width + at : width + at + TILE] = turn(
                delta, tab_ref[0, where], -tab_ref[1, where], -tab_ref[2, where]
            ).astype(BF)

        def put(item, deltas):
            pair, block, at, at_rows = place(item)
            turned, key_delta, value_delta = deltas
            md_ref[at_rows, at : at + TILE] = turn(
                one_row(turned) * scale,
                tab_ref[0, at_rows], -tab_ref[1, at_rows], -tab_ref[2, at_rows],
            ).astype(BF)
            value_at = slice(2 * width + at, 2 * width + at + TILE)
            if block == 0:
                mdh_ref[:, at : at + TILE] = turn(
                    key_delta[early], tabh_ref[0], -tabh_ref[1], -tabh_ref[2]
                ).astype(BF)
                mdh_ref[:, width + at : width + at + TILE] = value_delta[early].astype(BF)
                before[pair] = key_delta[late], value_delta[late]
            else:
                key_before, value_before = before.pop(pair)
                put_key(early, at, key_before + key_delta[early])
                put_key(late, at, key_delta[late])
                md_ref[early, value_at] = (value_before + value_delta[early]).astype(BF)
                md_ref[late, value_at] = value_delta[late].astype(BF)

        staged(2 * (width // TILE), score, weigh, gather, put)


def out_kernel(parts, info, ctx_ref, x_ref, w_ref, gb_ref, att_ref, n_ref):
    r = pl.program_id(0)
    rows = x_ref.shape[0] // parts
    places = [info[LEN0 + r * parts + p] for p in range(parts)]
    live = functools.reduce(jnp.logical_or, [info[3] < place for place in places])

    def at(p):
        return slice(p * rows, (p + 1) * rows)

    @pl.when(live)
    def _():
        def product(p):
            return mm(ctx_ref[at(p), :], w_ref[...])

        def put(p, attended):
            att_ref[at(p), :] = attended
            middle = x_ref[at(p), :].astype(F32) + gb_ref[2:3, :] * attended
            normal, _ = norm_stats(middle)
            n_ref[at(p), :] = (normal * gb_ref[1:2, :] + gb_ref[5:6, :]).astype(BF)

        staged(parts, product, put)

    @pl.when(jnp.logical_not(live))
    def _():
        att_ref[...] = jnp.zeros_like(att_ref)
        n_ref[...] = jnp.zeros_like(n_ref)


def row_valid(info, clip, rows):
    place = info[3] + lax.broadcasted_iota(jnp.int32, (rows, 1), 0)
    return (place < info[LEN0 + clip]).astype(F32)


def output_kernel(info, x_ref, att_ref, ba_ref, bb_ref, gb_ref, out_ref):
    r = pl.program_id(0)
    valid = row_valid(info, r, x_ref.shape[0])
    branch = ba_ref[...].astype(F32) + bb_ref[...].astype(F32)
    middle = x_ref[...].astype(F32) + gb_ref[2:3, :] * att_ref[...]
    out_ref[...] = ((middle + gb_ref[3:4, :] * branch) * valid).astype(BF)


def out_back_kernel(
    info, sa_ref, sb_ref, att_ref, x_ref, ct_ref, ctx_ref, w_ref, gb_ref,
    delta_ref, dctx_ref, out_ref, sum_ref, acc,
):
    r = pl.program_id(0)
    rows, width = x_ref.shape

    @pl.when(r == 0)
    def _():
        sum_ref[...] = jnp.zeros_like(sum_ref)
        acc[...] = jnp.zeros_like(acc)

    live = info[3] < info[LEN0 + r]

    @pl.when(live)
    def _():
        valid = row_valid(info, r, rows)
        attended = att_ref[...]
        middle = x_ref[...].astype(F32) + gb_ref[2:3, :] * attended
        normal, inverse = norm_stats(middle)
        second = sa_ref[...].astype(F32) + sb_ref[...].astype(F32)
        back = norm_back(second, normal, inverse, gb_ref[1:2, :])
        output_delta = ct_ref[...].astype(F32) * valid
        middle_delta = output_delta + back
        delta_ref[...] = middle_delta
        attended_delta = (middle_delta * gb_ref[2:3, :]).astype(BF)
        dctx_ref[...] = mm_t(attended_delta, w_ref[...]).astype(BF)
        acc[...] += t_mm(ctx_ref[...], attended_delta)
        sum_ref[0:1, :] += column_sum(second * normal)
        sum_ref[1:2, :] += column_sum(middle_delta * attended)
        sum_ref[2:3, :] += column_sum(second)

    @pl.when(jnp.logical_not(live))
    def _():
        delta_ref[...] = jnp.zeros_like(delta_ref)
        dctx_ref[...] = jnp.zeros_like(dctx_ref)

    @pl.when(r == pl.num_programs(0) - 1)
    def _():
        out_ref[...] = acc[...].astype(BF)


def qkv_grad_kernel(info, n_ref, md_ref, nh_ref, mdh_ref, *refs):
    t = pl.program_id(0)
    acc = refs[4]
    acc[...] = t_mm(n_ref[...], md_ref[...])

    @pl.when(jnp.logical_and(info[0] > 0, t >= 2))
    def _():
        acc[...] += t_mm(nh_ref[...], mdh_ref[...])

    def put(left):
        for y in range(2):
            for z in range(4):
                z_there = (info[4] // 2 + z // 2) % 2 * 2 + (info[4] + z) % 2
                base = z_there * 256 + ((info[1] + y) % 2) * 128
                for c in range(2):
                    row = pl.multiple_of(base + ((info[2] + c) % 2) * 64, 64)
                    value = acc[pl.ds(row, 64), :].astype(BF)
                    if left:
                        refs[2 * c][0, y, z] = value
                    else:
                        refs[2 * c + 1][y, 0, 0, z] = value

    pl.when(t % 3 == 0)(functools.partial(put, True))
    pl.when(t % 3 > 0)(functools.partial(put, False))


def first_back_kernel(parts, info, md_ref, w_ref, x_ref, delta_ref, gb_ref, out_ref, sum_ref):
    r = pl.program_id(0)
    rows = x_ref.shape[0] // parts

    @pl.when(r == 0)
    def _():
        sum_ref[...] = jnp.zeros_like(sum_ref)

    places = [info[LEN0 + r * parts + p] for p in range(parts)]
    live = functools.reduce(jnp.logical_or, [info[3] < place for place in places])

    def at(p):
        return slice(p * rows, (p + 1) * rows)

    @pl.when(live)
    def _():
        def product(p):
            return mm_t(md_ref[at(p), :], w_ref[...])

        def put(p, first):
            normal, inverse = norm_stats(x_ref[at(p), :].astype(F32))
            out_ref[at(p), :] = delta_ref[at(p), :] + norm_back(
                first, normal, inverse, gb_ref[0:1, :]
            )
            sum_ref[0:1, :] += column_sum(first * normal)
            sum_ref[1:2, :] += column_sum(first)

        staged(parts, product, put)

    @pl.when(jnp.logical_not(live))
    def _():
        out_ref[...] = jnp.zeros_like(out_ref)


def first_halo_kernel(info, mdh_ref, wk_ref, wv_ref, x_ref, out_ref, sum_ref):
    width = x_ref.shape[1]
    live = info[0] > 0
    sum_ref[...] = jnp.zeros_like(sum_ref)

    @pl.when(live)
    def _():
        first = mm_t(mdh_ref[:, :width], wk_ref[...]) + mm_t(mdh_ref[:, width:], wv_ref[...])
        out_ref[...] = first.astype(BF)
        normal, _ = norm_stats(x_ref[...].astype(F32))
        sum_ref[0:1, :] = column_sum(first * normal)
        sum_ref[1:2, :] = column_sum(first)

    @pl.when(jnp.logical_not(live))
    def _():
        out_ref[...] = jnp.zeros_like(out_ref)


def input_grad_kernel(info, part_ref, halo_ref, x_ref, gb_ref, out_ref):
    rows = part_ref.shape[0]
    split = rows - halo_ref.shape[0]
    out_ref[:split, :] = part_ref[:split, :].astype(BF)

    @pl.when(info[0] == 0)
    def _():
        normal, inverse = norm_stats(x_ref[split:, :].astype(F32))
        back = norm_back(halo_ref[...].astype(F32), normal, inverse, gb_ref[0:1, :])
        out_ref[split:, :] = (part_ref[split:, :] + back).astype(BF)

    @pl.when(info[0] > 0)
    def _():
        out_ref[split:, :] = part_ref[split:, :].astype(BF)


def hidden_block(info, c, k):
    z0, x, q = k // 4, k // 2 % 2, k % 2
    d = ((info[0] + x) % 2 * 2 + z0) * 4 + (info[1] + q) % 2 * 2 + info[2]
    return pl.ds(pl.multiple_of(d * 256 + c * TILE, TILE), TILE)


def ffn_kernel(c, first, half, info, n_own, n_other, b_own, b_other, *rest):
    if not first:
        earlier, rest = rest[:2], rest[2:]
    wg_hbm, wu_hbm, wd_hbm, hidden_ref, *rest = rest
    sums, rest = rest[:2], rest[2:]
    packs, rest = (rest[0:2], rest[2:4]), rest[4:]
    wg, wu, wd, ag, au, ad, n_buf, b_buf, sems, row_sems = rest
    r = pl.program_id(0)
    steps = pl.num_programs(0)
    block_rows = n_buf.shape[1]

    def weight_copies(kind):
        hbm, vmem = ((wg_hbm, wg), (wu_hbm, wu), (wd_hbm, wd))[kind]
        for k in range(8):
            src, dst = hidden_block(info, c, k), pl.ds(k * TILE, TILE)
            if kind < 2:
                yield pltpu.make_async_copy(hbm.at[:, src], vmem.at[:, dst], sems.at[kind, k])
            else:
                yield pltpu.make_async_copy(hbm.at[src, :], vmem.at[dst, :], sems.at[kind, k])

    def row_copies(step, sources):
        src = pl.ds(pl.multiple_of(step % half * block_rows, block_rows), block_rows)
        for i, (hbm, vmem) in enumerate(zip(sources, (n_buf, b_buf))):
            yield pltpu.make_async_copy(
                hbm.at[src, :], vmem.at[step % 2], row_sems.at[i, step % 2]
            )

    def start_rows(step):
        @pl.when(step < half)
        def _():
            for copy in row_copies(step, (n_own, b_own)):
                copy.start()

        @pl.when(step >= half)
        def _():
            for copy in row_copies(step, (n_other, b_other)):
                copy.start()

    @pl.when(r == 0)
    def _():
        start_rows(r)
        for kind in range(3):
            for copy in weight_copies(kind):
                copy.start()
        for acc in (ag, au, ad):
            acc[...] = jnp.zeros_like(acc)

    @pl.when(r + 1 < steps)
    def _():
        start_rows(r + 1)

    for copy in row_copies(r, (n_own, b_own)):
        copy.wait()

    @pl.when(r == 0)
    def _():
        for kind in range(3):
            for copy in weight_copies(kind):
                copy.wait()

    normed, delta = n_buf.at[r % 2], b_buf.at[r % 2]
    gate = mm(normed[...], wg[...])
    upward = mm(normed[...], wu[...])
    hidden_delta = mm_t(delta[...], wd[...])
    sigmoid = jax.nn.sigmoid(gate)
    active = gate * sigmoid
    hidden = (active * upward).astype(BF)
    up_delta = (hidden_delta * active).astype(BF)
    gate_delta = (hidden_delta * upward * (sigmoid + active * (1.0 - sigmoid))).astype(BF)
    hidden_ref[...] = hidden
    second = mm_t(gate_delta, wg[...]) + mm_t(up_delta, wu[...])
    if not first:
        second = second + jnp.where(r < half, earlier[0][...], earlier[1][...]).astype(F32)
    second = second.astype(BF)
    sums[0][...] = second
    sums[1][...] = second
    ag[...] += t_mm(normed[...], gate_delta)
    au[...] += t_mm(normed[...], up_delta)
    ad[...] += t_mm(delta[...], hidden)

    @pl.when(r == pl.num_programs(0) - 1)
    def _():
        def flip(bit, own):
            return (bit + own) % 2

        def tile(acc, row, col):
            row = pl.multiple_of(row * TILE, TILE)
            col = pl.multiple_of(col * TILE, TILE)
            return acc[pl.ds(row, TILE), pl.ds(col, TILE)].astype(BF)

        x_own, y_own, z1_own, z0_own = info[0], info[1], info[4] // 2, info[4] % 2
        for u in range(2):
            for x in range(2):
                for y in range(2):
                    lead, other = (x, y) if u == 0 else (y, x)
                    ref = packs[u][lead]

                    def put(at, value):
                        ref[other, at * TILE : (at + 1) * TILE, :] = value

                    for z0 in range(2):
                        for z1 in range(2):
                            z1_at, z0_at = flip(z1, z1_own), flip(z0, z0_own)
                            at = 12 * z0 + 6 * z1
                            row = (z1_at * 2 + z0_at) * 2 + flip(y, y_own)
                            for i, acc in enumerate((ag, au)):
                                for q in range(2):
                                    col = u * 4 + x * 2 + flip(q, y_own)
                                    put(at + 2 * i + q, tile(acc, row, col))
                            col = z0_at * 4 + flip(z1_at, x_own) * 2 + y
                            for dq in range(2):
                                row = flip(x, x_own) * 4 + 2 * u + dq
                                put(at + 4 + dq, tile(ad, row, col))


def ffn_call(c, info, pieces, weights, previous, after=(), block_rows=256):
    rows, width = pieces[0].shape
    half = rows // block_rows
    first = previous is None
    hidden = 8 * TILE
    own = pl.BlockSpec((block_rows, width), lambda r, info: (jnp.minimum(r, half), 0))
    other = pl.BlockSpec((block_rows, width), lambda r, info: (jnp.maximum(r - half, 0), 0))
    every = pl.BlockSpec((block_rows, hidden), lambda r, info: (r, 0))
    packed = (2, 24 * TILE, TILE)
    pack = pl.BlockSpec(packed, lambda r, info: (0, 0, 0), pipeline_mode=pl.Buffered(1))
    extra = [] if first else list(previous)
    anywhere = pl.BlockSpec(memory_space=pl.ANY)
    return call_kernel(
        functools.partial(ffn_kernel, c, first, half),
        info,
        [*pieces, *extra, *weights],
        name="feed_forward",
        grid=(2 * half,),
        ins=[anywhere] * 4 + [own, other] * (len(extra) // 2) + [anywhere] * 3,
        outs=[every, own, other] + [pack] * 4,
        shapes=[
            shape_of((2 * rows, hidden)), shape_of((rows + block_rows, width)), shape_of((rows, width))
        ] + [shape_of(packed)] * 4,
        scratch=[
            pltpu.VMEM((width, hidden), BF),
            pltpu.VMEM((width, hidden), BF),
            pltpu.VMEM((hidden, width), BF),
            pltpu.VMEM((width, hidden), F32),
            pltpu.VMEM((width, hidden), F32),
            pltpu.VMEM((width, hidden), F32),
            pltpu.VMEM((2, block_rows, width), BF),
            pltpu.VMEM((2, block_rows, width), BF),
            pltpu.SemaphoreType.DMA((3, 8)),
            pltpu.SemaphoreType.DMA((2, 2)),
        ],
        vmem=60,
        cost=(18 * 2 * rows * width * hidden, 30 * MIB),
        after=after,
    )


def branch_kernel(half, info, ha, hb, b_own, b_other, wd_hbm, own_ref, other_ref, sum_ref, wd, sems):
    r = pl.program_id(0)

    def copies():
        for c in range(2):
            for k in range(8):
                dst = wd.at[c, pl.ds(k * TILE, TILE), :]
                yield pltpu.make_async_copy(wd_hbm.at[hidden_block(info, c, k), :], dst, sems.at[c, k])

    @pl.when(r == 0)
    def _():
        for copy in copies():
            copy.start()
        sum_ref[...] = jnp.zeros_like(sum_ref)
        for copy in copies():
            copy.wait()

    branch = mm(ha[...], wd[0]) + mm(hb[...], wd[1])
    delta = jnp.where(r < half, b_own[...], b_other[...]).astype(F32)
    sum_ref[0:1, :] += column_sum(delta * branch)
    branch = branch.astype(BF)
    own_ref[...] = branch
    other_ref[...] = branch


def branch_call(info, hiddens, deltas, down_weight, after, block_rows=512):
    rows, width = deltas[0].shape
    half = rows // block_rows
    hidden = hiddens[0].shape[1]
    every = pl.BlockSpec((block_rows, hidden), lambda r, info: (r, 0))
    own = pl.BlockSpec((block_rows, width), lambda r, info: (jnp.minimum(r, half), 0))
    own_in = pl.BlockSpec((block_rows, width), lambda r, info: (jnp.minimum(r, half - 1), 0))
    other = pl.BlockSpec((block_rows, width), lambda r, info: (jnp.maximum(r - half, 0), 0))
    return call_kernel(
        functools.partial(branch_kernel, half), info, [*hiddens, *deltas, down_weight],
        name="branch", vmem=40, grid=(2 * half,),
        ins=[every, every, own_in, other, pl.BlockSpec(memory_space=pl.ANY)],
        outs=[own, other, whole_spec((8, width))],
        shapes=[
            shape_of((rows + block_rows, width)), shape_of((rows, width)), shape_of((8, width), F32)
        ],
        scratch=[pltpu.VMEM((2, hidden, width), BF), pltpu.SemaphoreType.DMA((2, 8))],
        cost=(4 * 2 * rows * width * hidden, 16 * MIB), after=after,
    )


SWAP = [(0, 1), (1, 0)]
Z_NEAR = [(0, 1), (1, 0), (2, 3), (3, 2)]
Z_FAR = [(0, 2), (2, 0), (1, 3), (3, 1)]


def meet(*values):
    return lax.optimization_barrier(values)


def later(values, *needed):
    return lax.optimization_barrier((values, needed))[0]


def swap(values, axis):
    return lax.ppermute(values, axis, SWAP)


def plus(left, right):
    return (left.astype(F32) + right.astype(F32)).astype(BF)


def fold(keep, send, axis):
    return plus(keep, swap(send, axis))


def fold_two(keep, send, lead, other):
    total = fold(keep, send, lead)
    return fold(total[0], total[1], other)


def scatter_z(values):
    return lax.psum_scatter(values, "z", scatter_dimension=0, tiled=True)[0]


def turn_table(first, last, head_dim):
    pairs = head_dim // 2
    rates = np.exp(np.arange(pairs, dtype=np.float32) * np.float32(-2.0 * math.log(10000.0) / head_dim))
    angles = np.arange(first, last, dtype=np.float32)[:, None] * rates[None, :].astype(np.float32)
    cosine, sine = (np.tile(t(angles), (1, TILE // pairs)) for t in (np.cos, np.sin))
    front = (np.arange(TILE) % head_dim < pairs)[None, :]
    return np.stack([cosine, np.where(front, -sine, 0), np.where(front, 0, sine)]).astype(np.float32)


def fast_body(
    frames, cotangent, lengths, qkv_weight, out_weight, gate_weight, up_weight, down_weight,
    gain_table, bias_table,
):
    clips, rows, width = frames.shape
    count = clips * rows
    head_dim = width // HEADS
    scale = 1.0 / math.sqrt(head_dim)
    x_at, y_at, core_at, z_at = (lax.axis_index(a) for a in ("seq", "y", "core", "z"))
    start = x_at * rows
    info = jnp.concatenate(
        [jnp.stack([x_at, y_at, core_at, start, z_at]).astype(jnp.int32), lengths.astype(jnp.int32)]
    )
    flat = frames.reshape(count, width)
    tangent = cotangent.reshape(count, width)
    halo = lax.ppermute(
        frames[:, rows - TILE :].reshape(clips * TILE, width), "seq", [(0, 1)]
    )
    places = start + jnp.arange(rows)
    valid = (places[None, :] < lengths[:, None]).astype(F32).reshape(count, 1)
    branch_delta = (tangent.astype(F32) * valid * gain_table[:, 3]).astype(BF)
    table = jnp.concatenate([gain_table, bias_table, jnp.zeros((width, 2), F32)], axis=1).T
    seats = lax.axis_size("seq")
    own_turns = jnp.asarray(turn_table(0, seats * rows, head_dim))
    halo_turns = jnp.asarray(
        np.concatenate([turn_table(i * rows - TILE, i * rows, head_dim) for i in range(seats)], axis=1)
    )
    own_tab = pl.BlockSpec((3, rows, TILE), lambda r, info: (0, info[0], 0))
    halo_tab = pl.BlockSpec((3, TILE, TILE), lambda r, info: (0, info[0], 0))
    gb = whole_spec(table.shape)
    own = rows_spec(rows, width)
    halo_rows = rows_spec(TILE, width)
    qkv_rows = rows_spec(rows, 3 * width)
    kv_rows = rows_spec(TILE, 2 * width)
    w_qkv = whole_spec((width, 3 * width))
    w_key = pl.BlockSpec((width, width), lambda r, info: (0, 1))
    w_value = pl.BlockSpec((width, width), lambda r, info: (0, 2))
    w_out = whole_spec((width, width))
    sums = whole_spec((8, width))

    grid = (clips,)
    mac = 2 * count * width * width

    def two_rows(width):
        return rows_spec(count // 2, width)

    qkv, normed_one = call_kernel(
        qkv_kernel, info, [flat, qkv_weight, table, own_turns], name="qkv", vmem=36, grid=(2,),
        ins=[two_rows(width), w_qkv, gb, own_tab], outs=[two_rows(3 * width), two_rows(width)],
        shapes=[shape_of((count, 3 * width)), shape_of((count, width))], cost=(3 * mac, 16 * MIB),
    )
    def half_rows(width, part):
        return pl.BlockSpec((TILE, width), lambda r, info: (2 * r + part, 0))

    totals_of = (2 * clips, width // TILE, 2 * TILE)
    seen = [shape_of((count, width)), shape_of(totals_of, F32)]

    def half_totals(part):
        return pl.BlockSpec((1, *totals_of[1:]), lambda r, info: (2 * r + part, 0, 0))

    late = call_kernel(
        functools.partial(attend_late_kernel, scale), info, [qkv], name="attend_late", vmem=16, grid=grid,
        ins=[qkv_rows], outs=[half_rows(width, 1), half_totals(1)], shapes=seen,
        cost=(2 * mac, 8 * MIB),
    )
    halo, branch_delta = lax.optimization_barrier((halo, branch_delta))
    branch_delta_other = swap(branch_delta, "core")
    kv_halo, normed_halo = call_kernel(
        halo_kernel, info, [halo, qkv_weight, qkv_weight, table, halo_turns], name="halo", vmem=24,
        grid=(1,), ins=[rows_spec(clips * TILE, width), w_key, w_value, gb, halo_tab],
        outs=[rows_spec(clips * TILE, 2 * width), rows_spec(clips * TILE, width)],
        shapes=[shape_of((clips * TILE, 2 * width)), shape_of((clips * TILE, width))],
        cost=(mac, 8 * MIB), after=late,
    )
    context, log_totals = call_kernel(
        functools.partial(attend_kernel, scale, 0), info, [qkv, kv_halo], name="attend_early", vmem=16,
        grid=grid, ins=[half_rows(3 * width, 0), kv_rows],
        outs=[half_rows(width, 0), half_totals(0)], shapes=seen,
        cost=(2 * mac, 12 * MIB), onto=late,
    )
    attended, normed_two = call_kernel(
        functools.partial(out_kernel, clips // 2), info, [context, flat, out_weight, table],
        name="project", vmem=24, grid=(2,), ins=[two_rows(width)] * 2 + [w_out, gb], outs=[two_rows(width)] * 2,
        shapes=[shape_of((count, width), F32), shape_of((count, width))], cost=(mac, 12 * MIB),
    )
    normed_two_other = swap(normed_two, "core")

    pieces = (normed_two, normed_two_other, branch_delta, branch_delta_other)
    weights = (gate_weight, up_weight, down_weight)
    def start_pair(keeps):
        (keep_a, send_a), (keep_b, send_b) = keeps
        return (keep_a, swap(send_a, "seq")), (keep_b, swap(send_b, "y"))

    def second_pair(totals):
        (stay_a, go_a), (stay_b, go_b) = totals
        return (stay_a, swap(go_a, "y")), (stay_b, swap(go_b, "seq"))

    def halves(pairs):
        return [tuple(plus(keep[k], came[k]) for k in range(2)) for keep, came in pairs]

    def near_parts(pairs):
        return [
            jnp.stack([plus(*(v.reshape(-1, 2, 12, TILE, TILE)[:, k] for v in pair)) for pair in pairs])
            for k in range(2)
        ]

    def to_near(values):
        return lax.ppermute(values, "z", Z_NEAR)

    def far_pair(*pair):
        total = plus(*pair).reshape(2, -1, 2, 6, TILE, TILE)
        return total[:, :, 0], lax.ppermute(total[:, :, 1], "z", Z_FAR)

    def run_ffn(c, previous, after):
        *state, keep_a, send_a, keep_b, send_b = ffn_call(
            c, info, pieces, weights, previous, after
        )
        return state, ((keep_a, send_a), (keep_b, send_b))

    (hidden_0, *previous), grads_0 = run_ffn(0, None, ())
    moved_0 = start_pair(grads_0)
    (hidden_1, second, second_sent), grads_1 = run_ffn(1, previous, ())
    second, second_sent, grads_1, moved_0 = meet(second, second_sent, grads_1, moved_0)
    second_other = swap(second_sent, "core")
    near_keep_0, near_send_0 = near_parts(moved_0)
    second_other, near_send_0, grads_1 = meet(second_other, near_send_0, grads_1)
    near_came_0 = to_near(near_send_0)
    moved_1 = start_pair(grads_1)

    middle_delta, context_delta, out_grad, sums_two = call_kernel(
        out_back_kernel, info,
        [second, second_other, attended, flat, tangent, context, out_weight, table],
        name="project_back", vmem=32, grid=grid,
        ins=[own, own, own, own, own, own, w_out, gb],
        outs=[own, own, w_out, sums],
        shapes=[
            shape_of((count, width), F32), shape_of((count, width)), shape_of((width, width)),
            shape_of((8, width), F32),
        ],
        scratch=[pltpu.VMEM((width, width), F32)], cost=(2 * mac, 24 * MIB), after=(near_keep_0,),
    )
    out_grad = lax.psum_scatter(out_grad, ("z", "y", "core"), scatter_dimension=0, tiled=True)

    mixed_delta, mixed_halo = call_kernel(
        functools.partial(attend_back_kernel, scale), info,
        [qkv, kv_halo, context_delta, log_totals, own_turns, halo_turns], name="attend_back",
        vmem=24, grid=grid,
        ins=[
            qkv_rows, kv_rows, own, pl.BlockSpec((2, *totals_of[1:]), lambda r, info: (r, 0, 0)),
            own_tab, halo_tab,
        ],
        outs=[qkv_rows, kv_rows],
        shapes=[shape_of((count, 3 * width)), shape_of((clips * TILE, 2 * width))],
        cost=(10 * mac, 24 * MIB),
    )
    mixed_delta, mixed_halo, moved_1, near_came_0 = meet(
        mixed_delta, mixed_halo, moved_1, near_came_0
    )
    totals_1 = halves(moved_1)
    moved_1 = second_pair(totals_1)
    far_0 = far_pair(near_keep_0, near_came_0)
    all_halo = rows_spec(clips * TILE, width)
    halo_back, sums_halo = call_kernel(
        first_halo_kernel, info, [mixed_halo, qkv_weight, qkv_weight, halo], name="first_halo",
        vmem=24, grid=(1,),
        ins=[rows_spec(clips * TILE, 2 * width), w_key, w_value, all_halo], outs=[all_halo, sums],
        shapes=[shape_of((clips * TILE, width)), shape_of((8, width), F32)],
        cost=(mac, 6 * MIB), after=(*(t for pair in totals_1 for t in pair), far_0[0]),
    )

    cut = 3 * width // 6
    def x_seat(t, info):
        return (t // 3 + info[0]) % 2

    left_spec = pl.BlockSpec((1, 2, 4, 64, cut), lambda t, info: (x_seat(t, info), 0, 0, 0, 0))
    right_spec = pl.BlockSpec(
        (2, 1, 1, 4, 64, cut),
        lambda t, info: (0, x_seat(t, info), jnp.maximum(t % 3 - 1, 0), 0, 0, 0),
    )
    packed = [shape_of((2, 2, 4, 64, cut)), shape_of((2, 2, 2, 4, 64, cut))]
    keep_l, keep_r, send_l, send_r = call_kernel(
        qkv_grad_kernel, info, [normed_one, mixed_delta, normed_halo, mixed_halo],
        name="qkv_grad", vmem=32, grid=(6,),
        ins=[
            whole_spec((count, width)),
            pl.BlockSpec((count, cut), lambda t, info: (0, t)),
            whole_spec((clips * TILE, width)),
            pl.BlockSpec((clips * TILE, cut), lambda t, info: (0, jnp.maximum(t - 2, 0))),
        ],
        outs=[left_spec, right_spec] * 2, shapes=packed * 2,
        scratch=[pltpu.VMEM((width, cut), F32)], cost=(4 * mac, 16 * MIB),
        after=(halo_back,),
    )
    moved_1, keep_l, keep_r, send_l, send_r = meet(moved_1, keep_l, keep_r, send_l, send_r)
    came_l, came_r = swap(send_l, "core"), swap(send_r, "core")
    near_keep_1, near_send_1 = near_parts(moved_1)
    came_l, came_r, near_send_1, halo_back = meet(came_l, came_r, near_send_1, halo_back)
    stay_l, go_l = (plus(keep_l[k], came_l[k]) for k in range(2))
    stay_r, go_r = (plus(keep_r[k], came_r[k]) for k in range(2))
    go_l, go_r = swap(go_l, "seq"), swap(go_r, "y")
    halo_came = lax.ppermute(halo_back, "seq", [(1, 0)])
    near_came_1 = to_near(near_send_1)
    branch, branch_sent, sums_branch = branch_call(
        info, (hidden_0, hidden_1), (branch_delta, branch_delta_other), down_weight,
        (stay_l, stay_r, near_keep_1),
    )
    part_grad, sums_one = call_kernel(
        functools.partial(first_back_kernel, clips // 2), info,
        [mixed_delta, qkv_weight, flat, middle_delta, table], name="first_back", vmem=44,
        grid=(2,), ins=[two_rows(3 * width), w_qkv, two_rows(width), two_rows(width), gb],
        outs=[two_rows(width), sums],
        shapes=[shape_of((count, width), F32), shape_of((8, width), F32)],
        cost=(3 * mac, 24 * MIB), after=(sums_branch,),
    )
    go_l, go_r, near_came_1, halo_came, far_0, part_grad, sums_one, branch_sent = meet(
        go_l, go_r, near_came_1, halo_came, far_0, part_grad, sums_one, branch_sent
    )
    share = width // 16
    ones = sums_one + sums_halo
    nought = jnp.zeros((width,), F32)
    scale_mlp = sums_branch[0] / gain_table[:, 3]
    vectors = jnp.stack(
        [ones[0], sums_two[0], ones[1], nought, sums_two[1], scale_mlp, sums_two[2], nought]
    )
    left, right = plus(stay_l, go_l), plus(stay_r, go_r)
    go_l, go_r = swap(left[1], "y"), swap(right[1], "seq")
    far_1 = far_pair(near_keep_1, near_came_1)
    branch_other = swap(branch_sent, "core")
    vectors_core = swap(vectors, "core")
    input_grad = call_kernel(
        input_grad_kernel, info, [part_grad, halo_came, flat, table], name="input_grad", vmem=16,
        grid=grid, ins=[own, halo_rows, own, gb], outs=own, shapes=shape_of((count, width)),
        cost=(0, 8 * MIB), after=(left, right, far_1[0], vectors),
    )
    go_l, go_r, branch_other, vectors_core, input_grad = meet(
        go_l, go_r, branch_other, vectors_core, input_grad
    )
    left, right = plus(left[0], go_l), plus(right[0], go_r)
    qkv_total = jnp.concatenate([left[None], right]).reshape(3, 2, 2, 64, cut)
    go = to_near(qkv_total[:, :, 1])
    first_tiles = plus(*far_0)
    late_a, late_b = swap(first_tiles[0, 1], "y"), swap(first_tiles[1, 1], "seq")
    vectors = vectors + vectors_core
    vectors_x = swap(vectors, "seq")
    output = call_kernel(
        output_kernel, info, [flat, attended, branch, branch_other, table],
        name="output", vmem=16, grid=grid, ins=[own, own, own, own, gb], outs=own,
        shapes=shape_of((count, width)), cost=(0, 14 * MIB),
        after=(qkv_total, first_tiles, vectors),
    )
    go, far_1, late_a, late_b, vectors_x, output = meet(
        go, far_1, late_a, late_b, vectors_x, output
    )
    vectors = vectors + vectors_x
    vectors = vectors + swap(vectors, "y")
    vectors = vectors + lax.ppermute(vectors, "z", Z_NEAR)
    vectors = vectors + lax.ppermute(vectors, "z", Z_FAR)
    qkv_total = plus(qkv_total[:, :, 0], go)
    qkv_total = plus(qkv_total[:, 0], lax.ppermute(qkv_total[:, 1], "z", Z_FAR))
    qkv_grad = qkv_total.transpose(1, 0, 2).reshape(-1, 3 * cut).astype(F32)
    out_halves = later(out_grad, qkv_total).reshape(-1, 2, width // 2)
    out_kept = lax.dynamic_index_in_dim(out_halves, x_at, axis=1, keepdims=False)
    out_sent = lax.dynamic_index_in_dim(out_halves, 1 - x_at, axis=1, keepdims=False)
    out_grad = out_kept.astype(F32) + swap(out_sent, "seq").astype(F32)

    vectors = vectors.reshape(2, 4, 16, share).transpose(2, 0, 1, 3).reshape(32, 4, share)
    seat = ((z_at * 2 + y_at) * 2 + core_at) * 2 + x_at
    vectors = lax.dynamic_index_in_dim(vectors, seat, keepdims=False).T
    gain_grad, bias_grad = vectors[:, :2], vectors[:, 2:3]

    first_tiles = [plus(first_tiles[k, 0], came) for k, came in enumerate((late_a, late_b))]
    tiles = jnp.stack([jnp.stack(first_tiles), plus(*far_1)[:, 0]])
    gates = tiles[:, :, :4].reshape(2, 2, 2, 2, 2, share, TILE)
    kept = lax.dynamic_index_in_dim(gates, core_at, axis=4, keepdims=False)
    sent = lax.dynamic_index_in_dim(gates, 1 - core_at, axis=4, keepdims=False)
    came = swap(sent, "core")
    both = jnp.where(core_at == 0, jnp.stack([kept, came], 4), jnp.stack([came, kept], 4))
    both = both.transpose(2, 5, 1, 3, 4, 0, 6).astype(F32)
    gate_grad = both[0].reshape(share, -1)
    up_grad = both[1].reshape(share, -1)
    down_grad = tiles[:, :, 4:].reshape(2, width // 2, TILE).transpose(0, 2, 1).astype(F32)
    down_grad = down_grad.reshape(2 * TILE, width // 2)
    shape = (clips, rows, width)
    return (
        output.reshape(shape), input_grad.reshape(shape), qkv_grad, out_grad, gate_grad, up_grad,
        down_grad, gain_grad, bias_grad,
    )


def solution(mesh):
    placed = (("dp", "seq", None),) * 2 + (("dp",),) + ((),) * 7
    given = (("dp", "seq", None),) * 2 + (("dp", "seq"),) * 7
    fast = mesh.shape["dp"] == 16 and mesh.shape["seq"] == 2
    dp_axes = ("z", "y", "core") if fast else "dp"

    def specs(entries):
        return tuple(P(*(dp_axes if a == "dp" else a for a in entry)) for entry in entries)

    if fast:
        mesh = Mesh(mesh.devices.reshape(4, 2, 2, 2), ("z", "y", "core", "seq"))
    return jax.shard_map(
        fast_body if fast else body,
        mesh=mesh,
        in_specs=specs(placed),
        out_specs=specs(given),
        check_vma=False,
    )
```

```python
import functools
import math

import jax
import jax.numpy as jnp
import numpy as np
from jax import lax
from jax.experimental import pallas as pl
from jax.experimental.pallas import tpu as pltpu
from jax.sharding import Mesh
from jax.sharding import PartitionSpec as P

HEADS = 16
WINDOW = 128


NORM_EPS = 1e-05
MASKED = -1e30


def norm_forward(values, gain_col, shift_col):
    row_mean = jnp.mean(values, axis=-1, keepdims=True)
    centred = values - row_mean
    inverse = lax.rsqrt(jnp.mean(centred * centred, axis=-1, keepdims=True) + NORM_EPS)
    normal = centred * inverse
    return (normal * gain_col + shift_col, normal, inverse)


def norm_backward(upstream, normal, inverse, gain_col):
    scaled = upstream * gain_col
    inner_term = (
        scaled
        - jnp.mean(scaled, axis=-1, keepdims=True)
        - normal * jnp.mean(scaled * normal, axis=-1, keepdims=True)
    )
    return (inverse * inner_term, jnp.sum(upstream * normal, axis=0), jnp.sum(upstream, axis=0))


def rotary_tables(places, head_dim):
    pair_count = head_dim // 2
    freq_rates = jnp.exp(
        jnp.arange(pair_count).astype(jnp.float32) * (-2.0 * math.log(10000.0) / head_dim)
    )
    angles = places.astype(jnp.float32)[:, None] * freq_rates[None, :]
    return (jnp.cos(angles), jnp.sin(angles))


def rotate(values, cosine, sine_table, direction):
    pair_count = values.shape[-1] // 2
    leading = values[..., :pair_count]
    trailing = values[..., pair_count:]
    cos_wide = cosine[:, None, :]
    sin_wide = sine_table[:, None, :] * direction
    return jnp.concatenate(
        [leading * cos_wide - trailing * sin_wide, trailing * cos_wide + leading * sin_wide],
        axis=-1,
    )


def inner_rows(left_op, right_op):
    return lax.dot_general(
        left_op, right_op, (((0,), (0,)), ((), ())), preferred_element_type=jnp.float32
    )


def times_transposed(left_op, right_op):
    return lax.dot_general(
        left_op, right_op, (((1,), (1,)), ((), ())), preferred_element_type=jnp.float32
    )


def body(
    frames,
    cotangent,
    lengths,
    qkv_weight,
    out_weight,
    gate_weight,
    up_weight,
    down_weight,
    gain_table,
    bias_table,
):
    seq_parts = lax.axis_size("seq")
    seq_index = lax.axis_index("seq")
    model_width = frames.shape[2]
    clip_len = frames.shape[1] * seq_parts
    head_dim = model_width // HEADS
    score_scale = 1.0 / math.sqrt(head_dim)
    frames_here, tangent_here = (frames, cotangent)
    places = seq_index * frames.shape[1] + jnp.arange(frames.shape[1])
    heads_here = HEADS // seq_parts
    groups, row_len = (frames_here.shape[0], frames_here.shape[1])
    row_count = groups * row_len
    width_here = heads_here * head_dim
    valid_rows = (places[None, :] < lengths[:, None]).astype(jnp.float32).reshape(row_count, 1)
    cosine, sine_table = rotary_tables(places, head_dim)
    full_cosine, full_sine = rotary_tables(jnp.arange(clip_len), head_dim)
    source = frames_here.astype(jnp.float32).reshape(row_count, model_width)
    normed_one, normal_one, inverse_one = norm_forward(source, gain_table[:, 0], bias_table[:, 0])
    normed_one = normed_one.astype(jnp.bfloat16)
    mixed_rows = jnp.dot(normed_one, qkv_weight, preferred_element_type=jnp.float32)
    shaped = mixed_rows.reshape(groups, row_len, 3, HEADS, head_dim)
    queries = (
        rotate(shaped[:, :, 0], cosine, sine_table, 1.0)
        .astype(jnp.bfloat16)
        .reshape(groups, row_len, model_width)
    )
    key_rows = (
        rotate(shaped[:, :, 1], cosine, sine_table, 1.0)
        .astype(jnp.bfloat16)
        .reshape(groups, row_len, model_width)
    )
    values = shaped[:, :, 2].astype(jnp.bfloat16).reshape(groups, row_len, model_width)
    head_queries, head_keys, head_values = (
        lax.all_to_all(queries, "seq", split_axis=2, concat_axis=1, tiled=True),
        lax.all_to_all(key_rows, "seq", split_axis=2, concat_axis=1, tiled=True),
        lax.all_to_all(values, "seq", split_axis=2, concat_axis=1, tiled=True),
    )
    head_queries = head_queries.reshape(groups, clip_len, heads_here, head_dim)
    head_keys = head_keys.reshape(groups, clip_len, heads_here, head_dim)
    head_values = head_values.reshape(groups, clip_len, heads_here, head_dim)
    query_pos = jnp.arange(clip_len)[:, None]
    key_pos = jnp.arange(clip_len)[None, :]
    window_mask = (key_pos <= query_pos) & (key_pos > query_pos - WINDOW)

    def clip_scores(clip_queries, clip_keys, length):
        products = jnp.einsum(
            "qhd,khd->hqk", clip_queries, clip_keys, preferred_element_type=jnp.float32
        )
        allowed = window_mask & (key_pos < length)
        return (jnp.where(allowed[None], products * score_scale, MASKED), allowed)

    def attend(block_item):
        clip_queries, clip_keys, clip_values, length = block_item
        scores, allowed = clip_scores(clip_queries, clip_keys, length)
        top_score = jnp.max(scores, axis=-1, keepdims=True)
        exponent = jnp.exp(scores - top_score)
        row_total = jnp.sum(exponent, axis=-1, keepdims=True)
        weights_low = (exponent / row_total).astype(jnp.bfloat16)
        context = jnp.einsum(
            "hqk,khd->qhd", weights_low, clip_values, preferred_element_type=jnp.float32
        )
        return (context.astype(jnp.bfloat16), top_score + jnp.log(row_total))

    context_heads, log_totals = lax.map(attend, (head_queries, head_keys, head_values, lengths))
    context_heads = context_heads.reshape(groups, clip_len, width_here)
    context = lax.all_to_all(context_heads, "seq", split_axis=1, concat_axis=2, tiled=True).reshape(
        row_count, model_width
    )
    attended = jnp.dot(context, out_weight, preferred_element_type=jnp.float32)
    middle = source + gain_table[:, 2] * attended
    normed_two, normal_two, inverse_two = norm_forward(middle, gain_table[:, 1], bias_table[:, 1])
    normed_two = normed_two.astype(jnp.bfloat16)
    gate_rows = jnp.dot(normed_two, gate_weight, preferred_element_type=jnp.float32)
    upward = jnp.dot(normed_two, up_weight, preferred_element_type=jnp.float32)
    sigmoid_gate = jax.nn.sigmoid(gate_rows)
    activated = gate_rows * sigmoid_gate
    hidden = (activated * upward).astype(jnp.bfloat16)
    branch = jnp.dot(hidden, down_weight, preferred_element_type=jnp.float32)
    output = (
        ((middle + gain_table[:, 3] * branch) * valid_rows)
        .astype(jnp.bfloat16)
        .reshape(groups, row_len, model_width)
    )
    output_delta = tangent_here.astype(jnp.float32).reshape(row_count, model_width) * valid_rows
    branch_delta = (output_delta * gain_table[:, 3]).astype(jnp.bfloat16)
    scale_mlp = jnp.sum(output_delta * branch, axis=0)
    down_grad = inner_rows(hidden, branch_delta)
    hidden_delta = times_transposed(branch_delta, down_weight)
    up_delta = (hidden_delta * activated).astype(jnp.bfloat16)
    gate_delta = (
        hidden_delta * upward * sigmoid_gate * (1.0 + gate_rows * (1.0 - sigmoid_gate))
    ).astype(jnp.bfloat16)
    gate_grad = inner_rows(normed_two, gate_delta)
    up_grad = inner_rows(normed_two, up_delta)
    second_delta = times_transposed(gate_delta, gate_weight) + times_transposed(up_delta, up_weight)
    back_two, gain_two, bias_two = norm_backward(
        second_delta, normal_two, inverse_two, gain_table[:, 1]
    )
    middle_delta = output_delta + back_two
    attended_delta = (middle_delta * gain_table[:, 2]).astype(jnp.bfloat16)
    scale_attn = jnp.sum(middle_delta * attended, axis=0)
    out_grad = inner_rows(context, attended_delta)
    context_delta = (
        times_transposed(attended_delta, out_weight)
        .astype(jnp.bfloat16)
        .reshape(groups, row_len, model_width)
    )
    context_heads_delta = lax.all_to_all(
        context_delta, "seq", split_axis=2, concat_axis=1, tiled=True
    )
    context_heads_delta = context_heads_delta.reshape(groups, clip_len, heads_here, head_dim)

    def attend_back(block_item):
        clip_queries, clip_keys, clip_values, length, log_total, clip_delta = block_item
        scores, allowed = clip_scores(clip_queries, clip_keys, length)
        weights = jnp.exp(scores - log_total)
        weights_low = weights.astype(jnp.bfloat16)
        weight_delta = jnp.einsum(
            "qhd,khd->hqk", clip_delta, clip_values, preferred_element_type=jnp.float32
        )
        row_inner = jnp.sum(weight_delta * weights, axis=-1, keepdims=True)
        product_delta = jnp.where(
            allowed[None], weights * (weight_delta - row_inner) * score_scale, 0.0
        ).astype(jnp.bfloat16)
        query_delta = jnp.einsum(
            "hqk,khd->qhd", product_delta, clip_keys, preferred_element_type=jnp.float32
        )
        key_delta = jnp.einsum(
            "hqk,qhd->khd", product_delta, clip_queries, preferred_element_type=jnp.float32
        )
        value_delta = jnp.einsum(
            "hqk,qhd->khd", weights_low, clip_delta, preferred_element_type=jnp.float32
        )
        query_delta = rotate(query_delta, full_cosine, full_sine, -1.0).astype(jnp.bfloat16)
        key_delta = rotate(key_delta, full_cosine, full_sine, -1.0).astype(jnp.bfloat16)
        return (query_delta, key_delta, value_delta.astype(jnp.bfloat16))

    query_delta, key_delta, value_delta = lax.map(
        attend_back,
        (head_queries, head_keys, head_values, lengths, log_totals, context_heads_delta),
    )
    query_delta = query_delta.reshape(groups, clip_len, width_here)
    key_delta = key_delta.reshape(groups, clip_len, width_here)
    value_delta = value_delta.reshape(groups, clip_len, width_here)
    query_back, key_back, value_back = (
        lax.all_to_all(query_delta, "seq", split_axis=1, concat_axis=2, tiled=True),
        lax.all_to_all(key_delta, "seq", split_axis=1, concat_axis=2, tiled=True),
        lax.all_to_all(value_delta, "seq", split_axis=1, concat_axis=2, tiled=True),
    )
    mixed_delta = jnp.concatenate(
        [
            query_back.reshape(row_count, model_width),
            key_back.reshape(row_count, model_width),
            value_back.reshape(row_count, model_width),
        ],
        axis=1,
    )
    qkv_grad = inner_rows(normed_one, mixed_delta)
    first_delta = times_transposed(mixed_delta, qkv_weight)
    back_one, gain_one, bias_one = norm_backward(
        first_delta, normal_one, inverse_one, gain_table[:, 0]
    )
    input_grad = (
        (middle_delta + back_one).astype(jnp.bfloat16).reshape(groups, row_len, model_width)
    )
    gain_grad = jnp.stack([gain_one, gain_two, scale_attn, scale_mlp], axis=1)
    bias_grad = jnp.stack([bias_one, bias_two], axis=1)
    over_clips = (
        lax.psum_scatter(qkv_grad, "dp", scatter_dimension=0, tiled=True),
        lax.psum_scatter(out_grad, "dp", scatter_dimension=0, tiled=True),
        lax.psum_scatter(gate_grad, "dp", scatter_dimension=0, tiled=True),
        lax.psum_scatter(up_grad, "dp", scatter_dimension=0, tiled=True),
        lax.psum_scatter(down_grad, "dp", scatter_dimension=0, tiled=True),
        lax.psum_scatter(gain_grad, "dp", scatter_dimension=0, tiled=True),
        lax.psum_scatter(bias_grad, "dp", scatter_dimension=0, tiled=True),
    )
    summed = (
        lax.psum_scatter(
            over_clips[0].astype(jnp.bfloat16), "seq", scatter_dimension=1, tiled=True
        ).astype(jnp.float32),
        lax.psum_scatter(
            over_clips[1].astype(jnp.bfloat16), "seq", scatter_dimension=1, tiled=True
        ).astype(jnp.float32),
        lax.psum_scatter(
            over_clips[2].astype(jnp.bfloat16), "seq", scatter_dimension=1, tiled=True
        ).astype(jnp.float32),
        lax.psum_scatter(
            over_clips[3].astype(jnp.bfloat16), "seq", scatter_dimension=1, tiled=True
        ).astype(jnp.float32),
        lax.psum_scatter(
            over_clips[4].astype(jnp.bfloat16), "seq", scatter_dimension=1, tiled=True
        ).astype(jnp.float32),
        lax.psum_scatter(
            over_clips[5].astype(jnp.bfloat16), "seq", scatter_dimension=1, tiled=True
        ).astype(jnp.float32),
        lax.psum_scatter(
            over_clips[6].astype(jnp.bfloat16), "seq", scatter_dimension=1, tiled=True
        ).astype(jnp.float32),
    )
    return (
        output,
        input_grad,
        summed[0],
        summed[1],
        summed[2],
        summed[3],
        summed[4],
        summed[5],
        summed[6],
    )


BF = jnp.bfloat16
F32 = jnp.float32
TILE = 128
MIB = 1024 * 1024
HINT = 0.25


def mm(left, right):
    return lax.dot_general(left, right, (((1,), (0,)), ((), ())), preferred_element_type=F32)


def mm_t(left, right):
    return lax.dot_general(left, right, (((1,), (1,)), ((), ())), preferred_element_type=F32)


def t_mm(left, right):
    return lax.dot_general(left, right, (((0,), (0,)), ((), ())), preferred_element_type=F32)


def call_kernel(
    kernel, info, args, *, name, grid, ins, outs, shapes, scratch=(), vmem=60, cost=None, after=(),
    onto=(),
):
    flops, moved = cost
    aliases = {1 + len(args) + len(after) + k: k for k in range(len(onto))}
    after = (*after, *onto)
    count, unread = len(args), len(after)

    def run(info, *refs):
        kernel(info, *refs[:count], *refs[count + unread :])

    args = [*args, *after]
    ins = [*ins] + [pl.BlockSpec(memory_space=pl.ANY)] * unread
    return pl.pallas_call(
        run,
        grid_spec=pltpu.PrefetchScalarGridSpec(
            num_scalar_prefetch=1, grid=grid, in_specs=ins, out_specs=outs, scratch_shapes=scratch
        ),
        out_shape=shapes,
        input_output_aliases=aliases,
        compiler_params=pltpu.CompilerParams(
            dimension_semantics=("arbitrary",) * len(grid), vmem_limit_bytes=vmem * MIB
        ),
        cost_estimate=pl.CostEstimate(
            flops=int(flops * HINT), bytes_accessed=int(moved * HINT), transcendentals=0
        ),
        name=name,
    )(info, *args)


def shape_of(shape, dtype=BF):
    return jax.ShapeDtypeStruct(shape, dtype)


def rows_spec(rows, width, column=0):
    return pl.BlockSpec((rows, width), lambda r, info: (r, column))


def whole_spec(shape):
    return pl.BlockSpec(shape, lambda r, info: (0,) * len(shape))


LEN0 = 5


def norm_stats(values):
    row_mean = jnp.mean(values, axis=-1, keepdims=True)
    centred = values - row_mean
    inverse = lax.rsqrt(jnp.mean(centred * centred, axis=-1, keepdims=True) + NORM_EPS)
    return centred * inverse, inverse


def norm_back(upstream, normal, inverse, gain):
    scaled = upstream * gain
    return inverse * (
        scaled
        - jnp.mean(scaled, axis=-1, keepdims=True)
        - normal * jnp.mean(scaled * normal, axis=-1, keepdims=True)
    )


def turn(values, cosine, sine_a, sine_b):
    return (
        values * cosine
        + pltpu.roll(values, TILE - 32, 1) * sine_a
        + pltpu.roll(values, 32, 1) * sine_b
    )


def column_sum(values):
    return jnp.sum(values, axis=0, keepdims=True)


def staged(count, *stages):
    kept = [{} for _ in stages]
    for step in range(count + len(stages) - 1):
        for k, stage in enumerate(stages):
            i = step - k
            if 0 <= i < count:
                kept[k][i] = stage(i, kept[k - 1].pop(i)) if k else stage(i)


def qkv_kernel(info, x_ref, w_ref, gb_ref, tab_ref, qkv_ref, n_ref):
    r = pl.program_id(0)
    rows = tab_ref.shape[1]
    parts = x_ref.shape[0] // rows
    places = [info[LEN0 + r * parts + p] for p in range(parts)]
    live = functools.reduce(jnp.logical_or, [info[3] < place for place in places])
    width = x_ref.shape[1]
    piece = 2 * TILE
    pieces = 3 * width // piece

    @pl.when(live)
    def _():
        normed = {}

        def product(i):
            p, k = divmod(i, pieces)
            at_rows = slice(p * rows, (p + 1) * rows)
            if k == 0:
                normal, _ = norm_stats(x_ref[at_rows, :].astype(F32))
                normed[p] = (normal * gb_ref[0:1, :] + gb_ref[4:5, :]).astype(BF)
                n_ref[at_rows, :] = normed[p]
            return mm(normed[p], w_ref[:, k * piece : (k + 1) * piece])

        def put(i, mixed):
            p, k = divmod(i, pieces)
            at_rows = slice(p * rows, (p + 1) * rows)
            for t in range(piece // TILE):
                value = mixed[:, t * TILE : (t + 1) * TILE]
                if k * piece < 2 * width:
                    value = turn(value, tab_ref[0], tab_ref[1], tab_ref[2])
                at = k * piece + t * TILE
                qkv_ref[at_rows, at : at + TILE] = value.astype(BF)

        staged(parts * pieces, product, put)

    @pl.when(jnp.logical_not(live))
    def _():
        qkv_ref[...] = jnp.zeros_like(qkv_ref)
        n_ref[...] = jnp.zeros_like(n_ref)


def halo_kernel(info, x_ref, wk_ref, wv_ref, gb_ref, tab_ref, kv_ref, n_ref):
    live = info[0] > 0
    rows, width = x_ref.shape
    piece = 2 * TILE
    pieces = width // piece

    @pl.when(live)
    def _():
        normal, _ = norm_stats(x_ref[...].astype(F32))
        normed = (normal * gb_ref[0:1, :] + gb_ref[4:5, :]).astype(BF)
        n_ref[...] = normed

        def product(i):
            ref, k = (wk_ref, i) if i < pieces else (wv_ref, i - pieces)
            return mm(normed, ref[:, k * piece : (k + 1) * piece])

        def put(i, mixed):
            if i >= pieces:
                kv_ref[:, i * piece : (i + 1) * piece] = mixed.astype(BF)
                return
            for t in range(piece // TILE):
                at = i * piece + t * TILE
                for row in range(0, rows, TILE):
                    value = mixed[row : row + TILE, t * TILE : (t + 1) * TILE]
                    value = turn(value, tab_ref[0], tab_ref[1], tab_ref[2])
                    kv_ref[row : row + TILE, at : at + TILE] = value.astype(BF)

        staged(2 * pieces, product, put)

    @pl.when(jnp.logical_not(live))
    def _():
        kv_ref[...] = jnp.zeros_like(kv_ref)
        n_ref[...] = jnp.zeros_like(n_ref)


def window_bias(info, clip, block):
    j = lax.broadcasted_iota(jnp.int32, (2 * TILE, 2 * TILE), 0)
    i = lax.broadcasted_iota(jnp.int32, (2 * TILE, 2 * TILE), 1) % TILE
    key = info[3] + (block - 1) * TILE + j
    allowed = (j > i) & (j <= i + TILE) & (key >= 0) & (key < info[LEN0 + clip])
    return jnp.where(allowed, 0.0, MASKED)


def two_heads(values):
    lane = lax.broadcasted_iota(jnp.int32, values.shape, 1)
    nought = jnp.zeros_like(values)
    return jnp.concatenate(
        [jnp.where(lane < 64, values, nought), jnp.where(lane < 64, nought, values)], axis=0
    )


def one_row(turned):
    return jnp.concatenate([turned[:64, :TILE], turned[64:, TILE:]], axis=0).T


def key_window(halo_ref, own_ref, block, at, own_at):
    if block == 0:
        return jnp.concatenate(
            [halo_ref[:, at : at + TILE], own_ref[0:TILE, own_at : own_at + TILE]], axis=0
        )
    return own_ref[(block - 1) * TILE : (block + 1) * TILE, own_at : own_at + TILE]


def attend_kernel(scale, block, info, qkv_ref, kvh_ref, ctx_ref, lse_ref):
    clip = pl.program_id(0)
    width = ctx_ref.shape[1]
    at_rows = slice(block * TILE, (block + 1) * TILE)
    live = info[3] < info[LEN0 + clip]

    @pl.when(live)
    def _():
        bias = window_bias(info, clip, block)

        def score(pair):
            at = pair * TILE
            queries = two_heads(qkv_ref[at_rows, at : at + TILE] * BF(scale))
            return mm_t(key_window(kvh_ref, qkv_ref, block, at, width + at), queries)

        def weigh(pair, scores):
            scores = scores + bias
            top = jnp.max(scores, axis=0, keepdims=True)
            exponent = jnp.exp(scores - top)
            total = jnp.sum(exponent, axis=0, keepdims=True)
            lse_ref[0, pair : pair + 1, :] = top + jnp.log(total)
            return (exponent * (1.0 / total)).astype(BF)

        def gather(pair, weights):
            at = pair * TILE
            values = key_window(kvh_ref, qkv_ref, block, width + at, 2 * width + at)
            return t_mm(values, weights)

        def put(pair, turned):
            ctx_ref[:, pair * TILE : (pair + 1) * TILE] = one_row(turned).astype(BF)

        staged(width // TILE, score, weigh, gather, put)

    @pl.when(jnp.logical_not(live))
    def _():
        ctx_ref[...] = jnp.zeros_like(ctx_ref)
        lse_ref[...] = jnp.zeros_like(lse_ref)


def attend_late_kernel(scale, info, qkv_ref, ctx_ref, lse_ref):
    attend_kernel(scale, 1, info, qkv_ref, None, ctx_ref, lse_ref)


def attend_back_kernel(
    scale, info, qkv_ref, kvh_ref, dctx_ref, lse_ref, tab_ref, tabh_ref, md_ref, mdh_ref
):
    clip = pl.program_id(0)
    rows, width = dctx_ref.shape
    live = info[3] < info[LEN0 + clip]

    @pl.when(jnp.logical_not(live))
    def _():
        md_ref[...] = jnp.zeros_like(md_ref)
        mdh_ref[...] = jnp.zeros_like(mdh_ref)

    @pl.when(live)
    def _():
        biases = [window_bias(info, clip, block) for block in range(2)]

        def place(item):
            pair, block = divmod(item, 2)
            return pair, block, pair * TILE, slice(block * TILE, (block + 1) * TILE)

        def score(item):
            pair, block, at, at_rows = place(item)
            queries = two_heads(qkv_ref[at_rows, at : at + TILE] * BF(scale))
            delta = two_heads(dctx_ref[at_rows, at : at + TILE])
            keys = key_window(kvh_ref, qkv_ref, block, at, width + at)
            values = key_window(kvh_ref, qkv_ref, block, width + at, 2 * width + at)
            return mm_t(keys, queries), mm_t(values, delta)

        def weigh(item, scores):
            pair, block, at, at_rows = place(item)
            products, weight_delta = scores
            weights = jnp.exp(products + biases[block] - lse_ref[block, pair : pair + 1, :])
            inner = jnp.sum(weight_delta * weights, axis=0, keepdims=True)
            return weights.astype(BF), (weights * (weight_delta - inner)).astype(BF)

        def gather(item, weighed):
            pair, block, at, at_rows = place(item)
            weights, score_delta = weighed
            queries = two_heads(qkv_ref[at_rows, at : at + TILE] * BF(scale))
            delta = two_heads(dctx_ref[at_rows, at : at + TILE])
            keys = key_window(kvh_ref, qkv_ref, block, at, width + at)
            return t_mm(keys, score_delta), mm(score_delta, queries), mm(weights, delta)

        before = {}
        early, late = slice(0, TILE), slice(TILE, 2 * TILE)

        def put_key(where, at, delta):
            md_ref[where, width + at : width + at + TILE] = turn(
                delta, tab_ref[0, where], -tab_ref[1, where], -tab_ref[2, where]
            ).astype(BF)

        def put(item, deltas):
            pair, block, at, at_rows = place(item)
            turned, key_delta, value_delta = deltas
            md_ref[at_rows, at : at + TILE] = turn(
                one_row(turned) * scale,
                tab_ref[0, at_rows], -tab_ref[1, at_rows], -tab_ref[2, at_rows],
            ).astype(BF)
            value_at = slice(2 * width + at, 2 * width + at + TILE)
            if block == 0:
                mdh_ref[:, at : at + TILE] = turn(
                    key_delta[early], tabh_ref[0], -tabh_ref[1], -tabh_ref[2]
                ).astype(BF)
                mdh_ref[:, width + at : width + at + TILE] = value_delta[early].astype(BF)
                before[pair] = key_delta[late], value_delta[late]
            else:
                key_before, value_before = before.pop(pair)
                put_key(early, at, key_before + key_delta[early])
                put_key(late, at, key_delta[late])
                md_ref[early, value_at] = (value_before + value_delta[early]).astype(BF)
                md_ref[late, value_at] = value_delta[late].astype(BF)

        staged(2 * (width // TILE), score, weigh, gather, put)


def out_kernel(parts, info, ctx_ref, x_ref, w_ref, gb_ref, att_ref, n_ref):
    r = pl.program_id(0)
    rows = x_ref.shape[0] // parts
    places = [info[LEN0 + r * parts + p] for p in range(parts)]
    live = functools.reduce(jnp.logical_or, [info[3] < place for place in places])

    def at(p):
        return slice(p * rows, (p + 1) * rows)

    @pl.when(live)
    def _():
        def product(p):
            return mm(ctx_ref[at(p), :], w_ref[...])

        def put(p, attended):
            att_ref[at(p), :] = attended.astype(BF)
            middle = x_ref[at(p), :].astype(F32) + gb_ref[2:3, :] * attended
            normal, _ = norm_stats(middle)
            n_ref[at(p), :] = (normal * gb_ref[1:2, :] + gb_ref[5:6, :]).astype(BF)

        staged(parts, product, put)

    @pl.when(jnp.logical_not(live))
    def _():
        att_ref[...] = jnp.zeros_like(att_ref)
        n_ref[...] = jnp.zeros_like(n_ref)


def row_valid(info, clip, rows):
    place = info[3] + lax.broadcasted_iota(jnp.int32, (rows, 1), 0)
    return (place < info[LEN0 + clip]).astype(F32)


def output_kernel(info, x_ref, att_ref, ba_ref, bb_ref, gb_ref, out_ref):
    r = pl.program_id(0)
    valid = row_valid(info, r, x_ref.shape[0])
    branch = ba_ref[...].astype(F32) + bb_ref[...].astype(F32)
    middle = x_ref[...].astype(F32) + gb_ref[2:3, :] * att_ref[...].astype(F32)
    out_ref[...] = ((middle + gb_ref[3:4, :] * branch) * valid).astype(BF)


def out_back_kernel(
    info, sa_ref, sb_ref, att_ref, x_ref, ct_ref, w_ref, gb_ref,
    delta_ref, dctx_ref, ad_ref, sum_ref,
):
    r = pl.program_id(0)
    rows, width = x_ref.shape

    @pl.when(r == 0)
    def _():
        sum_ref[...] = jnp.zeros_like(sum_ref)

    live = info[3] < info[LEN0 + r]

    @pl.when(live)
    def _():
        valid = row_valid(info, r, rows)
        attended = att_ref[...].astype(F32)
        middle = x_ref[...].astype(F32) + gb_ref[2:3, :] * attended
        normal, inverse = norm_stats(middle)
        second = sa_ref[...].astype(F32) + sb_ref[...].astype(F32)
        back = norm_back(second, normal, inverse, gb_ref[1:2, :])
        output_delta = ct_ref[...].astype(F32) * valid
        middle_delta = output_delta + back
        delta_ref[...] = middle_delta.astype(BF)
        attended_delta = (middle_delta * gb_ref[2:3, :]).astype(BF)
        dctx_ref[...] = mm_t(attended_delta, w_ref[...]).astype(BF)
        ad_ref[...] = attended_delta
        sum_ref[0:1, :] += column_sum(second * normal)
        sum_ref[1:2, :] += column_sum(middle_delta * attended)
        sum_ref[2:3, :] += column_sum(second)

    @pl.when(jnp.logical_not(live))
    def _():
        delta_ref[...] = jnp.zeros_like(delta_ref)
        dctx_ref[...] = jnp.zeros_like(dctx_ref)
        ad_ref[...] = jnp.zeros_like(ad_ref)


def qkv_grad_kernel(info, n_ref, md_ref, nh_ref, mdh_ref, ctx_ref, ad_ref, *refs):
    t = pl.program_id(0)
    acc = refs[4]

    @pl.when(t < 6)
    def _():
        acc[...] = t_mm(n_ref[...], md_ref[...])

    @pl.when((info[0] > 0) & (t >= 2) & (t < 6))
    def _():
        acc[...] += t_mm(nh_ref[...], mdh_ref[...])

    @pl.when(t >= 6)
    def _():
        acc[...] = t_mm(ctx_ref[...], ad_ref[...])

    def put(left):
        for y in range(2):
            for z in range(4):
                z_there = (info[4] // 2 + z // 2) % 2 * 2 + (info[4] + z) % 2
                base = z_there * 256 + ((info[1] + y) % 2) * 128
                for c in range(2):
                    row = pl.multiple_of(base + ((info[2] + c) % 2) * 64, 64)
                    value = acc[pl.ds(row, 64), :].astype(BF)
                    if left:
                        refs[2 * c][0, y, z] = value
                    else:
                        refs[2 * c + 1][y, 0, 0, z] = value

    leads = (t == 0) | (t == 3)
    pl.when(leads)(functools.partial(put, True))
    pl.when(jnp.logical_not(leads))(functools.partial(put, False))


def first_back_kernel(
    parts, info, md_ref, w_ref, x_ref, delta_ref, gb_ref, halo_ref, two_ref, branch_ref, out_ref, sum_ref
):
    r = pl.program_id(0)
    rows = x_ref.shape[0] // parts

    @pl.when(r == 0)
    def _():
        sum_ref[...] = jnp.zeros_like(sum_ref)
        sum_ref[0:1, :] = halo_ref[0:1, :]
        sum_ref[1:2, :] = two_ref[0:1, :]
        sum_ref[2:3, :] = halo_ref[1:2, :]
        sum_ref[4:5, :] = two_ref[1:2, :]
        sum_ref[5:6, :] = branch_ref[0:1, :] / gb_ref[3:4, :]
        sum_ref[6:7, :] = two_ref[2:3, :]

    places = [info[LEN0 + r * parts + p] for p in range(parts)]
    live = functools.reduce(jnp.logical_or, [info[3] < place for place in places])

    def at(p):
        return slice(p * rows, (p + 1) * rows)

    @pl.when(live)
    def _():
        def product(p):
            return mm_t(md_ref[at(p), :], w_ref[...])

        def put(p, first):
            normal, inverse = norm_stats(x_ref[at(p), :].astype(F32))
            back = norm_back(first, normal, inverse, gb_ref[0:1, :])
            out_ref[at(p), :] = (delta_ref[at(p), :].astype(F32) + back).astype(BF)
            sum_ref[0:1, :] += column_sum(first * normal)
            sum_ref[2:3, :] += column_sum(first)

        staged(parts, product, put)

    @pl.when(jnp.logical_not(live))
    def _():
        out_ref[...] = jnp.zeros_like(out_ref)


def first_halo_kernel(info, mdh_ref, wk_ref, wv_ref, x_ref, out_ref, sum_ref):
    width = x_ref.shape[1]
    live = info[0] > 0
    sum_ref[...] = jnp.zeros_like(sum_ref)

    @pl.when(live)
    def _():
        first = mm_t(mdh_ref[:, :width], wk_ref[...]) + mm_t(mdh_ref[:, width:], wv_ref[...])
        out_ref[...] = first.astype(BF)
        normal, _ = norm_stats(x_ref[...].astype(F32))
        sum_ref[0:1, :] = column_sum(first * normal)
        sum_ref[1:2, :] = column_sum(first)

    @pl.when(jnp.logical_not(live))
    def _():
        out_ref[...] = jnp.zeros_like(out_ref)


def input_grad_kernel(info, part_ref, halo_ref, x_ref, gb_ref, out_ref):
    rows = part_ref.shape[0]
    split = rows - halo_ref.shape[0]
    out_ref[:split, :] = part_ref[:split, :]

    @pl.when(info[0] == 0)
    def _():
        normal, inverse = norm_stats(x_ref[split:, :].astype(F32))
        back = norm_back(halo_ref[...].astype(F32), normal, inverse, gb_ref[0:1, :])
        out_ref[split:, :] = (part_ref[split:, :].astype(F32) + back).astype(BF)

    @pl.when(info[0] > 0)
    def _():
        out_ref[split:, :] = part_ref[split:, :]


def hidden_block(info, c, k):
    z0, x, q = k // 4, k // 2 % 2, k % 2
    d = ((info[0] + x) % 2 * 2 + z0) * 4 + (info[1] + q) % 2 * 2 + info[2]
    return pl.ds(pl.multiple_of(d * 256 + c * TILE, TILE), TILE)


def ffn_kernel(c, first, half, info, n_own, n_other, b_own, b_other, *rest):
    if not first:
        earlier, rest = rest[:2], rest[2:]
    wg_hbm, wu_hbm, wd_hbm, hidden_ref, *rest = rest
    sums, rest = rest[:2], rest[2:]
    packs, rest = (rest[0:2], rest[2:4]), rest[4:]
    wg, wu, wd, ag, au, ad, n_buf, b_buf, sems, row_sems = rest
    r = pl.program_id(0)
    steps = pl.num_programs(0)
    block_rows = n_buf.shape[1]

    def weight_copies(kind):
        hbm, vmem = ((wg_hbm, wg), (wu_hbm, wu), (wd_hbm, wd))[kind]
        for k in range(8):
            src, dst = hidden_block(info, c, k), pl.ds(k * TILE, TILE)
            if kind < 2:
                yield pltpu.make_async_copy(hbm.at[:, src], vmem.at[:, dst], sems.at[kind, k])
            else:
                yield pltpu.make_async_copy(hbm.at[src, :], vmem.at[dst, :], sems.at[kind, k])

    def row_copies(step, sources):
        src = pl.ds(pl.multiple_of(step % half * block_rows, block_rows), block_rows)
        for i, (hbm, vmem) in enumerate(zip(sources, (n_buf, b_buf))):
            yield pltpu.make_async_copy(
                hbm.at[src, :], vmem.at[step % 2], row_sems.at[i, step % 2]
            )

    def start_rows(step):
        @pl.when(step < half)
        def _():
            for copy in row_copies(step, (n_own, b_own)):
                copy.start()

        @pl.when(step >= half)
        def _():
            for copy in row_copies(step, (n_other, b_other)):
                copy.start()

    @pl.when(r == 0)
    def _():
        start_rows(r)
        for kind in range(3):
            for copy in weight_copies(kind):
                copy.start()
        for acc in (ag, au, ad):
            acc[...] = jnp.zeros_like(acc)

    @pl.when(r + 1 < steps)
    def _():
        start_rows(r + 1)

    for copy in row_copies(r, (n_own, b_own)):
        copy.wait()

    @pl.when(r == 0)
    def _():
        for kind in range(3):
            for copy in weight_copies(kind):
                copy.wait()

    normed, delta = n_buf.at[r % 2], b_buf.at[r % 2]
    gate = mm(normed[...], wg[...])
    upward = mm(normed[...], wu[...])
    hidden_delta = mm_t(delta[...], wd[...])
    sigmoid = jax.nn.sigmoid(gate)
    active = gate * sigmoid
    hidden = (active * upward).astype(BF)
    up_delta = (hidden_delta * active).astype(BF)
    gate_delta = (hidden_delta * upward * (sigmoid + active * (1.0 - sigmoid))).astype(BF)
    hidden_ref[...] = hidden
    second = mm_t(gate_delta, wg[...]) + mm_t(up_delta, wu[...])
    if not first:
        second = second + jnp.where(r < half, earlier[0][...], earlier[1][...]).astype(F32)
    second = second.astype(BF)
    sums[0][...] = second
    sums[1][...] = second
    ag[...] += t_mm(normed[...], gate_delta)
    au[...] += t_mm(normed[...], up_delta)
    ad[...] += t_mm(delta[...], hidden)

    @pl.when(r == pl.num_programs(0) - 1)
    def _():
        def flip(bit, own):
            return (bit + own) % 2

        def tile(acc, row, col):
            row = pl.multiple_of(row * TILE, TILE)
            col = pl.multiple_of(col * TILE, TILE)
            return acc[pl.ds(row, TILE), pl.ds(col, TILE)].astype(BF)

        x_own, y_own, z1_own, z0_own = info[0], info[1], info[4] // 2, info[4] % 2
        for u in range(2):
            for x in range(2):
                for y in range(2):
                    lead, other = (x, y) if u == 0 else (y, x)
                    ref = packs[u][lead]

                    def put(at, value):
                        ref[other, at * TILE : (at + 1) * TILE, :] = value

                    for z0 in range(2):
                        for z1 in range(2):
                            z1_at, z0_at = flip(z1, z1_own), flip(z0, z0_own)
                            at = 12 * z0 + 6 * z1
                            row = (z1_at * 2 + z0_at) * 2 + flip(y, y_own)
                            for i, acc in enumerate((ag, au)):
                                for q in range(2):
                                    col = u * 4 + x * 2 + flip(q, y_own)
                                    put(at + 2 * i + q, tile(acc, row, col))
                            col = z0_at * 4 + flip(z1_at, x_own) * 2 + y
                            for dq in range(2):
                                row = flip(x, x_own) * 4 + 2 * u + dq
                                put(at + 4 + dq, tile(ad, row, col))


def ffn_call(c, info, pieces, weights, previous, after=(), block_rows=256):
    rows, width = pieces[0].shape
    half = rows // block_rows
    first = previous is None
    hidden = 8 * TILE
    own = pl.BlockSpec((block_rows, width), lambda r, info: (jnp.minimum(r, half), 0))
    other = pl.BlockSpec((block_rows, width), lambda r, info: (jnp.maximum(r - half, 0), 0))
    every = pl.BlockSpec((block_rows, hidden), lambda r, info: (r, 0))
    packed = (2, 24 * TILE, TILE)
    pack = pl.BlockSpec(packed, lambda r, info: (0, 0, 0), pipeline_mode=pl.Buffered(1))
    extra = [] if first else list(previous)
    anywhere = pl.BlockSpec(memory_space=pl.ANY)
    return call_kernel(
        functools.partial(ffn_kernel, c, first, half),
        info,
        [*pieces, *extra, *weights],
        name="feed_forward",
        grid=(2 * half,),
        ins=[anywhere] * 4 + [own, other] * (len(extra) // 2) + [anywhere] * 3,
        outs=[every, own, other] + [pack] * 4,
        shapes=[
            shape_of((2 * rows, hidden)), shape_of((rows + block_rows, width)), shape_of((rows, width))
        ] + [shape_of(packed)] * 4,
        scratch=[
            pltpu.VMEM((width, hidden), BF),
            pltpu.VMEM((width, hidden), BF),
            pltpu.VMEM((hidden, width), BF),
            pltpu.VMEM((width, hidden), F32),
            pltpu.VMEM((width, hidden), F32),
            pltpu.VMEM((width, hidden), F32),
            pltpu.VMEM((2, block_rows, width), BF),
            pltpu.VMEM((2, block_rows, width), BF),
            pltpu.SemaphoreType.DMA((3, 8)),
            pltpu.SemaphoreType.DMA((2, 2)),
        ],
        vmem=60,
        cost=(18 * 2 * rows * width * hidden, 30 * MIB),
        after=after,
    )


def branch_kernel(half, info, ha, hb, b_own, b_other, wd_hbm, own_ref, other_ref, sum_ref, wd, sems):
    r = pl.program_id(0)

    def copies():
        for c in range(2):
            for k in range(8):
                dst = wd.at[c, pl.ds(k * TILE, TILE), :]
                yield pltpu.make_async_copy(wd_hbm.at[hidden_block(info, c, k), :], dst, sems.at[c, k])

    @pl.when(r == 0)
    def _():
        for copy in copies():
            copy.start()
        sum_ref[...] = jnp.zeros_like(sum_ref)
        for copy in copies():
            copy.wait()

    branch = mm(ha[...], wd[0]) + mm(hb[...], wd[1])
    delta = jnp.where(r < half, b_own[...], b_other[...]).astype(F32)
    sum_ref[0:1, :] += column_sum(delta * branch)
    branch = branch.astype(BF)
    own_ref[...] = branch
    other_ref[...] = branch


def branch_call(info, hiddens, deltas, down_weight, after, block_rows=512):
    rows, width = deltas[0].shape
    half = rows // block_rows
    hidden = hiddens[0].shape[1]
    every = pl.BlockSpec((block_rows, hidden), lambda r, info: (r, 0))
    own = pl.BlockSpec((block_rows, width), lambda r, info: (jnp.minimum(r, half), 0))
    own_in = pl.BlockSpec((block_rows, width), lambda r, info: (jnp.minimum(r, half - 1), 0))
    other = pl.BlockSpec((block_rows, width), lambda r, info: (jnp.maximum(r - half, 0), 0))
    return call_kernel(
        functools.partial(branch_kernel, half), info, [*hiddens, *deltas, down_weight],
        name="branch", vmem=40, grid=(2 * half,),
        ins=[every, every, own_in, other, pl.BlockSpec(memory_space=pl.ANY)],
        outs=[own, other, whole_spec((8, width))],
        shapes=[
            shape_of((rows + block_rows, width)), shape_of((rows, width)), shape_of((8, width), F32)
        ],
        scratch=[pltpu.VMEM((2, hidden, width), BF), pltpu.SemaphoreType.DMA((2, 8))],
        cost=(4 * 2 * rows * width * hidden, 16 * MIB), after=after,
    )


SWAP = [(0, 1), (1, 0)]
Z_NEAR = [(0, 1), (1, 0), (2, 3), (3, 2)]
Z_FAR = [(0, 2), (2, 0), (1, 3), (3, 1)]


def meet(*values):
    return lax.optimization_barrier(values)


def later(values, *needed):
    return lax.optimization_barrier((values, needed))[0]


def swap(values, axis):
    return lax.ppermute(values, axis, SWAP)


def plus(left, right):
    return (left.astype(F32) + right.astype(F32)).astype(BF)


def fold(keep, send, axis):
    return plus(keep, swap(send, axis))


def fold_two(keep, send, lead, other):
    total = fold(keep, send, lead)
    return fold(total[0], total[1], other)


def scatter_z(values):
    return lax.psum_scatter(values, "z", scatter_dimension=0, tiled=True)[0]


def turn_table(first, last, head_dim):
    pairs = head_dim // 2
    rates = np.exp(np.arange(pairs, dtype=np.float32) * np.float32(-2.0 * math.log(10000.0) / head_dim))
    angles = np.arange(first, last, dtype=np.float32)[:, None] * rates[None, :].astype(np.float32)
    cosine, sine = (np.tile(t(angles), (1, TILE // pairs)) for t in (np.cos, np.sin))
    front = (np.arange(TILE) % head_dim < pairs)[None, :]
    return np.stack([cosine, np.where(front, -sine, 0), np.where(front, 0, sine)]).astype(np.float32)


def fast_body(
    frames, cotangent, lengths, qkv_weight, out_weight, gate_weight, up_weight, down_weight,
    gain_table, bias_table,
):
    clips, rows, width = frames.shape
    count = clips * rows
    head_dim = width // HEADS
    scale = 1.0 / math.sqrt(head_dim)
    x_at, y_at, core_at, z_at = (lax.axis_index(a) for a in ("seq", "y", "core", "z"))
    start = x_at * rows
    info = jnp.concatenate(
        [jnp.stack([x_at, y_at, core_at, start, z_at]).astype(jnp.int32), lengths.astype(jnp.int32)]
    )
    flat = frames.reshape(count, width)
    tangent = cotangent.reshape(count, width)
    halo = lax.ppermute(
        frames[:, rows - TILE :].reshape(clips * TILE, width), "seq", [(0, 1)]
    )
    places = start + jnp.arange(rows)
    valid = (places[None, :] < lengths[:, None]).astype(F32).reshape(count, 1)
    branch_delta = (tangent.astype(F32) * valid * gain_table[:, 3]).astype(BF)
    table = jnp.concatenate([gain_table, bias_table, jnp.zeros((width, 2), F32)], axis=1).T
    seats = lax.axis_size("seq")
    own_turns = jnp.asarray(turn_table(0, seats * rows, head_dim))
    halo_turns = jnp.asarray(
        np.concatenate([turn_table(i * rows - TILE, i * rows, head_dim) for i in range(seats)], axis=1)
    )
    own_tab = pl.BlockSpec((3, rows, TILE), lambda r, info: (0, info[0], 0))
    halo_tab = pl.BlockSpec((3, TILE, TILE), lambda r, info: (0, info[0], 0))
    gb = whole_spec(table.shape)
    own = rows_spec(rows, width)
    halo_rows = rows_spec(TILE, width)
    qkv_rows = rows_spec(rows, 3 * width)
    kv_rows = rows_spec(TILE, 2 * width)
    w_qkv = whole_spec((width, 3 * width))
    w_key = pl.BlockSpec((width, width), lambda r, info: (0, 1))
    w_value = pl.BlockSpec((width, width), lambda r, info: (0, 2))
    w_out = whole_spec((width, width))
    sums = whole_spec((8, width))

    grid = (clips,)
    mac = 2 * count * width * width

    def two_rows(width):
        return rows_spec(count // 2, width)

    qkv, normed_one = call_kernel(
        qkv_kernel, info, [flat, qkv_weight, table, own_turns], name="qkv", vmem=36, grid=(2,),
        ins=[two_rows(width), w_qkv, gb, own_tab], outs=[two_rows(3 * width), two_rows(width)],
        shapes=[shape_of((count, 3 * width)), shape_of((count, width))], cost=(3 * mac, 16 * MIB),
    )
    def half_rows(width, part):
        return pl.BlockSpec((TILE, width), lambda r, info: (2 * r + part, 0))

    totals_of = (2 * clips, width // TILE, 2 * TILE)
    seen = [shape_of((count, width)), shape_of(totals_of, F32)]

    def half_totals(part):
        return pl.BlockSpec((1, *totals_of[1:]), lambda r, info: (2 * r + part, 0, 0))

    late = call_kernel(
        functools.partial(attend_late_kernel, scale), info, [qkv], name="attend_late", vmem=16, grid=grid,
        ins=[qkv_rows], outs=[half_rows(width, 1), half_totals(1)], shapes=seen,
        cost=(2 * mac, 8 * MIB),
    )
    halo, branch_delta = lax.optimization_barrier((halo, branch_delta))
    branch_delta_other = swap(branch_delta, "core")
    kv_halo, normed_halo = call_kernel(
        halo_kernel, info, [halo, qkv_weight, qkv_weight, table, halo_turns], name="halo", vmem=24,
        grid=(1,), ins=[rows_spec(clips * TILE, width), w_key, w_value, gb, halo_tab],
        outs=[rows_spec(clips * TILE, 2 * width), rows_spec(clips * TILE, width)],
        shapes=[shape_of((clips * TILE, 2 * width)), shape_of((clips * TILE, width))],
        cost=(mac, 8 * MIB), after=late,
    )
    context, log_totals = call_kernel(
        functools.partial(attend_kernel, scale, 0), info, [qkv, kv_halo], name="attend_early", vmem=16,
        grid=grid, ins=[half_rows(3 * width, 0), kv_rows],
        outs=[half_rows(width, 0), half_totals(0)], shapes=seen,
        cost=(2 * mac, 12 * MIB), onto=late,
    )
    attended, normed_two = call_kernel(
        functools.partial(out_kernel, clips // 2), info, [context, flat, out_weight, table],
        name="project", vmem=24, grid=(2,), ins=[two_rows(width)] * 2 + [w_out, gb], outs=[two_rows(width)] * 2,
        shapes=[shape_of((count, width))] * 2, cost=(mac, 12 * MIB),
    )
    normed_two_other = swap(normed_two, "core")

    pieces = (normed_two, normed_two_other, branch_delta, branch_delta_other)
    weights = (gate_weight, up_weight, down_weight)
    def start_pair(keeps):
        (keep_a, send_a), (keep_b, send_b) = keeps
        return (keep_a, swap(send_a, "seq")), (keep_b, swap(send_b, "y"))

    def second_pair(totals):
        (stay_a, go_a), (stay_b, go_b) = totals
        return (stay_a, swap(go_a, "y")), (stay_b, swap(go_b, "seq"))

    def halves(pairs):
        return [tuple(plus(keep[k], came[k]) for k in range(2)) for keep, came in pairs]

    def near_parts(pairs):
        return [
            jnp.stack([plus(*(v.reshape(-1, 2, 12, TILE, TILE)[:, k] for v in pair)) for pair in pairs])
            for k in range(2)
        ]

    def to_near(values):
        return lax.ppermute(values, "z", Z_NEAR)

    def far_pair(*pair):
        total = plus(*pair).reshape(2, -1, 2, 6, TILE, TILE)
        return total[:, :, 0], lax.ppermute(total[:, :, 1], "z", Z_FAR)

    def run_ffn(c, previous, after):
        *state, keep_a, send_a, keep_b, send_b = ffn_call(
            c, info, pieces, weights, previous, after
        )
        return state, ((keep_a, send_a), (keep_b, send_b))

    (hidden_0, *previous), grads_0 = run_ffn(0, None, ())
    moved_0 = start_pair(grads_0)
    (hidden_1, second, second_sent), grads_1 = run_ffn(1, previous, ())
    second, second_sent, grads_1, moved_0 = meet(second, second_sent, grads_1, moved_0)
    second_other = swap(second_sent, "core")
    near_keep_0, near_send_0 = near_parts(moved_0)
    second_other, near_send_0, grads_1 = meet(second_other, near_send_0, grads_1)
    near_came_0 = to_near(near_send_0)
    moved_1 = start_pair(grads_1)

    middle_delta, context_delta, attended_delta, sums_two = call_kernel(
        out_back_kernel, info,
        [second, second_other, attended, flat, tangent, out_weight, table],
        name="project_back", vmem=32, grid=grid,
        ins=[own, own, own, own, own, w_out, gb], outs=[own, own, own, sums],
        shapes=[shape_of((count, width))] * 3 + [shape_of((8, width), F32)],
        cost=(2 * mac, 24 * MIB), after=(near_keep_0,),
    )

    mixed_delta, mixed_halo = call_kernel(
        functools.partial(attend_back_kernel, scale), info,
        [qkv, kv_halo, context_delta, log_totals, own_turns, halo_turns], name="attend_back",
        vmem=24, grid=grid,
        ins=[
            qkv_rows, kv_rows, own, pl.BlockSpec((2, *totals_of[1:]), lambda r, info: (r, 0, 0)),
            own_tab, halo_tab,
        ],
        outs=[qkv_rows, kv_rows],
        shapes=[shape_of((count, 3 * width)), shape_of((clips * TILE, 2 * width))],
        cost=(10 * mac, 24 * MIB),
    )
    mixed_delta, mixed_halo, moved_1, near_came_0 = meet(
        mixed_delta, mixed_halo, moved_1, near_came_0
    )
    totals_1 = halves(moved_1)
    moved_1 = second_pair(totals_1)
    far_0 = far_pair(near_keep_0, near_came_0)
    all_halo = rows_spec(clips * TILE, width)
    halo_back, sums_halo = call_kernel(
        first_halo_kernel, info, [mixed_halo, qkv_weight, qkv_weight, halo], name="first_halo",
        vmem=24, grid=(1,),
        ins=[rows_spec(clips * TILE, 2 * width), w_key, w_value, all_halo], outs=[all_halo, sums],
        shapes=[shape_of((clips * TILE, width)), shape_of((8, width), F32)],
        cost=(mac, 6 * MIB),
        after=(*(t for pair in totals_1 for t in pair), far_0[0]),
    )

    cut = 3 * width // 6

    def right_block(t, info):
        x = jnp.where(t < 6, t // 3, t - 6)
        return (0, (x + info[0]) % 2, jnp.where(t < 6, jnp.maximum(t % 3 - 1, 0), 2), 0, 0, 0)

    left_spec = pl.BlockSpec(
        (1, 2, 4, 64, cut), lambda t, info: ((jnp.minimum(t // 3, 1) + info[0]) % 2, 0, 0, 0, 0)
    )
    right_spec = pl.BlockSpec((2, 1, 1, 4, 64, cut), right_block)
    packed = [shape_of((2, 2, 4, 64, cut)), shape_of((2, 2, 3, 4, 64, cut))]
    keep_l, keep_r, send_l, send_r = call_kernel(
        qkv_grad_kernel, info,
        [normed_one, mixed_delta, normed_halo, mixed_halo, context, attended_delta],
        name="qkv_grad", vmem=40, grid=(8,),
        ins=[
            whole_spec((count, width)),
            pl.BlockSpec((count, cut), lambda t, info: (0, jnp.minimum(t, 5))),
            whole_spec((clips * TILE, width)),
            pl.BlockSpec((clips * TILE, cut), lambda t, info: (0, jnp.clip(t - 2, 0, 3))),
            whole_spec((count, width)),
            pl.BlockSpec((count, cut), lambda t, info: (0, jnp.maximum(t - 6, 0))),
        ],
        outs=[left_spec, right_spec] * 2, shapes=packed * 2,
        scratch=[pltpu.VMEM((width, cut), F32)], cost=(5 * mac, 20 * MIB),
        after=(halo_back,),
    )
    moved_1, keep_l, keep_r, send_l, send_r = meet(moved_1, keep_l, keep_r, send_l, send_r)
    came_l, came_r = swap(send_l, "core"), swap(send_r, "core")
    near_keep_1, near_send_1 = near_parts(moved_1)
    came_l, came_r, near_send_1, halo_back = meet(came_l, came_r, near_send_1, halo_back)
    stay_l, go_l = (plus(keep_l[k], came_l[k]) for k in range(2))
    stay_r, go_r = (plus(keep_r[k], came_r[k]) for k in range(2))
    go_l, go_r = swap(go_l, "seq"), swap(go_r, "y")
    halo_came = lax.ppermute(halo_back, "seq", [(1, 0)])
    near_came_1 = to_near(near_send_1)
    branch, branch_sent, sums_branch = branch_call(
        info, (hidden_0, hidden_1), (branch_delta, branch_delta_other), down_weight,
        (stay_l, stay_r, near_keep_1),
    )
    part_grad, vectors = call_kernel(
        functools.partial(first_back_kernel, clips // 2), info,
        [
            mixed_delta, qkv_weight, flat, middle_delta, table, sums_halo, sums_two, sums_branch
        ],
        name="first_back", vmem=40, grid=(2,),
        ins=[two_rows(3 * width), w_qkv, two_rows(width), two_rows(width), gb, sums, sums, sums],
        outs=[two_rows(width), sums],
        shapes=[shape_of((count, width)), shape_of((8, width), F32)],
        cost=(3 * mac, 24 * MIB),
    )
    go_l, go_r, near_came_1, halo_came, far_0, part_grad, vectors, branch_sent = meet(
        go_l, go_r, near_came_1, halo_came, far_0, part_grad, vectors, branch_sent
    )
    vectors_core = swap(vectors, "core")
    left, right = plus(stay_l, go_l), plus(stay_r, go_r)
    vectors_core, left, right = meet(vectors_core, left, right)
    vectors = vectors + vectors_core
    go_l, go_r = swap(left[1], "y"), swap(right[1], "seq")
    far_1 = far_pair(near_keep_1, near_came_1)
    branch_other = swap(branch_sent, "core")
    vectors_x = swap(vectors, "seq")
    input_grad = call_kernel(
        input_grad_kernel, info, [part_grad, halo_came, flat, table], name="input_grad", vmem=16,
        grid=grid, ins=[own, halo_rows, own, gb], outs=own, shapes=shape_of((count, width)),
        cost=(0, 8 * MIB), after=(left, right, far_1[0], vectors),
    )
    go_l, go_r, branch_other, vectors_x, input_grad = meet(
        go_l, go_r, branch_other, vectors_x, input_grad
    )
    left, right = plus(left[0], go_l), plus(right[0], go_r)
    qkv_total = jnp.concatenate([left[None], right]).reshape(4, 2, 2, 64, cut)
    go = to_near(qkv_total[:, :, 1])
    first_tiles = plus(*far_0)
    late_a, late_b = swap(first_tiles[0, 1], "y"), swap(first_tiles[1, 1], "seq")
    vectors = vectors + vectors_x
    vectors_y = swap(vectors, "y")
    output = call_kernel(
        output_kernel, info, [flat, attended, branch, branch_other, table],
        name="output", vmem=16, grid=grid, ins=[own, own, own, own, gb], outs=own,
        shapes=shape_of((count, width)), cost=(0, 14 * MIB),
        after=(qkv_total, first_tiles, vectors),
    )
    go, far_1, late_a, late_b, vectors_y, output = meet(
        go, far_1, late_a, late_b, vectors_y, output
    )
    vectors = vectors + vectors_y
    vectors = vectors + lax.ppermute(vectors, "z", Z_NEAR)
    vectors = vectors + lax.ppermute(vectors, "z", Z_FAR)
    qkv_total = plus(qkv_total[:, :, 0], go)
    qkv_total = plus(qkv_total[:, 0], lax.ppermute(qkv_total[:, 1], "z", Z_FAR))
    qkv_grad = qkv_total[:3].transpose(1, 0, 2).reshape(-1, 3 * cut).astype(F32)
    out_grad = qkv_total[3].astype(F32)

    share = width // 16
    seat = (z_at * 2 + y_at) * 2 + core_at
    vectors = lax.dynamic_slice(vectors, (4 * x_at, share * seat), (4, share)).T
    gain_grad, bias_grad = vectors[:, :2], vectors[:, 2:3]

    first_tiles = [plus(first_tiles[k, 0], came) for k, came in enumerate((late_a, late_b))]
    tiles = jnp.stack([jnp.stack(first_tiles), plus(*far_1)[:, 0]])
    gates = tiles[:, :, :4].reshape(2, 2, 2, 2, 2, share, TILE)
    kept = lax.dynamic_index_in_dim(gates, core_at, axis=4, keepdims=False)
    sent = lax.dynamic_index_in_dim(gates, 1 - core_at, axis=4, keepdims=False)
    came = swap(sent, "core")
    both = jnp.where(core_at == 0, jnp.stack([kept, came], 4), jnp.stack([came, kept], 4))
    both = both.transpose(2, 5, 1, 3, 4, 0, 6).astype(F32)
    gate_grad = both[0].reshape(share, -1)
    up_grad = both[1].reshape(share, -1)
    down_grad = tiles[:, :, 4:].reshape(2, width // 2, TILE).transpose(0, 2, 1).astype(F32)
    down_grad = down_grad.reshape(2 * TILE, width // 2)
    shape = (clips, rows, width)
    return (
        output.reshape(shape), input_grad.reshape(shape), qkv_grad, out_grad, gate_grad, up_grad,
        down_grad, gain_grad, bias_grad,
    )


def solution(mesh):
    placed = (("dp", "seq", None),) * 2 + (("dp",),) + ((),) * 7
    given = (("dp", "seq", None),) * 2 + (("dp", "seq"),) * 7
    fast = mesh.shape["dp"] == 16 and mesh.shape["seq"] == 2
    dp_axes = ("z", "y", "core") if fast else "dp"

    def specs(entries):
        return tuple(P(*(dp_axes if a == "dp" else a for a in entry)) for entry in entries)

    if fast:
        mesh = Mesh(mesh.devices.reshape(4, 2, 2, 2), ("z", "y", "core", "seq"))
    return jax.shard_map(
        fast_body if fast else body,
        mesh=mesh,
        in_specs=specs(placed),
        out_specs=specs(given),
        check_vma=False,
    )
```

```python
import functools
import math

import jax
import jax.numpy as jnp
import numpy as np
from jax import lax
from jax.experimental import pallas as pl
from jax.experimental.pallas import tpu as pltpu
from jax.sharding import Mesh
from jax.sharding import PartitionSpec as P

HEADS = 16
WINDOW = 128


NORM_EPS = 1e-05
MASKED = -1e30


def norm_forward(values, gain_col, shift_col):
    row_mean = jnp.mean(values, axis=-1, keepdims=True)
    centred = values - row_mean
    inverse = lax.rsqrt(jnp.mean(centred * centred, axis=-1, keepdims=True) + NORM_EPS)
    normal = centred * inverse
    return (normal * gain_col + shift_col, normal, inverse)


def norm_backward(upstream, normal, inverse, gain_col):
    scaled = upstream * gain_col
    inner_term = (
        scaled
        - jnp.mean(scaled, axis=-1, keepdims=True)
        - normal * jnp.mean(scaled * normal, axis=-1, keepdims=True)
    )
    return (inverse * inner_term, jnp.sum(upstream * normal, axis=0), jnp.sum(upstream, axis=0))


def rotary_tables(places, head_dim):
    pair_count = head_dim // 2
    freq_rates = jnp.exp(
        jnp.arange(pair_count).astype(jnp.float32) * (-2.0 * math.log(10000.0) / head_dim)
    )
    angles = places.astype(jnp.float32)[:, None] * freq_rates[None, :]
    return (jnp.cos(angles), jnp.sin(angles))


def rotate(values, cosine, sine_table, direction):
    pair_count = values.shape[-1] // 2
    leading = values[..., :pair_count]
    trailing = values[..., pair_count:]
    cos_wide = cosine[:, None, :]
    sin_wide = sine_table[:, None, :] * direction
    return jnp.concatenate(
        [leading * cos_wide - trailing * sin_wide, trailing * cos_wide + leading * sin_wide],
        axis=-1,
    )


def inner_rows(left_op, right_op):
    return lax.dot_general(
        left_op, right_op, (((0,), (0,)), ((), ())), preferred_element_type=jnp.float32
    )


def times_transposed(left_op, right_op):
    return lax.dot_general(
        left_op, right_op, (((1,), (1,)), ((), ())), preferred_element_type=jnp.float32
    )


def body(
    frames,
    cotangent,
    lengths,
    qkv_weight,
    out_weight,
    gate_weight,
    up_weight,
    down_weight,
    gain_table,
    bias_table,
):
    seq_parts = lax.axis_size("seq")
    seq_index = lax.axis_index("seq")
    model_width = frames.shape[2]
    clip_len = frames.shape[1] * seq_parts
    head_dim = model_width // HEADS
    score_scale = 1.0 / math.sqrt(head_dim)
    frames_here, tangent_here = (frames, cotangent)
    places = seq_index * frames.shape[1] + jnp.arange(frames.shape[1])
    heads_here = HEADS // seq_parts
    groups, row_len = (frames_here.shape[0], frames_here.shape[1])
    row_count = groups * row_len
    width_here = heads_here * head_dim
    valid_rows = (places[None, :] < lengths[:, None]).astype(jnp.float32).reshape(row_count, 1)
    cosine, sine_table = rotary_tables(places, head_dim)
    full_cosine, full_sine = rotary_tables(jnp.arange(clip_len), head_dim)
    source = frames_here.astype(jnp.float32).reshape(row_count, model_width)
    normed_one, normal_one, inverse_one = norm_forward(source, gain_table[:, 0], bias_table[:, 0])
    normed_one = normed_one.astype(jnp.bfloat16)
    mixed_rows = jnp.dot(normed_one, qkv_weight, preferred_element_type=jnp.float32)
    shaped = mixed_rows.reshape(groups, row_len, 3, HEADS, head_dim)
    queries = (
        rotate(shaped[:, :, 0], cosine, sine_table, 1.0)
        .astype(jnp.bfloat16)
        .reshape(groups, row_len, model_width)
    )
    key_rows = (
        rotate(shaped[:, :, 1], cosine, sine_table, 1.0)
        .astype(jnp.bfloat16)
        .reshape(groups, row_len, model_width)
    )
    values = shaped[:, :, 2].astype(jnp.bfloat16).reshape(groups, row_len, model_width)
    head_queries, head_keys, head_values = (
        lax.all_to_all(queries, "seq", split_axis=2, concat_axis=1, tiled=True),
        lax.all_to_all(key_rows, "seq", split_axis=2, concat_axis=1, tiled=True),
        lax.all_to_all(values, "seq", split_axis=2, concat_axis=1, tiled=True),
    )
    head_queries = head_queries.reshape(groups, clip_len, heads_here, head_dim)
    head_keys = head_keys.reshape(groups, clip_len, heads_here, head_dim)
    head_values = head_values.reshape(groups, clip_len, heads_here, head_dim)
    query_pos = jnp.arange(clip_len)[:, None]
    key_pos = jnp.arange(clip_len)[None, :]
    window_mask = (key_pos <= query_pos) & (key_pos > query_pos - WINDOW)

    def clip_scores(clip_queries, clip_keys, length):
        products = jnp.einsum(
            "qhd,khd->hqk", clip_queries, clip_keys, preferred_element_type=jnp.float32
        )
        allowed = window_mask & (key_pos < length)
        return (jnp.where(allowed[None], products * score_scale, MASKED), allowed)

    def attend(block_item):
        clip_queries, clip_keys, clip_values, length = block_item
        scores, allowed = clip_scores(clip_queries, clip_keys, length)
        top_score = jnp.max(scores, axis=-1, keepdims=True)
        exponent = jnp.exp(scores - top_score)
        row_total = jnp.sum(exponent, axis=-1, keepdims=True)
        weights_low = (exponent / row_total).astype(jnp.bfloat16)
        context = jnp.einsum(
            "hqk,khd->qhd", weights_low, clip_values, preferred_element_type=jnp.float32
        )
        return (context.astype(jnp.bfloat16), top_score + jnp.log(row_total))

    context_heads, log_totals = lax.map(attend, (head_queries, head_keys, head_values, lengths))
    context_heads = context_heads.reshape(groups, clip_len, width_here)
    context = lax.all_to_all(context_heads, "seq", split_axis=1, concat_axis=2, tiled=True).reshape(
        row_count, model_width
    )
    attended = jnp.dot(context, out_weight, preferred_element_type=jnp.float32)
    middle = source + gain_table[:, 2] * attended
    normed_two, normal_two, inverse_two = norm_forward(middle, gain_table[:, 1], bias_table[:, 1])
    normed_two = normed_two.astype(jnp.bfloat16)
    gate_rows = jnp.dot(normed_two, gate_weight, preferred_element_type=jnp.float32)
    upward = jnp.dot(normed_two, up_weight, preferred_element_type=jnp.float32)
    sigmoid_gate = jax.nn.sigmoid(gate_rows)
    activated = gate_rows * sigmoid_gate
    hidden = (activated * upward).astype(jnp.bfloat16)
    branch = jnp.dot(hidden, down_weight, preferred_element_type=jnp.float32)
    output = (
        ((middle + gain_table[:, 3] * branch) * valid_rows)
        .astype(jnp.bfloat16)
        .reshape(groups, row_len, model_width)
    )
    output_delta = tangent_here.astype(jnp.float32).reshape(row_count, model_width) * valid_rows
    branch_delta = (output_delta * gain_table[:, 3]).astype(jnp.bfloat16)
    scale_mlp = jnp.sum(output_delta * branch, axis=0)
    down_grad = inner_rows(hidden, branch_delta)
    hidden_delta = times_transposed(branch_delta, down_weight)
    up_delta = (hidden_delta * activated).astype(jnp.bfloat16)
    gate_delta = (
        hidden_delta * upward * sigmoid_gate * (1.0 + gate_rows * (1.0 - sigmoid_gate))
    ).astype(jnp.bfloat16)
    gate_grad = inner_rows(normed_two, gate_delta)
    up_grad = inner_rows(normed_two, up_delta)
    second_delta = times_transposed(gate_delta, gate_weight) + times_transposed(up_delta, up_weight)
    back_two, gain_two, bias_two = norm_backward(
        second_delta, normal_two, inverse_two, gain_table[:, 1]
    )
    middle_delta = output_delta + back_two
    attended_delta = (middle_delta * gain_table[:, 2]).astype(jnp.bfloat16)
    scale_attn = jnp.sum(middle_delta * attended, axis=0)
    out_grad = inner_rows(context, attended_delta)
    context_delta = (
        times_transposed(attended_delta, out_weight)
        .astype(jnp.bfloat16)
        .reshape(groups, row_len, model_width)
    )
    context_heads_delta = lax.all_to_all(
        context_delta, "seq", split_axis=2, concat_axis=1, tiled=True
    )
    context_heads_delta = context_heads_delta.reshape(groups, clip_len, heads_here, head_dim)

    def attend_back(block_item):
        clip_queries, clip_keys, clip_values, length, log_total, clip_delta = block_item
        scores, allowed = clip_scores(clip_queries, clip_keys, length)
        weights = jnp.exp(scores - log_total)
        weights_low = weights.astype(jnp.bfloat16)
        weight_delta = jnp.einsum(
            "qhd,khd->hqk", clip_delta, clip_values, preferred_element_type=jnp.float32
        )
        row_inner = jnp.sum(weight_delta * weights, axis=-1, keepdims=True)
        product_delta = jnp.where(
            allowed[None], weights * (weight_delta - row_inner) * score_scale, 0.0
        ).astype(jnp.bfloat16)
        query_delta = jnp.einsum(
            "hqk,khd->qhd", product_delta, clip_keys, preferred_element_type=jnp.float32
        )
        key_delta = jnp.einsum(
            "hqk,qhd->khd", product_delta, clip_queries, preferred_element_type=jnp.float32
        )
        value_delta = jnp.einsum(
            "hqk,qhd->khd", weights_low, clip_delta, preferred_element_type=jnp.float32
        )
        query_delta = rotate(query_delta, full_cosine, full_sine, -1.0).astype(jnp.bfloat16)
        key_delta = rotate(key_delta, full_cosine, full_sine, -1.0).astype(jnp.bfloat16)
        return (query_delta, key_delta, value_delta.astype(jnp.bfloat16))

    query_delta, key_delta, value_delta = lax.map(
        attend_back,
        (head_queries, head_keys, head_values, lengths, log_totals, context_heads_delta),
    )
    query_delta = query_delta.reshape(groups, clip_len, width_here)
    key_delta = key_delta.reshape(groups, clip_len, width_here)
    value_delta = value_delta.reshape(groups, clip_len, width_here)
    query_back, key_back, value_back = (
        lax.all_to_all(query_delta, "seq", split_axis=1, concat_axis=2, tiled=True),
        lax.all_to_all(key_delta, "seq", split_axis=1, concat_axis=2, tiled=True),
        lax.all_to_all(value_delta, "seq", split_axis=1, concat_axis=2, tiled=True),
    )
    mixed_delta = jnp.concatenate(
        [
            query_back.reshape(row_count, model_width),
            key_back.reshape(row_count, model_width),
            value_back.reshape(row_count, model_width),
        ],
        axis=1,
    )
    qkv_grad = inner_rows(normed_one, mixed_delta)
    first_delta = times_transposed(mixed_delta, qkv_weight)
    back_one, gain_one, bias_one = norm_backward(
        first_delta, normal_one, inverse_one, gain_table[:, 0]
    )
    input_grad = (
        (middle_delta + back_one).astype(jnp.bfloat16).reshape(groups, row_len, model_width)
    )
    gain_grad = jnp.stack([gain_one, gain_two, scale_attn, scale_mlp], axis=1)
    bias_grad = jnp.stack([bias_one, bias_two], axis=1)
    over_clips = (
        lax.psum_scatter(qkv_grad, "dp", scatter_dimension=0, tiled=True),
        lax.psum_scatter(out_grad, "dp", scatter_dimension=0, tiled=True),
        lax.psum_scatter(gate_grad, "dp", scatter_dimension=0, tiled=True),
        lax.psum_scatter(up_grad, "dp", scatter_dimension=0, tiled=True),
        lax.psum_scatter(down_grad, "dp", scatter_dimension=0, tiled=True),
        lax.psum_scatter(gain_grad, "dp", scatter_dimension=0, tiled=True),
        lax.psum_scatter(bias_grad, "dp", scatter_dimension=0, tiled=True),
    )
    summed = (
        lax.psum_scatter(
            over_clips[0].astype(jnp.bfloat16), "seq", scatter_dimension=1, tiled=True
        ).astype(jnp.float32),
        lax.psum_scatter(
            over_clips[1].astype(jnp.bfloat16), "seq", scatter_dimension=1, tiled=True
        ).astype(jnp.float32),
        lax.psum_scatter(
            over_clips[2].astype(jnp.bfloat16), "seq", scatter_dimension=1, tiled=True
        ).astype(jnp.float32),
        lax.psum_scatter(
            over_clips[3].astype(jnp.bfloat16), "seq", scatter_dimension=1, tiled=True
        ).astype(jnp.float32),
        lax.psum_scatter(
            over_clips[4].astype(jnp.bfloat16), "seq", scatter_dimension=1, tiled=True
        ).astype(jnp.float32),
        lax.psum_scatter(
            over_clips[5].astype(jnp.bfloat16), "seq", scatter_dimension=1, tiled=True
        ).astype(jnp.float32),
        lax.psum_scatter(
            over_clips[6].astype(jnp.bfloat16), "seq", scatter_dimension=1, tiled=True
        ).astype(jnp.float32),
    )
    return (
        output,
        input_grad,
        summed[0],
        summed[1],
        summed[2],
        summed[3],
        summed[4],
        summed[5],
        summed[6],
    )


BF = jnp.bfloat16
F32 = jnp.float32
TILE = 128
MIB = 1024 * 1024
HINT = 0.25


def mm(left, right):
    return lax.dot_general(left, right, (((1,), (0,)), ((), ())), preferred_element_type=F32)


def mm_t(left, right):
    return lax.dot_general(left, right, (((1,), (1,)), ((), ())), preferred_element_type=F32)


def t_mm(left, right):
    return lax.dot_general(left, right, (((0,), (0,)), ((), ())), preferred_element_type=F32)


def call_kernel(
    kernel, info, args, *, name, grid, ins, outs, shapes, scratch=(), vmem=60, cost=None, after=(),
    onto=(),
):
    flops, moved = cost
    aliases = {1 + len(args) + len(after) + k: k for k in range(len(onto))}
    after = (*after, *onto)
    count, unread = len(args), len(after)

    def run(info, *refs):
        kernel(info, *refs[:count], *refs[count + unread :])

    args = [*args, *after]
    ins = [*ins] + [pl.BlockSpec(memory_space=pl.ANY)] * unread
    return pl.pallas_call(
        run,
        grid_spec=pltpu.PrefetchScalarGridSpec(
            num_scalar_prefetch=1, grid=grid, in_specs=ins, out_specs=outs, scratch_shapes=scratch
        ),
        out_shape=shapes,
        input_output_aliases=aliases,
        compiler_params=pltpu.CompilerParams(
            dimension_semantics=("arbitrary",) * len(grid), vmem_limit_bytes=vmem * MIB
        ),
        cost_estimate=pl.CostEstimate(
            flops=int(flops * HINT), bytes_accessed=int(moved * HINT), transcendentals=0
        ),
        name=name,
    )(info, *args)


def shape_of(shape, dtype=BF):
    return jax.ShapeDtypeStruct(shape, dtype)


def rows_spec(rows, width, column=0):
    return pl.BlockSpec((rows, width), lambda r, info: (r, column))


def whole_spec(shape):
    return pl.BlockSpec(shape, lambda r, info: (0,) * len(shape))


LEN0 = 5


def norm_stats(values):
    row_mean = jnp.mean(values, axis=-1, keepdims=True)
    centred = values - row_mean
    inverse = lax.rsqrt(jnp.mean(centred * centred, axis=-1, keepdims=True) + NORM_EPS)
    return centred * inverse, inverse


def norm_back(upstream, normal, inverse, gain):
    scaled = upstream * gain
    return inverse * (
        scaled
        - jnp.mean(scaled, axis=-1, keepdims=True)
        - normal * jnp.mean(scaled * normal, axis=-1, keepdims=True)
    )


def turn(values, cosine, sine_a, sine_b):
    return (
        values * cosine
        + pltpu.roll(values, TILE - 32, 1) * sine_a
        + pltpu.roll(values, 32, 1) * sine_b
    )


def column_sum(values):
    return jnp.sum(values, axis=0, keepdims=True)


def staged(count, *stages):
    kept = [{} for _ in stages]
    for step in range(count + len(stages) - 1):
        for k, stage in enumerate(stages):
            i = step - k
            if 0 <= i < count:
                kept[k][i] = stage(i, kept[k - 1].pop(i)) if k else stage(i)


def qkv_kernel(info, x_ref, w_ref, gb_ref, tab_ref, qkv_ref, n_ref):
    r = pl.program_id(0)
    rows = tab_ref.shape[1]
    parts = x_ref.shape[0] // rows
    places = [info[LEN0 + r * parts + p] for p in range(parts)]
    live = functools.reduce(jnp.logical_or, [info[3] < place for place in places])
    width = x_ref.shape[1]
    piece = 2 * TILE
    pieces = 3 * width // piece

    @pl.when(live)
    def _():
        normed = {}

        def product(i):
            p, k = divmod(i, pieces)
            at_rows = slice(p * rows, (p + 1) * rows)
            if k == 0:
                normal, _ = norm_stats(x_ref[at_rows, :].astype(F32))
                normed[p] = (normal * gb_ref[0:1, :] + gb_ref[4:5, :]).astype(BF)
                n_ref[at_rows, :] = normed[p]
            return mm(normed[p], w_ref[:, k * piece : (k + 1) * piece])

        def put(i, mixed):
            p, k = divmod(i, pieces)
            at_rows = slice(p * rows, (p + 1) * rows)
            for t in range(piece // TILE):
                value = mixed[:, t * TILE : (t + 1) * TILE]
                if k * piece < 2 * width:
                    value = turn(value, tab_ref[0], tab_ref[1], tab_ref[2])
                at = k * piece + t * TILE
                qkv_ref[at_rows, at : at + TILE] = value.astype(BF)

        staged(parts * pieces, product, put)

    @pl.when(jnp.logical_not(live))
    def _():
        qkv_ref[...] = jnp.zeros_like(qkv_ref)
        n_ref[...] = jnp.zeros_like(n_ref)


def halo_kernel(info, x_ref, wk_ref, wv_ref, gb_ref, tab_ref, kv_ref, n_ref):
    live = info[0] > 0
    rows, width = x_ref.shape
    piece = 2 * TILE
    pieces = width // piece

    @pl.when(live)
    def _():
        normal, _ = norm_stats(x_ref[...].astype(F32))
        normed = (normal * gb_ref[0:1, :] + gb_ref[4:5, :]).astype(BF)
        n_ref[...] = normed

        def product(i):
            ref, k = (wk_ref, i) if i < pieces else (wv_ref, i - pieces)
            return mm(normed, ref[:, k * piece : (k + 1) * piece])

        def put(i, mixed):
            if i >= pieces:
                kv_ref[:, i * piece : (i + 1) * piece] = mixed.astype(BF)
                return
            for t in range(piece // TILE):
                at = i * piece + t * TILE
                for row in range(0, rows, TILE):
                    value = mixed[row : row + TILE, t * TILE : (t + 1) * TILE]
                    value = turn(value, tab_ref[0], tab_ref[1], tab_ref[2])
                    kv_ref[row : row + TILE, at : at + TILE] = value.astype(BF)

        staged(2 * pieces, product, put)

    @pl.when(jnp.logical_not(live))
    def _():
        kv_ref[...] = jnp.zeros_like(kv_ref)
        n_ref[...] = jnp.zeros_like(n_ref)


def window_bias(info, clip, block):
    j = lax.broadcasted_iota(jnp.int32, (2 * TILE, 2 * TILE), 0)
    i = lax.broadcasted_iota(jnp.int32, (2 * TILE, 2 * TILE), 1) % TILE
    key = info[3] + (block - 1) * TILE + j
    allowed = (j > i) & (j <= i + TILE) & (key >= 0) & (key < info[LEN0 + clip])
    return jnp.where(allowed, 0.0, MASKED)


def two_heads(values):
    lane = lax.broadcasted_iota(jnp.int32, values.shape, 1)
    nought = jnp.zeros_like(values)
    return jnp.concatenate(
        [jnp.where(lane < 64, values, nought), jnp.where(lane < 64, nought, values)], axis=0
    )


def one_row(turned):
    return jnp.concatenate([turned[:64, :TILE], turned[64:, TILE:]], axis=0).T


def key_window(halo_ref, own_ref, block, at, own_at):
    if block == 0:
        return jnp.concatenate(
            [halo_ref[:, at : at + TILE], own_ref[0:TILE, own_at : own_at + TILE]], axis=0
        )
    return own_ref[(block - 1) * TILE : (block + 1) * TILE, own_at : own_at + TILE]


def attend_kernel(scale, block, info, qkv_ref, kvh_ref, ctx_ref, lse_ref):
    clip = pl.program_id(0)
    width = ctx_ref.shape[1]
    at_rows = slice(block * TILE, (block + 1) * TILE)
    live = info[3] < info[LEN0 + clip]

    @pl.when(live)
    def _():
        bias = window_bias(info, clip, block)

        def score(pair):
            at = pair * TILE
            queries = two_heads(qkv_ref[at_rows, at : at + TILE] * BF(scale))
            return mm_t(key_window(kvh_ref, qkv_ref, block, at, width + at), queries)

        def weigh(pair, scores):
            scores = scores + bias
            top = jnp.max(scores, axis=0, keepdims=True)
            exponent = jnp.exp(scores - top)
            total = jnp.sum(exponent, axis=0, keepdims=True)
            lse_ref[0, pair : pair + 1, :] = top + jnp.log(total)
            return (exponent * (1.0 / total)).astype(BF)

        def gather(pair, weights):
            at = pair * TILE
            values = key_window(kvh_ref, qkv_ref, block, width + at, 2 * width + at)
            return t_mm(values, weights)

        def put(pair, turned):
            ctx_ref[:, pair * TILE : (pair + 1) * TILE] = one_row(turned).astype(BF)

        staged(width // TILE, score, weigh, gather, put)

    @pl.when(jnp.logical_not(live))
    def _():
        ctx_ref[...] = jnp.zeros_like(ctx_ref)
        lse_ref[...] = jnp.zeros_like(lse_ref)


def attend_late_kernel(scale, info, qkv_ref, ctx_ref, lse_ref):
    attend_kernel(scale, 1, info, qkv_ref, None, ctx_ref, lse_ref)


def attend_back_kernel(
    scale, info, qkv_ref, kvh_ref, dctx_ref, lse_ref, tab_ref, tabh_ref, md_ref, mdh_ref
):
    clip = pl.program_id(0)
    rows, width = dctx_ref.shape
    live = info[3] < info[LEN0 + clip]

    @pl.when(jnp.logical_not(live))
    def _():
        md_ref[...] = jnp.zeros_like(md_ref)
        mdh_ref[...] = jnp.zeros_like(mdh_ref)

    @pl.when(live)
    def _():
        biases = [window_bias(info, clip, block) for block in range(2)]

        def place(item):
            pair, block = divmod(item, 2)
            return pair, block, pair * TILE, slice(block * TILE, (block + 1) * TILE)

        def score(item):
            pair, block, at, at_rows = place(item)
            queries = two_heads(qkv_ref[at_rows, at : at + TILE] * BF(scale))
            delta = two_heads(dctx_ref[at_rows, at : at + TILE])
            keys = key_window(kvh_ref, qkv_ref, block, at, width + at)
            values = key_window(kvh_ref, qkv_ref, block, width + at, 2 * width + at)
            return mm_t(keys, queries), mm_t(values, delta)

        def weigh(item, scores):
            pair, block, at, at_rows = place(item)
            products, weight_delta = scores
            weights = jnp.exp(products + biases[block] - lse_ref[block, pair : pair + 1, :])
            inner = jnp.sum(weight_delta * weights, axis=0, keepdims=True)
            return weights.astype(BF), (weights * (weight_delta - inner)).astype(BF)

        def gather(item, weighed):
            pair, block, at, at_rows = place(item)
            weights, score_delta = weighed
            queries = two_heads(qkv_ref[at_rows, at : at + TILE] * BF(scale))
            delta = two_heads(dctx_ref[at_rows, at : at + TILE])
            keys = key_window(kvh_ref, qkv_ref, block, at, width + at)
            return t_mm(keys, score_delta), mm(score_delta, queries), mm(weights, delta)

        before = {}
        early, late = slice(0, TILE), slice(TILE, 2 * TILE)

        def put_key(where, at, delta):
            md_ref[where, width + at : width + at + TILE] = turn(
                delta, tab_ref[0, where], -tab_ref[1, where], -tab_ref[2, where]
            ).astype(BF)

        def put(item, deltas):
            pair, block, at, at_rows = place(item)
            turned, key_delta, value_delta = deltas
            md_ref[at_rows, at : at + TILE] = turn(
                one_row(turned) * scale,
                tab_ref[0, at_rows], -tab_ref[1, at_rows], -tab_ref[2, at_rows],
            ).astype(BF)
            value_at = slice(2 * width + at, 2 * width + at + TILE)
            if block == 0:
                mdh_ref[:, at : at + TILE] = turn(
                    key_delta[early], tabh_ref[0], -tabh_ref[1], -tabh_ref[2]
                ).astype(BF)
                mdh_ref[:, width + at : width + at + TILE] = value_delta[early].astype(BF)
                before[pair] = key_delta[late], value_delta[late]
            else:
                key_before, value_before = before.pop(pair)
                put_key(early, at, key_before + key_delta[early])
                put_key(late, at, key_delta[late])
                md_ref[early, value_at] = (value_before + value_delta[early]).astype(BF)
                md_ref[late, value_at] = value_delta[late].astype(BF)

        staged(2 * (width // TILE), score, weigh, gather, put)


def out_kernel(parts, info, ctx_ref, x_ref, w_ref, gb_ref, att_ref, n_ref):
    r = pl.program_id(0)
    rows = x_ref.shape[0] // parts
    places = [info[LEN0 + r * parts + p] for p in range(parts)]
    live = functools.reduce(jnp.logical_or, [info[3] < place for place in places])

    def at(p):
        return slice(p * rows, (p + 1) * rows)

    @pl.when(live)
    def _():
        def product(p):
            return mm(ctx_ref[at(p), :], w_ref[...])

        def put(p, attended):
            att_ref[at(p), :] = attended.astype(BF)
            middle = x_ref[at(p), :].astype(F32) + gb_ref[2:3, :] * attended
            normal, _ = norm_stats(middle)
            n_ref[at(p), :] = (normal * gb_ref[1:2, :] + gb_ref[5:6, :]).astype(BF)

        staged(parts, product, put)

    @pl.when(jnp.logical_not(live))
    def _():
        att_ref[...] = jnp.zeros_like(att_ref)
        n_ref[...] = jnp.zeros_like(n_ref)


def row_valid(info, clip, rows):
    place = info[3] + lax.broadcasted_iota(jnp.int32, (rows, 1), 0)
    return (place < info[LEN0 + clip]).astype(F32)


def output_kernel(info, x_ref, att_ref, ba_ref, bb_ref, gb_ref, out_ref):
    r = pl.program_id(0)
    valid = row_valid(info, r, x_ref.shape[0])
    branch = ba_ref[...].astype(F32) + bb_ref[...].astype(F32)
    middle = x_ref[...].astype(F32) + gb_ref[2:3, :] * att_ref[...].astype(F32)
    out_ref[...] = ((middle + gb_ref[3:4, :] * branch) * valid).astype(BF)


def out_back_kernel(
    info, sa_ref, sb_ref, att_ref, x_ref, ct_ref, w_ref, gb_ref,
    delta_ref, dctx_ref, ad_ref, sum_ref,
):
    r = pl.program_id(0)
    rows, width = x_ref.shape

    @pl.when(r == 0)
    def _():
        sum_ref[...] = jnp.zeros_like(sum_ref)

    live = info[3] < info[LEN0 + r]

    @pl.when(live)
    def _():
        valid = row_valid(info, r, rows)
        attended = att_ref[...].astype(F32)
        middle = x_ref[...].astype(F32) + gb_ref[2:3, :] * attended
        normal, inverse = norm_stats(middle)
        second = sa_ref[...].astype(F32) + sb_ref[...].astype(F32)
        back = norm_back(second, normal, inverse, gb_ref[1:2, :])
        output_delta = ct_ref[...].astype(F32) * valid
        middle_delta = output_delta + back
        delta_ref[...] = middle_delta.astype(BF)
        attended_delta = (middle_delta * gb_ref[2:3, :]).astype(BF)
        dctx_ref[...] = mm_t(attended_delta, w_ref[...]).astype(BF)
        ad_ref[...] = attended_delta
        sum_ref[0:1, :] += column_sum(second * normal)
        sum_ref[1:2, :] += column_sum(middle_delta * attended)
        sum_ref[2:3, :] += column_sum(second)

    @pl.when(jnp.logical_not(live))
    def _():
        delta_ref[...] = jnp.zeros_like(delta_ref)
        dctx_ref[...] = jnp.zeros_like(dctx_ref)
        ad_ref[...] = jnp.zeros_like(ad_ref)


def qkv_grad_kernel(info, n_ref, md_ref, nh_ref, mdh_ref, ctx_ref, ad_ref, *refs):
    t = pl.program_id(0)
    acc = refs[4]

    @pl.when(t < 6)
    def _():
        acc[...] = t_mm(n_ref[...], md_ref[...])

    @pl.when((info[0] > 0) & (t >= 2) & (t < 6))
    def _():
        acc[...] += t_mm(nh_ref[...], mdh_ref[...])

    @pl.when(t >= 6)
    def _():
        acc[...] = t_mm(ctx_ref[...], ad_ref[...])

    def put(left):
        for y in range(2):
            for z in range(4):
                z_there = (info[4] // 2 + z // 2) % 2 * 2 + (info[4] + z) % 2
                base = z_there * 256 + ((info[1] + y) % 2) * 128
                for c in range(2):
                    row = pl.multiple_of(base + ((info[2] + c) % 2) * 64, 64)
                    value = acc[pl.ds(row, 64), :].astype(BF)
                    if left:
                        refs[2 * c][0, y, z] = value
                    else:
                        refs[2 * c + 1][y, 0, 0, z] = value

    leads = (t == 0) | (t == 3)
    pl.when(leads)(functools.partial(put, True))
    pl.when(jnp.logical_not(leads))(functools.partial(put, False))


def first_back_kernel(
    parts, info, md_ref, w_ref, x_ref, delta_ref, gb_ref, halo_ref, two_ref, branch_ref, out_ref, sum_ref
):
    r = pl.program_id(0)
    rows = x_ref.shape[0] // parts

    @pl.when(r == 0)
    def _():
        sum_ref[...] = jnp.zeros_like(sum_ref)
        sum_ref[0:1, :] = halo_ref[0:1, :]
        sum_ref[1:2, :] = two_ref[0:1, :]
        sum_ref[2:3, :] = halo_ref[1:2, :]
        sum_ref[4:5, :] = two_ref[1:2, :]
        sum_ref[5:6, :] = branch_ref[0:1, :] / gb_ref[3:4, :]
        sum_ref[6:7, :] = two_ref[2:3, :]

    places = [info[LEN0 + r * parts + p] for p in range(parts)]
    live = functools.reduce(jnp.logical_or, [info[3] < place for place in places])

    def at(p):
        return slice(p * rows, (p + 1) * rows)

    @pl.when(live)
    def _():
        def product(p):
            return mm_t(md_ref[at(p), :], w_ref[...])

        def put(p, first):
            normal, inverse = norm_stats(x_ref[at(p), :].astype(F32))
            back = norm_back(first, normal, inverse, gb_ref[0:1, :])
            out_ref[at(p), :] = (delta_ref[at(p), :].astype(F32) + back).astype(BF)
            sum_ref[0:1, :] += column_sum(first * normal)
            sum_ref[2:3, :] += column_sum(first)

        staged(parts, product, put)

    @pl.when(jnp.logical_not(live))
    def _():
        out_ref[...] = jnp.zeros_like(out_ref)


def first_halo_kernel(info, mdh_ref, wk_ref, wv_ref, x_ref, out_ref, sum_ref):
    width = x_ref.shape[1]
    live = info[0] > 0
    sum_ref[...] = jnp.zeros_like(sum_ref)

    @pl.when(live)
    def _():
        first = mm_t(mdh_ref[:, :width], wk_ref[...]) + mm_t(mdh_ref[:, width:], wv_ref[...])
        out_ref[...] = first.astype(BF)
        normal, _ = norm_stats(x_ref[...].astype(F32))
        sum_ref[0:1, :] = column_sum(first * normal)
        sum_ref[1:2, :] = column_sum(first)

    @pl.when(jnp.logical_not(live))
    def _():
        out_ref[...] = jnp.zeros_like(out_ref)


def input_grad_kernel(info, part_ref, halo_ref, x_ref, gb_ref, out_ref):
    rows = part_ref.shape[0]
    split = rows - halo_ref.shape[0]
    out_ref[:split, :] = part_ref[:split, :]

    @pl.when(info[0] == 0)
    def _():
        normal, inverse = norm_stats(x_ref[split:, :].astype(F32))
        back = norm_back(halo_ref[...].astype(F32), normal, inverse, gb_ref[0:1, :])
        out_ref[split:, :] = (part_ref[split:, :].astype(F32) + back).astype(BF)

    @pl.when(info[0] > 0)
    def _():
        out_ref[split:, :] = part_ref[split:, :]


def hidden_block(info, c, k):
    z0, x, q = k // 4, k // 2 % 2, k % 2
    d = ((info[0] + x) % 2 * 2 + z0) * 4 + (info[1] + q) % 2 * 2 + info[2]
    return pl.ds(pl.multiple_of(d * 256 + c * TILE, TILE), TILE)


def ffn_kernel(c, first, half, info, n_own, n_other, b_own, b_other, *rest):
    if not first:
        earlier, rest = rest[:2], rest[2:]
    wg_hbm, wu_hbm, wd_hbm, hidden_ref, *rest = rest
    sums, rest = rest[:2], rest[2:]
    packs, rest = (rest[0:2], rest[2:4]), rest[4:]
    wg, wu, wd, ag, au, ad, n_buf, b_buf, sems, row_sems = rest
    r = pl.program_id(0)
    steps = pl.num_programs(0)
    block_rows = n_buf.shape[1]

    def weight_copies(kind):
        hbm, vmem = ((wg_hbm, wg), (wu_hbm, wu), (wd_hbm, wd))[kind]
        for k in range(8):
            src, dst = hidden_block(info, c, k), pl.ds(k * TILE, TILE)
            if kind < 2:
                yield pltpu.make_async_copy(hbm.at[:, src], vmem.at[:, dst], sems.at[kind, k])
            else:
                yield pltpu.make_async_copy(hbm.at[src, :], vmem.at[dst, :], sems.at[kind, k])

    def row_copies(step, sources):
        src = pl.ds(pl.multiple_of(step % half * block_rows, block_rows), block_rows)
        for i, (hbm, vmem) in enumerate(zip(sources, (n_buf, b_buf))):
            yield pltpu.make_async_copy(
                hbm.at[src, :], vmem.at[step % 2], row_sems.at[i, step % 2]
            )

    def start_rows(step):
        @pl.when(step < half)
        def _():
            for copy in row_copies(step, (n_own, b_own)):
                copy.start()

        @pl.when(step >= half)
        def _():
            for copy in row_copies(step, (n_other, b_other)):
                copy.start()

    @pl.when(r == 0)
    def _():
        start_rows(r)
        for kind in range(3):
            for copy in weight_copies(kind):
                copy.start()
        for acc in (ag, au, ad):
            acc[...] = jnp.zeros_like(acc)

    @pl.when(r + 1 < steps)
    def _():
        start_rows(r + 1)

    for copy in row_copies(r, (n_own, b_own)):
        copy.wait()

    @pl.when(r == 0)
    def _():
        for kind in range(3):
            for copy in weight_copies(kind):
                copy.wait()

    normed, delta = n_buf.at[r % 2], b_buf.at[r % 2]
    gate = mm(normed[...], wg[...])
    upward = mm(normed[...], wu[...])
    hidden_delta = mm_t(delta[...], wd[...])
    sigmoid = jax.nn.sigmoid(gate)
    active = gate * sigmoid
    hidden = (active * upward).astype(BF)
    up_delta = (hidden_delta * active).astype(BF)
    gate_delta = (hidden_delta * upward * (sigmoid + active * (1.0 - sigmoid))).astype(BF)
    hidden_ref[...] = hidden
    second = mm_t(gate_delta, wg[...]) + mm_t(up_delta, wu[...])
    if not first:
        second = second + jnp.where(r < half, earlier[0][...], earlier[1][...]).astype(F32)
    second = second.astype(BF)
    sums[0][...] = second
    sums[1][...] = second
    ag[...] += t_mm(normed[...], gate_delta)
    au[...] += t_mm(normed[...], up_delta)
    ad[...] += t_mm(delta[...], hidden)

    @pl.when(r == pl.num_programs(0) - 1)
    def _():
        def flip(bit, own):
            return (bit + own) % 2

        def tile(acc, row, col):
            row = pl.multiple_of(row * TILE, TILE)
            col = pl.multiple_of(col * TILE, TILE)
            return acc[pl.ds(row, TILE), pl.ds(col, TILE)].astype(BF)

        x_own, y_own, z1_own, z0_own = info[0], info[1], info[4] // 2, info[4] % 2
        for u in range(2):
            for x in range(2):
                for y in range(2):
                    lead, other = (x, y) if u == 0 else (y, x)
                    ref = packs[u][lead]

                    def put(at, value):
                        ref[other, at * TILE : (at + 1) * TILE, :] = value

                    for z0 in range(2):
                        for z1 in range(2):
                            z1_at, z0_at = flip(z1, z1_own), flip(z0, z0_own)
                            at = 12 * z0 + 6 * z1
                            row = (z1_at * 2 + z0_at) * 2 + flip(y, y_own)
                            for i, acc in enumerate((ag, au)):
                                for q in range(2):
                                    col = u * 4 + x * 2 + flip(q, y_own)
                                    put(at + 2 * i + q, tile(acc, row, col))
                            col = z0_at * 4 + flip(z1_at, x_own) * 2 + y
                            for dq in range(2):
                                row = flip(x, x_own) * 4 + 2 * u + dq
                                put(at + 4 + dq, tile(ad, row, col))


def ffn_call(c, info, pieces, weights, previous, after=(), block_rows=256):
    rows, width = pieces[0].shape
    half = rows // block_rows
    first = previous is None
    hidden = 8 * TILE
    own = pl.BlockSpec((block_rows, width), lambda r, info: (jnp.minimum(r, half), 0))
    other = pl.BlockSpec((block_rows, width), lambda r, info: (jnp.maximum(r - half, 0), 0))
    every = pl.BlockSpec((block_rows, hidden), lambda r, info: (r, 0))
    packed = (2, 24 * TILE, TILE)
    pack = pl.BlockSpec(packed, lambda r, info: (0, 0, 0), pipeline_mode=pl.Buffered(1))
    extra = [] if first else list(previous)
    anywhere = pl.BlockSpec(memory_space=pl.ANY)
    return call_kernel(
        functools.partial(ffn_kernel, c, first, half),
        info,
        [*pieces, *extra, *weights],
        name="feed_forward",
        grid=(2 * half,),
        ins=[anywhere] * 4 + [own, other] * (len(extra) // 2) + [anywhere] * 3,
        outs=[every, own, other] + [pack] * 4,
        shapes=[
            shape_of((2 * rows, hidden)), shape_of((rows + block_rows, width)), shape_of((rows, width))
        ] + [shape_of(packed)] * 4,
        scratch=[
            pltpu.VMEM((width, hidden), BF),
            pltpu.VMEM((width, hidden), BF),
            pltpu.VMEM((hidden, width), BF),
            pltpu.VMEM((width, hidden), F32),
            pltpu.VMEM((width, hidden), F32),
            pltpu.VMEM((width, hidden), F32),
            pltpu.VMEM((2, block_rows, width), BF),
            pltpu.VMEM((2, block_rows, width), BF),
            pltpu.SemaphoreType.DMA((3, 8)),
            pltpu.SemaphoreType.DMA((2, 2)),
        ],
        vmem=60,
        cost=(18 * 2 * rows * width * hidden, 30 * MIB),
        after=after,
    )


def branch_kernel(half, info, ha, hb, b_own, b_other, wd_hbm, own_ref, other_ref, sum_ref, wd, sems):
    r = pl.program_id(0)

    def copies():
        for c in range(2):
            for k in range(8):
                dst = wd.at[c, pl.ds(k * TILE, TILE), :]
                yield pltpu.make_async_copy(wd_hbm.at[hidden_block(info, c, k), :], dst, sems.at[c, k])

    @pl.when(r == 0)
    def _():
        for copy in copies():
            copy.start()
        sum_ref[...] = jnp.zeros_like(sum_ref)
        for copy in copies():
            copy.wait()

    branch = mm(ha[...], wd[0]) + mm(hb[...], wd[1])
    delta = jnp.where(r < half, b_own[...], b_other[...]).astype(F32)
    sum_ref[0:1, :] += column_sum(delta * branch)
    branch = branch.astype(BF)
    own_ref[...] = branch
    other_ref[...] = branch


def branch_call(info, hiddens, deltas, down_weight, after, block_rows=512):
    rows, width = deltas[0].shape
    half = rows // block_rows
    hidden = hiddens[0].shape[1]
    every = pl.BlockSpec((block_rows, hidden), lambda r, info: (r, 0))
    own = pl.BlockSpec((block_rows, width), lambda r, info: (jnp.minimum(r, half), 0))
    own_in = pl.BlockSpec((block_rows, width), lambda r, info: (jnp.minimum(r, half - 1), 0))
    other = pl.BlockSpec((block_rows, width), lambda r, info: (jnp.maximum(r - half, 0), 0))
    return call_kernel(
        functools.partial(branch_kernel, half), info, [*hiddens, *deltas, down_weight],
        name="branch", vmem=40, grid=(2 * half,),
        ins=[every, every, own_in, other, pl.BlockSpec(memory_space=pl.ANY)],
        outs=[own, other, whole_spec((8, width))],
        shapes=[
            shape_of((rows + block_rows, width)), shape_of((rows, width)), shape_of((8, width), F32)
        ],
        scratch=[pltpu.VMEM((2, hidden, width), BF), pltpu.SemaphoreType.DMA((2, 8))],
        cost=(4 * 2 * rows * width * hidden, 16 * MIB), after=after,
    )


SWAP = [(0, 1), (1, 0)]
Z_NEAR = [(0, 1), (1, 0), (2, 3), (3, 2)]
Z_FAR = [(0, 2), (2, 0), (1, 3), (3, 1)]


def meet(*values):
    return lax.optimization_barrier(values)


def later(values, *needed):
    return lax.optimization_barrier((values, needed))[0]


def swap(values, axis):
    return lax.ppermute(values, axis, SWAP)


def plus(left, right):
    return (left.astype(F32) + right.astype(F32)).astype(BF)


def fold(keep, send, axis):
    return plus(keep, swap(send, axis))


def fold_two(keep, send, lead, other):
    total = fold(keep, send, lead)
    return fold(total[0], total[1], other)


def scatter_z(values):
    return lax.psum_scatter(values, "z", scatter_dimension=0, tiled=True)[0]


def turn_table(first, last, head_dim):
    pairs = head_dim // 2
    rates = np.exp(np.arange(pairs, dtype=np.float32) * np.float32(-2.0 * math.log(10000.0) / head_dim))
    angles = np.arange(first, last, dtype=np.float32)[:, None] * rates[None, :].astype(np.float32)
    cosine, sine = (np.tile(t(angles), (1, TILE // pairs)) for t in (np.cos, np.sin))
    front = (np.arange(TILE) % head_dim < pairs)[None, :]
    return np.stack([cosine, np.where(front, -sine, 0), np.where(front, 0, sine)]).astype(np.float32)


def fast_body(
    frames, cotangent, lengths, qkv_weight, out_weight, gate_weight, up_weight, down_weight,
    gain_table, bias_table,
):
    clips, rows, width = frames.shape
    count = clips * rows
    head_dim = width // HEADS
    scale = 1.0 / math.sqrt(head_dim)
    x_at, y_at, core_at, z_at = (lax.axis_index(a) for a in ("seq", "y", "core", "z"))
    start = x_at * rows
    info = jnp.concatenate(
        [jnp.stack([x_at, y_at, core_at, start, z_at]).astype(jnp.int32), lengths.astype(jnp.int32)]
    )
    flat = frames.reshape(count, width)
    tangent = cotangent.reshape(count, width)
    halo = lax.ppermute(
        frames[:, rows - TILE :].reshape(clips * TILE, width), "seq", [(0, 1)]
    )
    places = start + jnp.arange(rows)
    valid = (places[None, :] < lengths[:, None]).astype(F32).reshape(count, 1)
    branch_delta = (tangent.astype(F32) * valid * gain_table[:, 3]).astype(BF)
    table = jnp.concatenate([gain_table, bias_table, jnp.zeros((width, 2), F32)], axis=1).T
    seats = lax.axis_size("seq")
    own_turns = jnp.asarray(turn_table(0, seats * rows, head_dim))
    halo_turns = jnp.asarray(
        np.concatenate([turn_table(i * rows - TILE, i * rows, head_dim) for i in range(seats)], axis=1)
    )
    own_tab = pl.BlockSpec((3, rows, TILE), lambda r, info: (0, info[0], 0))
    halo_tab = pl.BlockSpec((3, TILE, TILE), lambda r, info: (0, info[0], 0))
    gb = whole_spec(table.shape)
    own = rows_spec(rows, width)
    halo_rows = rows_spec(TILE, width)
    qkv_rows = rows_spec(rows, 3 * width)
    kv_rows = rows_spec(TILE, 2 * width)
    w_qkv = whole_spec((width, 3 * width))
    w_key = pl.BlockSpec((width, width), lambda r, info: (0, 1))
    w_value = pl.BlockSpec((width, width), lambda r, info: (0, 2))
    w_out = whole_spec((width, width))
    sums = whole_spec((8, width))

    grid = (clips,)
    mac = 2 * count * width * width

    def two_rows(width):
        return rows_spec(count // 2, width)

    qkv, normed_one = call_kernel(
        qkv_kernel, info, [flat, qkv_weight, table, own_turns], name="qkv", vmem=36, grid=(2,),
        ins=[two_rows(width), w_qkv, gb, own_tab], outs=[two_rows(3 * width), two_rows(width)],
        shapes=[shape_of((count, 3 * width)), shape_of((count, width))], cost=(3 * mac, 16 * MIB),
    )
    def half_rows(width, part):
        return pl.BlockSpec((TILE, width), lambda r, info: (2 * r + part, 0))

    totals_of = (2 * clips, width // TILE, 2 * TILE)
    seen = [shape_of((count, width)), shape_of(totals_of, F32)]

    def half_totals(part):
        return pl.BlockSpec((1, *totals_of[1:]), lambda r, info: (2 * r + part, 0, 0))

    late = call_kernel(
        functools.partial(attend_late_kernel, scale), info, [qkv], name="attend_late", vmem=16, grid=grid,
        ins=[qkv_rows], outs=[half_rows(width, 1), half_totals(1)], shapes=seen,
        cost=(2 * mac, 8 * MIB),
    )
    halo, branch_delta = lax.optimization_barrier((halo, branch_delta))
    branch_delta_other = swap(branch_delta, "core")
    kv_halo, normed_halo = call_kernel(
        halo_kernel, info, [halo, qkv_weight, qkv_weight, table, halo_turns], name="halo", vmem=24,
        grid=(1,), ins=[rows_spec(clips * TILE, width), w_key, w_value, gb, halo_tab],
        outs=[rows_spec(clips * TILE, 2 * width), rows_spec(clips * TILE, width)],
        shapes=[shape_of((clips * TILE, 2 * width)), shape_of((clips * TILE, width))],
        cost=(mac, 8 * MIB), after=late,
    )
    context, log_totals = call_kernel(
        functools.partial(attend_kernel, scale, 0), info, [qkv, kv_halo], name="attend_early", vmem=16,
        grid=grid, ins=[half_rows(3 * width, 0), kv_rows],
        outs=[half_rows(width, 0), half_totals(0)], shapes=seen,
        cost=(2 * mac, 12 * MIB), onto=late,
    )
    attended, normed_two = call_kernel(
        functools.partial(out_kernel, clips // 2), info, [context, flat, out_weight, table],
        name="project", vmem=24, grid=(2,), ins=[two_rows(width)] * 2 + [w_out, gb], outs=[two_rows(width)] * 2,
        shapes=[shape_of((count, width))] * 2, cost=(mac, 12 * MIB),
    )
    normed_two_other = swap(normed_two, "core")

    pieces = (normed_two, normed_two_other, branch_delta, branch_delta_other)
    weights = (gate_weight, up_weight, down_weight)
    def start_pair(keeps):
        (keep_a, send_a), (keep_b, send_b) = keeps
        return (keep_a, swap(send_a, "seq")), (keep_b, swap(send_b, "y"))

    def second_pair(totals):
        (stay_a, go_a), (stay_b, go_b) = totals
        return (stay_a, swap(go_a, "y")), (stay_b, swap(go_b, "seq"))

    def halves(pairs):
        return [tuple(plus(keep[k], came[k]) for k in range(2)) for keep, came in pairs]

    def near_parts(pairs):
        return [
            jnp.stack([plus(*(v.reshape(-1, 2, 12, TILE, TILE)[:, k] for v in pair)) for pair in pairs])
            for k in range(2)
        ]

    def to_near(values):
        return lax.ppermute(values, "z", Z_NEAR)

    def far_pair(*pair):
        total = plus(*pair).reshape(2, -1, 2, 6, TILE, TILE)
        return total[:, :, 0], lax.ppermute(total[:, :, 1], "z", Z_FAR)

    def run_ffn(c, previous, after):
        *state, keep_a, send_a, keep_b, send_b = ffn_call(
            c, info, pieces, weights, previous, after
        )
        return state, ((keep_a, send_a), (keep_b, send_b))

    (hidden_0, *previous), grads_0 = run_ffn(0, None, ())
    moved_0 = start_pair(grads_0)
    (hidden_1, second, second_sent), grads_1 = run_ffn(1, previous, ())
    second, second_sent, grads_1, moved_0 = meet(second, second_sent, grads_1, moved_0)
    second_other = swap(second_sent, "core")
    near_keep_0, near_send_0 = near_parts(moved_0)
    second_other, near_send_0, grads_1 = meet(second_other, near_send_0, grads_1)
    near_came_0 = to_near(near_send_0)
    moved_1 = start_pair(grads_1)

    middle_delta, context_delta, attended_delta, sums_two = call_kernel(
        out_back_kernel, info,
        [second, second_other, attended, flat, tangent, out_weight, table],
        name="project_back", vmem=32, grid=grid,
        ins=[own, own, own, own, own, w_out, gb], outs=[own, own, own, sums],
        shapes=[shape_of((count, width))] * 3 + [shape_of((8, width), F32)],
        cost=(2 * mac, 24 * MIB), after=(near_keep_0,),
    )

    mixed_delta, mixed_halo = call_kernel(
        functools.partial(attend_back_kernel, scale), info,
        [qkv, kv_halo, context_delta, log_totals, own_turns, halo_turns], name="attend_back",
        vmem=24, grid=grid,
        ins=[
            qkv_rows, kv_rows, own, pl.BlockSpec((2, *totals_of[1:]), lambda r, info: (r, 0, 0)),
            own_tab, halo_tab,
        ],
        outs=[qkv_rows, kv_rows],
        shapes=[shape_of((count, 3 * width)), shape_of((clips * TILE, 2 * width))],
        cost=(10 * mac, 24 * MIB),
    )
    mixed_delta, mixed_halo, moved_1, near_came_0 = meet(
        mixed_delta, mixed_halo, moved_1, near_came_0
    )
    totals_1 = halves(moved_1)
    moved_1 = second_pair(totals_1)
    far_0 = far_pair(near_keep_0, near_came_0)
    all_halo = rows_spec(clips * TILE, width)
    halo_back, sums_halo = call_kernel(
        first_halo_kernel, info, [mixed_halo, qkv_weight, qkv_weight, halo], name="first_halo",
        vmem=24, grid=(1,),
        ins=[rows_spec(clips * TILE, 2 * width), w_key, w_value, all_halo], outs=[all_halo, sums],
        shapes=[shape_of((clips * TILE, width)), shape_of((8, width), F32)],
        cost=(mac, 6 * MIB),
        after=(*(t for pair in totals_1 for t in pair), far_0[0]),
    )

    cut = 3 * width // 6

    def right_block(t, info):
        x = jnp.where(t < 6, t // 3, t - 6)
        return (0, (x + info[0]) % 2, jnp.where(t < 6, jnp.maximum(t % 3 - 1, 0), 2), 0, 0, 0)

    left_spec = pl.BlockSpec(
        (1, 2, 4, 64, cut), lambda t, info: ((jnp.minimum(t // 3, 1) + info[0]) % 2, 0, 0, 0, 0)
    )
    right_spec = pl.BlockSpec((2, 1, 1, 4, 64, cut), right_block)
    packed = [shape_of((2, 2, 4, 64, cut)), shape_of((2, 2, 3, 4, 64, cut))]
    keep_l, keep_r, send_l, send_r = call_kernel(
        qkv_grad_kernel, info,
        [normed_one, mixed_delta, normed_halo, mixed_halo, context, attended_delta],
        name="qkv_grad", vmem=40, grid=(8,),
        ins=[
            whole_spec((count, width)),
            pl.BlockSpec((count, cut), lambda t, info: (0, jnp.minimum(t, 5))),
            whole_spec((clips * TILE, width)),
            pl.BlockSpec((clips * TILE, cut), lambda t, info: (0, jnp.clip(t - 2, 0, 3))),
            whole_spec((count, width)),
            pl.BlockSpec((count, cut), lambda t, info: (0, jnp.maximum(t - 6, 0))),
        ],
        outs=[left_spec, right_spec] * 2, shapes=packed * 2,
        scratch=[pltpu.VMEM((width, cut), F32)], cost=(5 * mac, 20 * MIB),
        after=(halo_back,),
    )
    moved_1, keep_l, keep_r, send_l, send_r = meet(moved_1, keep_l, keep_r, send_l, send_r)
    came_l, came_r = swap(send_l, "core"), swap(send_r, "core")
    near_keep_1, near_send_1 = near_parts(moved_1)
    came_l, came_r, near_send_1, halo_back = meet(came_l, came_r, near_send_1, halo_back)
    stay_l, go_l = (plus(keep_l[k], came_l[k]) for k in range(2))
    stay_r, go_r = (plus(keep_r[k], came_r[k]) for k in range(2))
    go_l, go_r = swap(go_l, "seq"), swap(go_r, "y")
    halo_came = lax.ppermute(halo_back, "seq", [(1, 0)])
    near_came_1 = to_near(near_send_1)
    branch, branch_sent, sums_branch = branch_call(
        info, (hidden_0, hidden_1), (branch_delta, branch_delta_other), down_weight,
        (stay_l, stay_r, near_keep_1),
    )
    part_grad, vectors = call_kernel(
        functools.partial(first_back_kernel, clips // 2), info,
        [
            mixed_delta, qkv_weight, flat, middle_delta, table, sums_halo, sums_two, sums_branch
        ],
        name="first_back", vmem=40, grid=(2,),
        ins=[two_rows(3 * width), w_qkv, two_rows(width), two_rows(width), gb, sums, sums, sums],
        outs=[two_rows(width), sums],
        shapes=[shape_of((count, width)), shape_of((8, width), F32)],
        cost=(3 * mac, 24 * MIB),
    )
    go_l, go_r, near_came_1, halo_came, far_0, part_grad, vectors, branch_sent = meet(
        go_l, go_r, near_came_1, halo_came, far_0, part_grad, vectors, branch_sent
    )
    vectors_core = swap(vectors, "core")
    left, right = plus(stay_l, go_l), plus(stay_r, go_r)
    vectors = vectors + vectors_core
    go_l, go_r = swap(left[1], "y"), swap(right[1], "seq")
    far_1 = far_pair(near_keep_1, near_came_1)
    branch_other = swap(branch_sent, "core")
    vectors_x = swap(vectors, "seq")
    input_grad = call_kernel(
        input_grad_kernel, info, [part_grad, halo_came, flat, table], name="input_grad", vmem=16,
        grid=grid, ins=[own, halo_rows, own, gb], outs=own, shapes=shape_of((count, width)),
        cost=(0, 8 * MIB), after=(left, right, far_1[0], vectors),
    )
    go_l, go_r, branch_other, vectors_x, input_grad = meet(
        go_l, go_r, branch_other, vectors_x, input_grad
    )
    left, right = plus(left[0], go_l), plus(right[0], go_r)
    qkv_total = jnp.concatenate([left[None], right]).reshape(4, 2, 2, 64, cut)
    go = to_near(qkv_total[:, :, 1])
    first_tiles = plus(*far_0)
    late_a, late_b = swap(first_tiles[0, 1], "y"), swap(first_tiles[1, 1], "seq")
    vectors = vectors + vectors_x
    vectors_y = swap(vectors, "y")
    output = call_kernel(
        output_kernel, info, [flat, attended, branch, branch_other, table],
        name="output", vmem=16, grid=grid, ins=[own, own, own, own, gb], outs=own,
        shapes=shape_of((count, width)), cost=(0, 14 * MIB),
        after=(qkv_total, first_tiles, vectors),
    )
    go, far_1, late_a, late_b, vectors_y, output = meet(
        go, far_1, late_a, late_b, vectors_y, output
    )
    vectors = vectors + vectors_y
    vectors = vectors + lax.ppermute(vectors, "z", Z_NEAR)
    vectors = vectors + lax.ppermute(vectors, "z", Z_FAR)
    qkv_total = plus(qkv_total[:, :, 0], go)
    qkv_total = plus(qkv_total[:, 0], lax.ppermute(qkv_total[:, 1], "z", Z_FAR))
    qkv_grad = qkv_total[:3].transpose(1, 0, 2).reshape(-1, 3 * cut).astype(F32)
    out_grad = qkv_total[3].astype(F32)

    share = width // 16
    seat = (z_at * 2 + y_at) * 2 + core_at
    vectors = lax.dynamic_slice(vectors, (4 * x_at, share * seat), (4, share)).T
    gain_grad, bias_grad = vectors[:, :2], vectors[:, 2:3]

    first_tiles = [plus(first_tiles[k, 0], came) for k, came in enumerate((late_a, late_b))]
    tiles = jnp.stack([jnp.stack(first_tiles), plus(*far_1)[:, 0]])
    gates = tiles[:, :, :4].reshape(2, 2, 2, 2, 2, share, TILE)
    kept = lax.dynamic_index_in_dim(gates, core_at, axis=4, keepdims=False)
    sent = lax.dynamic_index_in_dim(gates, 1 - core_at, axis=4, keepdims=False)
    came = swap(sent, "core")
    both = jnp.where(core_at == 0, jnp.stack([kept, came], 4), jnp.stack([came, kept], 4))
    both = both.transpose(2, 5, 1, 3, 4, 0, 6).astype(F32)
    gate_grad = both[0].reshape(share, -1)
    up_grad = both[1].reshape(share, -1)
    down_grad = tiles[:, :, 4:].reshape(2, width // 2, TILE).transpose(0, 2, 1).astype(F32)
    down_grad = down_grad.reshape(2 * TILE, width // 2)
    shape = (clips, rows, width)
    return (
        output.reshape(shape), input_grad.reshape(shape), qkv_grad, out_grad, gate_grad, up_grad,
        down_grad, gain_grad, bias_grad,
    )


def solution(mesh):
    placed = (("dp", "seq", None),) * 2 + (("dp",),) + ((),) * 7
    given = (("dp", "seq", None),) * 2 + (("dp", "seq"),) * 7
    fast = mesh.shape["dp"] == 16 and mesh.shape["seq"] == 2
    dp_axes = ("z", "y", "core") if fast else "dp"

    def specs(entries):
        return tuple(P(*(dp_axes if a == "dp" else a for a in entry)) for entry in entries)

    if fast:
        mesh = Mesh(mesh.devices.reshape(4, 2, 2, 2), ("z", "y", "core", "seq"))
    return jax.shard_map(
        fast_body if fast else body,
        mesh=mesh,
        in_specs=specs(placed),
        out_specs=specs(given),
        check_vma=False,
    )
```
